32 devices in a mesh: maps: 8 (over z, y), rows: 4 (over x, core).
Axes of the slice: x: 2, y: 2, z: 4, core: 2. Of those that a mesh axis runs over, the one named last changes fastest.
Arguments:
- block_input: bfloat16 [8, 48, 32, 512], P('maps', 'rows'), may hold values from -6 to 6
- conv_weights: bfloat16 [3, 9, 512, 512], replicated, may hold values from -0.09375 to 0.09375
- norm_params: float32 [2, 3, 512], replicated, may hold values from -1.1 to 3.6, as said below
- pool_index: int32 [8, 24, 16, 512], P('maps', 'rows'), may hold values from 0 to 3
- task_mask: int32 [8, 24, 16], P('maps'), may hold values 0 or 1
- map_kind: int32 [8], replicated, may hold values from 0 to 1
- map_domain: int32 [8], replicated, may hold values from 0 to 3, as said below
- out_grad: bfloat16 [8, 24, 16, 512], P('maps', None, None, 'rows'), may hold values from -6 to 6
- step: int32 [1], replicated, may hold values from 2 to 20
- conv_master: float32 [3, 9, 512, 512], P(None, None, 'maps', 'rows'), may hold values from -0.09375 to 0.09375
- conv_moment1: float32 [3, 9, 512, 512], P(None, None, 'maps', 'rows')
- conv_moment2: float32 [3, 9, 512, 512], P(None, None, 'maps', 'rows'), as said below
- norm_moment1: float32 [2, 3, 512], replicated
- norm_moment2: float32 [2, 3, 512], replicated, as said below
Outputs:
- pooled: bfloat16 [8, 24, 16, 512], P('maps', None, None, 'rows')
- input_grad: bfloat16 [8, 48, 32, 512], P('maps', 'rows')
- grad_norm: float32 [1], replicated
- conv_moment1_new: float32 [3, 9, 512, 512], P(None, None, 'maps', 'rows')
- conv_moment2_new: float32 [3, 9, 512, 512], P(None, None, 'maps', 'rows')
- conv_master_new: float32 [3, 9, 512, 512], P(None, None, 'maps', 'rows')
- norm_moment1_new: float32 [2, 3, 512], replicated
- norm_moment2_new: float32 [2, 3, 512], replicated
- norm_params_new: float32 [2, 3, 512], replicated
The draws below stay inside these ranges and needn't reach their ends.
Inputs may be any that keep to these rules, and one draw needn't show every extreme that they name: `pool_index`: index of the window's maximum, 2 x row offset + column offset. `task_mask`: 1 where the pooled pixel carries a label. `map_kind`: kind 0: 42 x 32 valid pixels; kind 1: 48 x 26; the rest of the grid is padding. `map_domain`: each domain holds exactly 2 maps. `norm_params`: gains in row 0 are positive. `conv_moment2`: every entry positive. `norm_moment2`: every entry positive.
All inputs are finite; a program needn't handle non-finite values. No bound on the sum of `task_mask` on one device may be relied on, other than what follows from the above.
Results may differ from the reference program's by a relative error of at most 0.012.
Values may be sent and summed in bfloat16 or wider, within the bound.
No kernel may reach another device: no remote copies, remote signals or barrier semaphores. Data moves between devices by JAX's collectives and lax.ppermute only.
A program may use at most 128 MiB of HBM per device.

```python
import math
import jax
import jax.numpy as jnp
from jax import lax

C = 512
MAP_W = 32
DOMAINS = 4
MAPS = 8
HEIGHT = 48
H_SHORT = 42
W_SHORT = 26
HP = 24
WP = 16


def draw_map_domain(key, part):
    return (jax.random.permutation(key, MAPS) % DOMAINS).astype(jnp.int32)


def channel_gains(key):
    position = jnp.arange(C, dtype=jnp.float32) / float(max(C - 1, 1))
    low_end = 0.5
    span = 4.0
    rough = jax.random.uniform(jax.random.fold_in(key, 4111), (3, C), jnp.float32, 0.8, 1.25)
    return low_end * jnp.power(span, position)[None, :] * rough


def gradient_scales(key):
    gains = channel_gains(key)
    inputs_scale = jnp.stack([jnp.ones((C,), jnp.float32), gains[0], gains[1]])
    profile = inputs_scale / jnp.sqrt(jnp.mean(inputs_scale * inputs_scale, axis=1, keepdims=True))
    total = 9.0 * jnp.sum(jnp.sum(profile * profile, axis=1) * jnp.sum(gains * gains, axis=1))
    unit = 1.0 / jnp.sqrt(total)
    kernel_scale = unit * profile[:, None, :, None] * gains[:, None, None, :]
    return (kernel_scale, unit)


def draw_norm_params(key, part):
    gains = channel_gains(key)
    factor = jax.random.uniform(jax.random.fold_in(key, 4112), (3, C), jnp.float32, -0.3, 1.0)
    return jnp.stack([gains, gains * factor]).astype(jnp.float32)


def draw_conv_moment1(key, part):
    kernel_scale, unit = gradient_scales(key)
    noise = jax.random.normal(jax.random.fold_in(key, 4113), (3, 9, C, C), jnp.float32)
    return (0.11 * kernel_scale * noise).astype(jnp.float32)


def draw_conv_moment2(key, part):
    kernel_scale, unit = gradient_scales(key)
    factor = jnp.exp(jax.random.uniform(jax.random.fold_in(key, 4114), (3, 9, C, C), jnp.float32, 0.0, 1.3862944))
    return (0.001 * factor * kernel_scale * kernel_scale).astype(jnp.float32)


def draw_norm_moment1(key, part):
    kernel_scale, unit = gradient_scales(key)
    noise = jax.random.normal(jax.random.fold_in(key, 4115), (2, 3, C), jnp.float32)
    return (0.11 * unit * noise).astype(jnp.float32)


def draw_norm_moment2(key, part):
    kernel_scale, unit = gradient_scales(key)
    factor = jnp.exp(jax.random.uniform(jax.random.fold_in(key, 4116), (2, 3, C), jnp.float32, 0.0, 1.3862944))
    return (0.001 * factor * unit * unit).astype(jnp.float32)


def with_ends(drawn, stream_key, low, high):
    longest = drawn.shape.index(max(drawn.shape))
    spots = []
    for shift in (0, 1):
        where = [jax.random.randint(jax.random.fold_in(stream_key, axis), (), 0, length) for axis, length in enumerate(drawn.shape)]
        where[longest] = (where[longest] + shift) % drawn.shape[longest]
        spots.append(tuple(where))
    return drawn.at[spots[0]].set(low).at[spots[1]].set(high)


def block_scale(key, dims, shards, low, high):
    factor_of, own = 1.0, jax.random.fold_in(key, 6)
    for dim, shards_of in shards:
        draws = jnp.exp(jax.random.uniform(jax.random.fold_in(own, dim), (shards_of,), jnp.float32, low / len(shards), high / len(shards)))
        factor_of = factor_of * jnp.repeat(draws, dims[dim] // shards_of).reshape([-1 if axis == dim else 1 for axis in range(len(dims))])
    return factor_of


def bell_draw(stream_key, dims, width, limit, shards=(), kind=jnp.bfloat16):
    drawn = width * jax.random.normal(stream_key, dims, jnp.float32)
    if shards:
        drawn = drawn * block_scale(stream_key, dims, shards, -0.22, 0.18)
    return jnp.clip(drawn, -limit, limit).astype(kind)


def setup_inputs(seed: int = 0) -> dict:
    key_list = jax.random.split(jax.random.key(seed), 15)
    return {
        "block_input": bell_draw(key_list[0], (MAPS, HEIGHT, MAP_W, C), 1.0, 6.0, ((0, 8), (1, 4))),
        "conv_weights": bell_draw(key_list[1], (3, 9, C, C), (9 * C) ** -0.5, 0.09375),
        "norm_params": draw_norm_params(jax.random.fold_in(key_list[14], 71), 0),
        "pool_index": with_ends(jax.random.randint(key_list[3], (MAPS, HP, WP, C), 0, 4), jax.random.fold_in(key_list[3], 1), 0, 3).astype(jnp.int32),
        "task_mask": with_ends((jax.random.randint(key_list[4], (MAPS, HP, WP), 0, 4) < 3).astype(jnp.int32), jax.random.fold_in(key_list[4], 1), 0, 1),
        "map_kind": with_ends(jax.random.randint(key_list[5], (MAPS,), 0, 2), jax.random.fold_in(key_list[5], 1), 0, 1).astype(jnp.int32),
        "map_domain": draw_map_domain(jax.random.fold_in(key_list[14], 71), 0),
        "out_grad": bell_draw(key_list[7], (MAPS, HP, WP, C), 1.0, 6.0, ((0, 8), (3, 4))),
        "step": jax.random.randint(key_list[8], (1,), 2, 21).astype(jnp.int32),
        "conv_master": bell_draw(key_list[9], (3, 9, C, C), (9 * C) ** -0.5, 0.09375, ((2, 8), (3, 4)), jnp.float32),
        "conv_moment1": draw_conv_moment1(jax.random.fold_in(key_list[14], 71), 0),
        "conv_moment2": draw_conv_moment2(jax.random.fold_in(key_list[14], 71), 0),
        "norm_moment1": draw_norm_moment1(jax.random.fold_in(key_list[14], 71), 0),
        "norm_moment2": draw_norm_moment2(jax.random.fold_in(key_list[14], 71), 0),
    }


@jax.custom_vjp
def low(v):
    return lax.optimization_barrier(v.astype(jnp.bfloat16)).astype(jnp.float32)

@jax.custom_vjp
def low_back(v):
    return v

def low_keep(v):
    return (low(v), None)

def low_pass(kept, grad):
    return (grad,)

def back_keep(v):
    return (v, None)

def back_low(kept, grad):
    return (low(grad),)
low.defvjp(low_keep, low_pass)
low_back.defvjp(back_keep, back_low)
norm_epsilon = 1e-05
clip_limit = 1.0
first_decay = 0.9
second_decay = 0.999
adam_epsilon = 1e-08
norm_rate = 0.5
weight_decay = 0.01
highest = lax.Precision.HIGHEST

def conv_apply(values, kernel):
    shaped = kernel.reshape(3, 3, kernel.shape[1], kernel.shape[2])
    return lax.conv_general_dilated(values, shaped, (1, 1), 'SAME', dimension_numbers=('NHWC', 'HWIO', 'NHWC'), precision=highest)

def geometry(map_kind, map_domain):
    tall = map_kind == 1
    heights = jnp.where(tall, HEIGHT, H_SHORT).astype(jnp.int32)
    widths = jnp.where(tall, W_SHORT, MAP_W).astype(jnp.int32)
    row_pos = jnp.arange(HEIGHT, dtype=jnp.int32)
    col_pos = jnp.arange(MAP_W, dtype=jnp.int32)
    valid = ((row_pos[None, :, None] < heights[:, None, None]) & (col_pos[None, None, :] < widths[:, None, None])).astype(jnp.float32)
    member = (map_domain[:, None] == jnp.arange(DOMAINS, dtype=jnp.int32)[None, :]).astype(jnp.float32)
    counts = jnp.dot(member.T, (heights * widths).astype(jnp.float32), precision=highest)
    return (valid, member, counts)

def domain_sums(member, first_term, second_term):
    return (jnp.dot(member.T, lax.optimization_barrier(jnp.sum(first_term, axis=(1, 2))), precision=highest), jnp.dot(member.T, lax.optimization_barrier(jnp.sum(second_term, axis=(1, 2))), precision=highest))

def forward(inputs, kernels, params, pool_index, valid, member, counts):
    values = inputs
    mask = valid[..., None]
    for layer_index in range(3):
        conv_out = low_back(conv_apply(low(values), kernels[layer_index]))
        masked = conv_out * mask
        sums, squares = domain_sums(member, masked, masked * conv_out)
        mean = sums / counts[:, None]
        inverse = lax.rsqrt(squares / counts[:, None] - mean * mean + norm_epsilon)
        map_mean = jnp.dot(member, mean, precision=highest)
        map_inverse = jnp.dot(member, inverse, precision=highest)
        normed = (conv_out - map_mean[:, None, None, :]) * map_inverse[:, None, None, :]
        values = jax.nn.silu(params[0, layer_index] * normed + params[1, layer_index]) * mask
    values = low(values)
    pooled = jnp.zeros(pool_index.shape, jnp.float32)
    for corner in range(4):
        pooled = pooled + jnp.where(pool_index == corner, values[:, corner // 2::2, corner % 2::2, :], 0.0)
    return pooled

def adamw_update(param, grad, first, second, rate, decay, scale, count):
    clipped = scale * grad
    first_new = first_decay * first + (1.0 - first_decay) * clipped
    second_new = second_decay * second + (1.0 - second_decay) * clipped * clipped
    first_fix = 1.0 - jnp.power(first_decay, count)
    second_fix = 1.0 - jnp.power(second_decay, count)
    update = first_new / first_fix / (jnp.sqrt(second_new / second_fix) + adam_epsilon)
    return (first_new, second_new, param - rate * (update + decay * param))

def reference(block_input, conv_weights, norm_params, pool_index, task_mask, map_kind, map_domain, out_grad, step, conv_master, conv_moment1, conv_moment2, norm_moment1, norm_moment2):
    valid, member, counts = geometry(map_kind, map_domain)
    conv_rate = 2.0 / math.sqrt(9.0 * C)

    def forward_fn(inputs, kernels, params):
        return forward(inputs, kernels, params, pool_index, valid, member, counts)
    pooled, pullback = jax.vjp(forward_fn, block_input.astype(jnp.float32), conv_weights.astype(jnp.float32), norm_params)
    cotangent = out_grad.astype(jnp.float32) * task_mask[..., None].astype(jnp.float32)
    input_grad, kernel_grad, norm_grad = pullback(cotangent)
    total = jnp.sqrt(jnp.sum(kernel_grad * kernel_grad) + jnp.sum(norm_grad * norm_grad))
    scale = jnp.minimum(1.0, clip_limit / total)
    count = step[0].astype(jnp.float32)
    conv_first, conv_second, conv_new = adamw_update(conv_master, kernel_grad, conv_moment1, conv_moment2, conv_rate, weight_decay, scale, count)
    norm_first, norm_second, norm_new = adamw_update(norm_params, norm_grad, norm_moment1, norm_moment2, norm_rate, 0.0, scale, count)
    return (pooled.astype(jnp.bfloat16), input_grad.astype(jnp.bfloat16), total.reshape(1), conv_first, conv_second, conv_new, norm_first, norm_second, norm_new)
```

```python
import functools
import math

import jax
import jax.numpy as jnp
from jax import lax
from jax.experimental import pallas as pl
from jax.experimental.pallas import tpu as pltpu
from jax.sharding import PartitionSpec as P

DOMAINS = 4
norm_epsilon = 1e-05
clip_limit = 1.0
first_decay = 0.9
second_decay = 0.999
adam_epsilon = 1e-08
norm_rate = 0.5
weight_decay = 0.01

HALO = 6
AXES = ("maps", "rows")
F32 = jnp.float32
BF16 = jnp.bfloat16


class Sizes:
    def __init__(self, maps, bands, rows, width, channels):
        self.maps = maps
        self.bands = bands
        self.devices = maps * bands
        self.rows = rows
        self.width = width
        self.channels = channels
        self.height = rows * bands
        self.short_height = 2 * (self.height * 7 // 16)
        self.short_width = 2 * (width * 13 // 32)
        self.pixels = rows * width
        self.quarter = channels // bands


def spec_vmem():
    return pl.BlockSpec(memory_space=pltpu.VMEM)


def spec_smem():
    return pl.BlockSpec(memory_space=pltpu.SMEM)


def spec_any():
    return pl.BlockSpec(memory_space=pl.ANY)


def params(megabytes):
    return pltpu.CompilerParams(vmem_limit_bytes=megabytes << 20)


def area_of(sz, kind):
    return jnp.where(kind == 1, sz.height * sz.short_width, sz.short_height * sz.width)


def own_count(sz, kind_ref, domain_ref, place_ref):
    own = domain_ref[place_ref[0]]
    total = jnp.int32(0)
    for m in range(sz.maps):
        total = total + jnp.where(domain_ref[m] == own, area_of(sz, kind_ref[m]), 0)
    return total.astype(F32)


def own_sums(sz, gathered_ref, domain_ref, place_ref):
    own = domain_ref[place_ref[0]]
    total = jnp.zeros(gathered_ref.shape[1:], F32)
    for m in range(sz.maps):
        part = gathered_ref[m * sz.bands]
        for b in range(1, sz.bands):
            part = part + gathered_ref[m * sz.bands + b]
        total = total + jnp.where(domain_ref[m] == own, part, 0.0)
    return total


def all_sums(sz, gathered_ref):
    total = gathered_ref[0]
    for k in range(1, sz.devices):
        total = total + gathered_ref[k]
    return total


def split_rows(tile, channels):
    first = jnp.concatenate([tile[k : k + 1, :] for k in range(4)], axis=1)
    second = jnp.concatenate([tile[k : k + 1, :] for k in range(4, 8)], axis=1)
    return first, second


def join_rows(first, second):
    lanes = first.shape[1] // 4
    return jnp.concatenate(
        [row[:, k * lanes : (k + 1) * lanes] for row in (first, second) for k in range(4)], axis=0
    )


def valid_mask(sz, kind_ref, place_ref, first_row, count_rows):
    shape = (count_rows * sz.width, sz.channels)
    pixel = lax.broadcasted_iota(jnp.int32, shape, 0)
    row = pixel // sz.width + (place_ref[1] * sz.rows + first_row)
    col = pixel % sz.width
    tall = kind_ref[place_ref[0]] == 1
    limit = jnp.where(tall, sz.height, sz.short_height)
    wide = jnp.where(tall, sz.short_width, sz.width)
    return (row >= 0) & (row < limit) & (col < wide)


def store_shifted(sz, x3_ref, value, reverse):
    rows = value.shape[0]
    col = lax.broadcasted_iota(jnp.int32, value.shape, 0) % sz.width
    before = jnp.where(col == 0, 0.0, pltpu.roll(value, 1, 0))
    after = jnp.where(col == sz.width - 1, 0.0, pltpu.roll(value, rows - 1, 0))
    if reverse:
        before, after = after, before
    c = sz.channels
    x3_ref[:, 0:c] = before.astype(BF16)
    x3_ref[:, c : 2 * c] = value.astype(BF16)
    x3_ref[:, 2 * c : 3 * c] = after.astype(BF16)


def start_weights(weights_ref, buffer_ref, sems, layer, order):
    copies = {}
    for i in order:
        copies[i] = pltpu.make_async_copy(
            weights_ref.at[layer, pl.ds(3 * i, 3)], buffer_ref.at[pl.ds(3 * i, 3)], sems.at[i]
        )
        copies[i].start()
    return copies


def conv_forward(sz, x3_ref, buffer_ref, copies, out_ref, out_rows):
    c = sz.channels
    n = out_rows * sz.width
    for i in range(3):
        copies[i].wait()
        lhs = x3_ref[i * sz.width : i * sz.width + n, :]
        rhs = buffer_ref[3 * i : 3 * i + 3].reshape(3 * c, c)
        term = jnp.dot(lhs, rhs, preferred_element_type=F32)
        if i == 0:
            out_ref[...] = term
        else:
            out_ref[...] += term


def conv_backward(sz, x3_ref, buffer_ref, copies, acc_ref, out_rows):
    c = sz.channels
    n = out_rows * sz.width
    for i in (0, 1, 2):
        copies[i].wait()
        for j in range(3):
            lhs = x3_ref[(2 - i) * sz.width : (2 - i) * sz.width + n, j * c : (j + 1) * c]
            term = lax.dot_general(
                lhs,
                buffer_ref[3 * i + j],
                (((1,), (1,)), ((), ())),
                preferred_element_type=F32,
            )
            if i == 0 and j == 0:
                acc_ref[...] = term
            else:
                acc_ref[...] += term


def put_stats(sz, first, second, out_ref):
    tile = join_rows(first, second)
    out_ref[...] = jnp.broadcast_to(tile[None], out_ref.shape)


def sigmoid(v):
    return 1.0 / (1.0 + jnp.exp(-v))


def kernel_first(sz, kind_ref, domain_ref, place_ref, up_ref, x_ref, down_ref, weights_ref,
                 conv_ref, stats_ref, x3_ref, buffer_ref, sems):
    copies = start_weights(weights_ref, buffer_ref, sems, 0, (0, 1, 2))
    value = jnp.concatenate([up_ref[...], x_ref[...], down_ref[...]], axis=0).astype(F32)
    store_shifted(sz, x3_ref, value, False)
    rows = sz.rows + 2 * HALO - 2
    conv_forward(sz, x3_ref, buffer_ref, copies, conv_ref, rows)
    start = (HALO - 1) * sz.width
    centre = conv_ref[start : start + sz.pixels, :]
    masked = jnp.where(valid_mask(sz, kind_ref, place_ref, 0, sz.rows), centre, 0.0)
    put_stats(
        sz,
        jnp.sum(masked, axis=0, keepdims=True),
        jnp.sum(masked * centre, axis=0, keepdims=True),
        stats_ref,
    )


def norm_of(sz, gathered_ref, kind_ref, domain_ref, place_ref):
    count = own_count(sz, kind_ref, domain_ref, place_ref)
    tile = own_sums(sz, gathered_ref, domain_ref, place_ref)
    total, squares = split_rows(tile / count, sz.channels)
    return total, lax.rsqrt(squares - total * total + norm_epsilon)


def kernel_forward(sz, layer, kind_ref, domain_ref, place_ref, before_ref, gathered_ref, norm_ref, weights_ref,
                   conv_ref, stats_ref, act_ref, moments_ref, x3_ref, buffer_ref, sems):
    copies = start_weights(weights_ref, buffer_ref, sems, layer, (0, 1, 2))
    mean, inverse = norm_of(sz, gathered_ref, kind_ref, domain_ref, place_ref)
    moments_ref[...] = join_rows(mean, inverse)
    halo = HALO - layer
    rows = sz.rows + 2 * halo
    gain = norm_ref[0, layer - 1 : layer, :]
    shift = norm_ref[1, layer - 1 : layer, :]
    shifted = gain * ((before_ref[...] - mean) * inverse) + shift
    act = jnp.where(
        valid_mask(sz, kind_ref, place_ref, -halo, rows), shifted * sigmoid(shifted), 0.0
    )
    act_ref[...] = act[halo * sz.width : halo * sz.width + sz.pixels, :].astype(BF16)
    store_shifted(sz, x3_ref, act, False)
    conv_forward(sz, x3_ref, buffer_ref, copies, conv_ref, rows - 2)
    start = (halo - 1) * sz.width
    centre = conv_ref[start : start + sz.pixels, :]
    masked = jnp.where(valid_mask(sz, kind_ref, place_ref, 0, sz.rows), centre, 0.0)
    put_stats(
        sz,
        jnp.sum(masked, axis=0, keepdims=True),
        jnp.sum(masked * centre, axis=0, keepdims=True),
        stats_ref,
    )


def kernel_pool(sz, kind_ref, domain_ref, place_ref, before_ref, gathered_ref, norm_ref, index_ref, index_up_ref,
                index_down_ref, cotangent_ref, label_ref, pooled_ref, stats_ref, moments_ref, grad_ref,
                spread_ref, act_ref):
    c, w, q = sz.channels, sz.width, sz.quarter
    half = w // 2
    mean, inverse = norm_of(sz, gathered_ref, kind_ref, domain_ref, place_ref)
    moments_ref[...] = join_rows(mean, inverse)
    gain = norm_ref[0, 2:3, :]
    shift = norm_ref[1, 2:3, :]
    halo = HALO - 3
    rows = sz.rows + 2 * halo
    valid = valid_mask(sz, kind_ref, place_ref, -halo, rows)
    normed = (before_ref[...] - mean) * inverse
    shifted = gain * normed + shift
    sig = sigmoid(shifted)
    act = jnp.where(valid, shifted * sig, 0.0)
    groups = c // 128
    for g in range(groups):
        act_ref[g] = act[:, g * 128 : (g + 1) * 128]
    windows = sz.rows // 2
    for p in range(windows):
        index = index_ref[p * half : (p + 1) * half, :]
        result = jnp.zeros(index.shape, F32)
        for corner in range(4):
            start = (halo + 2 * p + corner // 2) * w + corner % 2
            taken = jnp.concatenate(
                [act_ref[g, pl.ds(start, half, stride=2), :] for g in range(groups)], axis=1
            )
            result = jnp.where(index == corner, taken, result)
        for b in range(sz.bands):
            pooled_ref[b, p * half : (p + 1) * half, :] = result[:, b * q : (b + 1) * q].astype(BF16)
    for p in range(windows + 4):
        if p < 2:
            index = index_up_ref[p * half : (p + 1) * half, :]
        elif p < windows + 2:
            index = index_ref[(p - 2) * half : (p - 1) * half, :]
        else:
            index = index_down_ref[(p - windows - 2) * half : (p - windows - 1) * half, :]
        given = jnp.concatenate(
            [cotangent_ref[b, p * half : (p + 1) * half, :] for b in range(sz.bands)], axis=1
        ).astype(F32)
        given = given * jnp.concatenate([label_ref[p * half : (p + 1) * half, :]] * (c // 128), axis=1)
        for corner in range(4):
            start = (2 * p + corner // 2) * w + corner % 2
            placed = jnp.where(index == corner, given, 0.0)
            for g in range(groups):
                spread_ref[g, pl.ds(start, half, stride=2), :] = placed[:, g * 128 : (g + 1) * 128]
    upstream = jnp.concatenate([spread_ref[g, w : w + rows * w, :] for g in range(groups)], axis=1)
    grad = jnp.where(valid, upstream * (sig * (1.0 + shifted * (1.0 - sig))), 0.0)
    grad_ref[...] = grad
    centre = grad[halo * w : halo * w + sz.pixels, :]
    put_stats(
        sz,
        jnp.sum(centre, axis=0, keepdims=True),
        jnp.sum(centre * normed[halo * w : halo * w + sz.pixels, :], axis=0, keepdims=True),
        stats_ref,
    )


def conv_grad_of(sz, layer, halo, kind_ref, domain_ref, place_ref, grad, conv, moments_ref, gathered_ref, norm_ref):
    mean, inverse = split_rows(moments_ref[...], sz.channels)
    count = own_count(sz, kind_ref, domain_ref, place_ref)
    one, two = split_rows(own_sums(sz, gathered_ref, domain_ref, place_ref) / count, sz.channels)
    normed = (conv - mean) * inverse
    gain = norm_ref[0, layer : layer + 1, :]
    valid = valid_mask(sz, kind_ref, place_ref, -halo, sz.rows + 2 * halo)
    return jnp.where(valid, (gain * inverse) * (grad - one - normed * two), 0.0)


def kernel_backward(sz, layer, kind_ref, domain_ref, place_ref, grad_ref, conv_ref, moments_ref, gathered_ref,
                    norm_ref, weights_ref, conv_below_ref, moments_below_ref,
                    below_ref, stats_ref, conv_grad_ref, totals_ref, x3_ref, acc_ref, buffer_ref, sems):
    w = sz.width
    copies = start_weights(weights_ref, buffer_ref, sems, layer, (0, 1, 2))
    halo = layer + 1
    skip = (HALO - 1 - layer) - halo
    rows = sz.rows + 2 * halo
    totals_ref[...] = all_sums(sz, gathered_ref)
    conv = conv_ref[skip * w : (skip + rows) * w, :]
    conv_grad = conv_grad_of(
        sz, layer, halo, kind_ref, domain_ref, place_ref, grad_ref[...], conv, moments_ref, gathered_ref, norm_ref
    )
    conv_grad_ref[...] = conv_grad[halo * w : halo * w + sz.pixels, :].astype(BF16)
    store_shifted(sz, x3_ref, conv_grad, True)
    conv_backward(sz, x3_ref, buffer_ref, copies, acc_ref, rows - 2)
    below = layer - 1
    mean, inverse = split_rows(moments_below_ref[...], sz.channels)
    gain = norm_ref[0, below : below + 1, :]
    shift = norm_ref[1, below : below + 1, :]
    skip_below = (HALO - 1 - below) - (halo - 1)
    normed = (conv_below_ref[skip_below * w : (skip_below + rows - 2) * w, :] - mean) * inverse
    shifted = gain * normed + shift
    sig = sigmoid(shifted)
    valid = valid_mask(sz, kind_ref, place_ref, -(halo - 1), rows - 2)
    grad = jnp.where(valid, acc_ref[...] * (sig * (1.0 + shifted * (1.0 - sig))), 0.0)
    below_ref[...] = grad
    start = (halo - 1) * w
    centre = grad[start : start + sz.pixels, :]
    put_stats(
        sz,
        jnp.sum(centre, axis=0, keepdims=True),
        jnp.sum(centre * normed[start : start + sz.pixels, :], axis=0, keepdims=True),
        stats_ref,
    )


def kernel_last_grad(sz, kind_ref, domain_ref, place_ref, grad_ref, conv_ref, moments_ref, gathered_ref,
                     norm_ref, conv_grad_ref, chunks_ref, totals_ref):
    w, q = sz.width, sz.quarter
    totals_ref[...] = all_sums(sz, gathered_ref)
    skip = HALO - 2
    rows = sz.rows + 2
    conv_grad = conv_grad_of(
        sz, 0, 1, kind_ref, domain_ref, place_ref, grad_ref[...], conv_ref[skip * w : (skip + rows) * w, :],
        moments_ref, gathered_ref, norm_ref,
    )
    conv_grad_ref[...] = conv_grad
    centre = conv_grad[w : w + sz.pixels, :].astype(BF16)
    for b in range(sz.bands):
        chunks_ref[b] = centre[:, b * q : (b + 1) * q]


def kernel_input_grad(sz, conv_grad_ref, weights_ref, out_ref, x3_ref, acc_ref, buffer_ref, sems):
    copies = start_weights(weights_ref, buffer_ref, sems, 0, (0, 1, 2))
    store_shifted(sz, x3_ref, conv_grad_ref[...], True)
    conv_backward(sz, x3_ref, buffer_ref, copies, acc_ref, sz.rows)
    out_ref[...] = acc_ref[...].astype(BF16)


def kernel_weight_grad(sz, split, place_ref, act_ref, conv_grad_ref, out_ref, x9_ref, part_ref, sem):
    w, q, c = sz.width, sz.quarter, sz.channels
    pixels = sz.height * w
    if split:
        copy = pltpu.make_async_copy(
            conv_grad_ref.at[:, pl.ds(pl.multiple_of(place_ref[1] * q, q), q)], part_ref, sem
        )
        copy.start()
        copy.wait()
        value = part_ref[...].astype(F32)
    else:
        value = conv_grad_ref[...].astype(F32)
    col = lax.broadcasted_iota(jnp.int32, value.shape, 0) % w
    before = jnp.where(col == 0, 0.0, pltpu.roll(value, 1, 0)).astype(BF16)
    after = jnp.where(col == w - 1, 0.0, pltpu.roll(value, pixels - 1, 0)).astype(BF16)
    value = value.astype(BF16)
    blank = jnp.zeros((w, q), BF16)
    for i in range(3):
        for j in range(3):
            piece = (after, value, before)[j]
            lanes = slice((3 * i + j) * q, (3 * i + j + 1) * q)
            if i == 0:
                x9_ref[0 : pixels - w, lanes] = piece[w:, :]
                x9_ref[pixels - w : pixels, lanes] = blank
            elif i == 1:
                x9_ref[:, lanes] = piece
            else:
                x9_ref[w:pixels, lanes] = piece[: pixels - w, :]
                x9_ref[0:w, lanes] = blank
    share = c // sz.maps
    for i in range(3):
        term = lax.dot_general(
            act_ref[...],
            x9_ref[:, 3 * i * q : 3 * (i + 1) * q],
            (((0,), (0,)), ((), ())),
            preferred_element_type=F32,
        )
        for m in range(sz.maps):
            for j in range(3):
                out_ref[m, (3 * i + j) * share : (3 * i + j + 1) * share, :] = term[
                    m * share : (m + 1) * share, j * q : (j + 1) * q
                ].astype(out_ref.dtype)


def kernel_squares(sz, first_ref, second_ref, third_ref, totals2_ref, totals1_ref, totals0_ref,
                   shard_ref, squares_ref, norm_grad_ref):
    taps = third_ref.shape[0]
    received = first_ref[0].astype(F32)
    for m in range(1, sz.maps):
        received = received + first_ref[m].astype(F32)
    shard_ref[...] = received
    total = jnp.sum(received * received, axis=0, keepdims=True)
    for ref in (second_ref, third_ref):
        value = ref[...].astype(F32)
        total = total + jnp.sum(value * value, axis=0, keepdims=True)
    squares_ref[...] = jnp.broadcast_to(total[None], squares_ref.shape)
    for layer, ref in enumerate((totals0_ref, totals1_ref, totals2_ref)):
        shift_row, gain_row = split_rows(ref[...], sz.channels)
        norm_grad_ref[0, layer : layer + 1, :] = gain_row
        norm_grad_ref[1, layer : layer + 1, :] = shift_row


def adam(param, grad, first, second, rate, decay, scale, first_fix, second_fix):
    clipped = scale * grad
    first_new = first_decay * first + (1.0 - first_decay) * clipped
    second_new = second_decay * second + (1.0 - second_decay) * clipped * clipped
    update = first_new / first_fix / (jnp.sqrt(second_new / second_fix) + adam_epsilon)
    return first_new, second_new, param - rate * (update + decay * param)


def local(sz, block_input, conv_weights, norm_params, pool_index, task_mask, map_kind, map_domain, out_grad, step,
          conv_master, conv_moment1, conv_moment2, norm_moment1, norm_moment2):
    w, c, q = sz.width, sz.channels, sz.quarter
    half = w // 2
    n_maps, bands = sz.maps, sz.bands
    place = jnp.stack([lax.axis_index("maps"), lax.axis_index("rows")]).astype(jnp.int32)
    scalars = (map_kind, map_domain, place)
    smem3 = [spec_smem()] * 3
    forward = [(i, i + 1) for i in range(bands - 1)]
    backward = [(i + 1, i) for i in range(bands - 1)]
    x = block_input.reshape(sz.pixels, c)

    up = lax.ppermute(x[sz.pixels - HALO * w :], "rows", forward)
    down = lax.ppermute(x[: HALO * w], "rows", backward)

    def spread(stats):
        return lax.all_to_all(stats, AXES, 0, 0, tiled=True)

    stats_shape = jax.ShapeDtypeStruct((sz.devices, 8, c // 4), F32)
    tile_shape = jax.ShapeDtypeStruct((8, c // 4), F32)

    def pixel_shape(rows, dtype):
        return jax.ShapeDtypeStruct((rows * w, c), dtype)

    def conv_scratch(rows, acc_rows=None):
        shapes = [pltpu.VMEM((rows * w, 3 * c), BF16)]
        if acc_rows is not None:
            shapes.append(pltpu.VMEM((acc_rows * w, c), F32))
        return shapes + [pltpu.VMEM((9, c, c), BF16), pltpu.SemaphoreType.DMA((3,))]

    act_0 = lax.all_gather(x, "rows", axis=0, tiled=True)
    rows = sz.rows + 2 * HALO
    conv0, stats0 = pl.pallas_call(
        functools.partial(kernel_first, sz),
        out_shape=(pixel_shape(rows - 2, F32), stats_shape),
        in_specs=smem3 + [spec_vmem()] * 3 + [spec_any()],
        out_specs=(spec_vmem(), spec_vmem()),
        scratch_shapes=conv_scratch(rows),
        compiler_params=params(40),
        name="first",
    )(*scalars, up, x, down, conv_weights)
    gathered = spread(stats0)

    index = pool_index.reshape(sz.pixels // 4, c)
    index_up = lax.ppermute(index[sz.pixels // 4 - 2 * half :], "rows", forward)
    index_down = lax.ppermute(index[: 2 * half], "rows", backward)
    windows = sz.rows // 2
    padded = jnp.pad(out_grad.reshape(sz.height // 2 * half, q), ((2 * half, 2 * half), (0, 0)))
    pieces = jnp.stack(
        [padded[b * windows * half : (b * windows + windows + 4) * half] for b in range(bands)]
    )
    cotangent = lax.all_to_all(pieces, "rows", 0, 0, tiled=True)
    labels = jnp.pad(task_mask.reshape(sz.height // 2 * half), (2 * half, 2 * half)).astype(F32)
    labels = lax.dynamic_slice_in_dim(labels, place[1] * windows * half, (windows + 4) * half)
    labels = jnp.broadcast_to(labels[:, None], ((windows + 4) * half, 128))

    convs = [conv0]
    moments = []
    acts = [act_0]
    for layer in (1, 2):
        rows = sz.rows + 2 * (HALO - layer)
        conv, stats, act, moment = pl.pallas_call(
            functools.partial(kernel_forward, sz, layer),
            out_shape=(pixel_shape(rows - 2, F32), stats_shape, pixel_shape(sz.rows, BF16), tile_shape),
            in_specs=smem3 + [spec_vmem()] * 3 + [spec_any()],
            out_specs=(spec_vmem(),) * 4,
            scratch_shapes=conv_scratch(rows),
            compiler_params=params(40),
            name="forward",
        )(*scalars, convs[-1], gathered, norm_params, conv_weights)
        convs.append(conv)
        moments.append(moment)
        gathered = spread(stats)
        acts.append(lax.all_gather(act, "rows", axis=0, tiled=True))

    rows = sz.rows + 2 * (HALO - 3)
    pooled_chunks, stats, moment, grad = pl.pallas_call(
        functools.partial(kernel_pool, sz),
        out_shape=(
            jax.ShapeDtypeStruct((bands, sz.pixels // 4, q), BF16),
            stats_shape,
            tile_shape,
            pixel_shape(rows, F32),
        ),
        in_specs=smem3 + [spec_vmem()] * 8,
        out_specs=(spec_vmem(),) * 4,
        scratch_shapes=[pltpu.VMEM((c // 128, (rows + 2) * w, 128), F32), pltpu.VMEM((c // 128, rows * w, 128), F32)],
        compiler_params=params(40),
        name="pool",
    )(*scalars, convs[2], gathered, norm_params, index, index_up, index_down, cotangent, labels)
    moments.append(moment)
    gathered = spread(stats)
    pooled = lax.all_to_all(pooled_chunks, "rows", 0, 0, tiled=True)

    totals = [None, None, None]
    shards = [None, None, None]
    whole = sz.height * w
    share = 9 * (c // n_maps)

    def weight_grad(act, conv_grad, split):
        return pl.pallas_call(
            functools.partial(kernel_weight_grad, sz, split),
            out_shape=jax.ShapeDtypeStruct((n_maps, share, q), BF16),
            in_specs=[spec_smem(), spec_vmem(), spec_any() if split else spec_vmem()],
            out_specs=spec_vmem(),
            scratch_shapes=[
                pltpu.VMEM((whole, 9 * q), BF16),
                pltpu.VMEM((whole, q), BF16),
                pltpu.SemaphoreType.DMA,
            ],
            compiler_params=params(40),
            name="weight_grad",
        )(place, act, conv_grad)

    for layer in (2, 1):
        halo = layer + 1
        rows = sz.rows + 2 * halo
        grad, stats, conv_grad, totals[layer] = pl.pallas_call(
            functools.partial(kernel_backward, sz, layer),
            out_shape=(pixel_shape(rows - 2, F32), stats_shape, pixel_shape(sz.rows, BF16), tile_shape),
            in_specs=smem3 + [spec_vmem()] * 5 + [spec_any()] + [spec_vmem()] * 2,
            out_specs=(spec_vmem(),) * 4,
            scratch_shapes=conv_scratch(rows, rows - 2),
            compiler_params=params(40),
            name="backward",
        )(
            *scalars, grad, convs[layer], moments[layer], gathered, norm_params, conv_weights,
            convs[layer - 1], moments[layer - 1],
        )
        gathered = spread(stats)
        whole_grad = lax.all_gather(conv_grad, "rows", axis=0, tiled=True)
        partial = weight_grad(acts[layer], whole_grad, True)
        shards[layer] = lax.psum_scatter(
            partial.reshape(n_maps * share, q), "maps", scatter_dimension=0, tiled=True
        )

    conv_grad, chunks, totals[0] = pl.pallas_call(
        functools.partial(kernel_last_grad, sz),
        out_shape=(
            pixel_shape(sz.rows + 2, F32),
            jax.ShapeDtypeStruct((bands, sz.pixels, q), BF16),
            tile_shape,
        ),
        in_specs=smem3 + [spec_vmem()] * 5,
        out_specs=(spec_vmem(),) * 3,
        compiler_params=params(40),
        name="last_grad",
    )(*scalars, grad, convs[0], moments[0], gathered, norm_params)
    whole_grad = lax.all_to_all(chunks, "rows", 0, 0, tiled=True).reshape(whole, q)
    input_grad = pl.pallas_call(
        functools.partial(kernel_input_grad, sz),
        out_shape=pixel_shape(sz.rows, BF16),
        in_specs=[spec_vmem(), spec_any()],
        out_specs=spec_vmem(),
        scratch_shapes=conv_scratch(sz.rows + 2, sz.rows),
        compiler_params=params(40),
        name="input_grad",
    )(conv_grad, conv_weights)
    partial = weight_grad(acts[0], whole_grad, False)
    received = lax.all_to_all(partial, "maps", 0, 0, tiled=True)

    shard0, squares, norm_grad = pl.pallas_call(
        functools.partial(kernel_squares, sz),
        out_shape=(
            jax.ShapeDtypeStruct((share, q), F32),
            jax.ShapeDtypeStruct((sz.devices, 1, q), F32),
            jax.ShapeDtypeStruct((2, 3, c), F32),
        ),
        in_specs=[spec_vmem()] * 6,
        out_specs=(spec_vmem(),) * 3,
        compiler_params=params(40),
        name="squares",
    )(received, shards[1], shards[2], totals[2], totals[1], totals[0])
    every = lax.all_to_all(squares, AXES, 0, 0, tiled=True)
    total = jnp.sqrt(jnp.sum(every) + jnp.sum(norm_grad * norm_grad))
    scale = jnp.minimum(1.0, clip_limit / total)
    count = step[0].astype(F32)
    first_fix = 1.0 - jnp.power(first_decay, count)
    second_fix = 1.0 - jnp.power(second_decay, count)
    rate = 2.0 / math.sqrt(9.0 * c)
    kernel_grad = jnp.stack([shard0, shards[1].astype(F32), shards[2].astype(F32)]).reshape(conv_master.shape)
    conv_first, conv_second, conv_new = adam(
        conv_master, kernel_grad, conv_moment1, conv_moment2, rate, weight_decay, scale, first_fix, second_fix
    )
    norm_first, norm_second, norm_new = adam(
        norm_params, norm_grad, norm_moment1, norm_moment2, norm_rate, 0.0, scale, first_fix, second_fix
    )
    return (
        pooled.reshape(1, sz.height // 2, half, q),
        input_grad.reshape(block_input.shape),
        total.reshape(1),
        conv_first,
        conv_second,
        conv_new,
        norm_first,
        norm_second,
        norm_new,
    )


def solution(mesh):
    def run(*args):
        bands = mesh.shape["rows"]
        maps = mesh.shape["maps"]
        shape = args[0].shape
        sz = Sizes(maps, bands, shape[1] // bands, shape[2], shape[3])
        return jax.shard_map(
            functools.partial(local, sz),
            mesh=mesh,
            in_specs=(
                P("maps", "rows", None, None),
                P(),
                P(),
                P("maps", "rows", None, None),
                P("maps", None, None),
                P(),
                P(),
                P("maps", None, None, "rows"),
                P(),
                P(None, None, "maps", "rows"),
                P(None, None, "maps", "rows"),
                P(None, None, "maps", "rows"),
                P(),
                P(),
            ),
            out_specs=(
                P("maps", None, None, "rows"),
                P("maps", "rows", None, None),
                P(),
                P(None, None, "maps", "rows"),
                P(None, None, "maps", "rows"),
                P(None, None, "maps", "rows"),
                P(),
                P(),
                P(),
            ),
            check_vma=False,
        )(*args)

    return run
```

```python
import functools
import math

import jax
import jax.numpy as jnp
from jax import lax
from jax.experimental import pallas as pl
from jax.experimental.pallas import tpu as pltpu
from jax.sharding import PartitionSpec as P

DOMAINS = 4
norm_epsilon = 1e-05
clip_limit = 1.0
first_decay = 0.9
second_decay = 0.999
adam_epsilon = 1e-08
norm_rate = 0.5
weight_decay = 0.01

HALO = 6
SPACE = 28
AXES = ("maps", "rows")
F32 = jnp.float32
BF16 = jnp.bfloat16


class Sizes:
    def __init__(self, maps, bands, rows, width, channels):
        self.maps = maps
        self.bands = bands
        self.devices = maps * bands
        self.rows = rows
        self.width = width
        self.channels = channels
        self.height = rows * bands
        self.short_height = 2 * (self.height * 7 // 16)
        self.short_width = 2 * (width * 13 // 32)
        self.pixels = rows * width
        self.quarter = channels // bands


def spec(space):
    return pl.BlockSpec(memory_space=space)


def params(megabytes):
    return pltpu.CompilerParams(vmem_limit_bytes=megabytes << 20)


class Copies:
    def __init__(self, sems):
        self.sems = sems
        self.used = 0

    def start(self, source, target):
        copy = pltpu.make_async_copy(source, target, self.sems.at[self.used])
        self.used += 1
        copy.start()
        return copy


def wait(*copies):
    for copy in copies:
        copy.wait()


def line_share(ref, start, step, size):
    return ref.at[pl.ds(pl.multiple_of(start, step), size)]


def own_sums(gathered_ref, weights_ref):
    return jnp.sum(gathered_ref[...] * weights_ref[...], axis=0)


def all_sums(gathered_ref):
    return jnp.sum(gathered_ref[...], axis=0)


def split_rows(tile, channels):
    first = jnp.concatenate([tile[k : k + 1, :] for k in range(4)], axis=1)
    second = jnp.concatenate([tile[k : k + 1, :] for k in range(4, 8)], axis=1)
    return first, second


def join_rows(first, second):
    lanes = first.shape[1] // 4
    return jnp.concatenate(
        [row[:, k * lanes : (k + 1) * lanes] for row in (first, second) for k in range(4)], axis=0
    )


def tiled(sz, value):
    return jnp.concatenate([value] * (sz.channels // value.shape[1]), axis=1)


class Masks:
    def __init__(self, sz, limits_ref):
        self.col = lax.broadcasted_iota(jnp.int32, (sz.width, 128), 0)
        self.wide = jnp.where(self.col < limits_ref[2:3, :], 1.0, 0.0)
        self.inner_left = jnp.where(self.col > 0, 1.0, 0.0)
        self.inner_right = jnp.where(self.col < sz.width - 1, 1.0, 0.0)
        self.limits_ref = limits_ref

    def valid(self, row):
        inside = (self.limits_ref[0:1, :] <= row) & (self.limits_ref[1:2, :] > row)
        return self.wide * jnp.where(inside, 1.0, 0.0)

    def valid_of_map(self, row):
        return self.wide * jnp.where(self.limits_ref[3:4, :] > row, 1.0, 0.0)


def line(sz, row):
    return slice(row * sz.width, (row + 1) * sz.width)


def shifted_right(sz, masks, value):
    mask = masks.inner_left
    return pltpu.roll(value, 1, 0) * (mask if value.shape[1] == 128 else tiled(sz, mask))


def shifted_left(sz, masks, value):
    mask = masks.inner_right
    return pltpu.roll(value, sz.width - 1, 0) * (mask if value.shape[1] == 128 else tiled(sz, mask))


def put_shifted(sz, masks, x3_ref, row, value, reverse=False):
    before = shifted_right(sz, masks, value)
    after = shifted_left(sz, masks, value)
    if reverse:
        before, after = after, before
    c = sz.channels
    x3_ref[line(sz, row), 0:c] = before.astype(BF16)
    x3_ref[line(sz, row), c : 2 * c] = value.astype(BF16)
    x3_ref[line(sz, row), 2 * c : 3 * c] = after.astype(BF16)


def fold(value):
    total = value[0:8, :]
    for k in range(1, value.shape[0] // 8):
        total = total + value[8 * k : 8 * (k + 1), :]
    return total


HEAD = 2


class Weights:
    def __init__(self, copies, head_ref, weights_hbm, buffer_ref, layer):
        self.head_ref, self.buffer_ref = head_ref, buffer_ref
        self.loads = {
            first: copies.start(
                weights_hbm.at[layer, pl.ds(first, 3 - first % 3)],
                buffer_ref.at[pl.ds(first - HEAD, 3 - first % 3)],
            )
            for first in (HEAD, 3, 6)
        }

    def wait(self, tap):
        if tap in self.loads:
            wait(self.loads[tap])

    def taps(self, first, last):
        if first < HEAD:
            part = self.head_ref[first:last]
        else:
            part = self.buffer_ref[first - HEAD : last - HEAD]
        return part.reshape(-1, part.shape[-1])


def conv_rows(sz, x3_ref, weights, out_ref, rows, reverse=False):
    c, w = sz.channels, sz.width
    n = rows * w
    spans = [(0, HEAD), (HEAD, 3), (3, 6), (6, 9)]
    if reverse:
        spans = [(tap, tap + 1) for tap in range(9)]
    for first, last in spans:
        weights.wait(first)
        i = first // 3
        start = (2 - i if reverse else i) * w
        lhs = x3_ref[start : start + n, (first - 3 * i) * c : (last - 3 * i) * c]
        across = 1 if reverse else 0
        term = lax.dot_general(
            lhs, weights.taps(first, last), (((1,), (across,)), ((), ())), preferred_element_type=F32
        )
        if first == 0:
            out_ref[...] = term
        else:
            out_ref[...] += term


def put_stats(sz, first, second, out_ref):
    tile = join_rows(jnp.sum(first, axis=0, keepdims=True), jnp.sum(second, axis=0, keepdims=True))
    out_ref[...] = jnp.broadcast_to(tile[None], out_ref.shape)


def silu_parts(half):
    t = jnp.tanh(half)
    product = half * t
    return half + product, (0.5 + 0.5 * t) * (1.0 + (half - product))


class Stats:
    def __init__(self, sz):
        self.first = jnp.zeros((8, sz.channels), F32)
        self.second = jnp.zeros((8, sz.channels), F32)

    def add(self, first, second):
        self.first = self.first + fold(first)
        self.second = self.second + fold(second)


def add_conv_rows(sz, masks, stats, conv_ref, skip, first, last):
    for row in range(max(first, skip), min(last, skip + sz.rows)):
        value = conv_ref[line(sz, row), :]
        masked = value * tiled(sz, masks.valid(row - skip))
        stats.add(masked, masked * value)


def band_lanes(sz, n):
    return pl.ds(pl.multiple_of((lax.axis_index("rows") ^ n) * sz.quarter, sz.quarter), sz.quarter)


def send_shares(sz, copies, source_ref, targets, first):
    lines = source_ref.shape[0]
    return [
        copies.start(source_ref.at[:, band_lanes(sz, n)], target.at[pl.ds(first, lines)])
        for n, target in enumerate(targets)
    ]


def kernel_spans(sz, given_ref, *rest):
    shares = rest[: sz.bands]
    span = sz.rows // 2 * (sz.width // 2)
    for n, share in enumerate(shares):
        start = pl.multiple_of((lax.axis_index("rows") ^ n) * span, span)
        share[...] = given_ref[pl.ds(start, share.shape[0]), :]


def kernel_edges(sz, x_hbm, index_hbm, low_ref, high_ref, index_ref, sems):
    copies = Copies(sems)
    edge = HALO * sz.width
    few = sz.width
    lines = index_hbm.shape[0]
    first = copies.start(index_hbm.at[pl.ds(lines - few, few)], index_ref.at[0])
    second = copies.start(index_hbm.at[pl.ds(0, few)], index_ref.at[1])
    rest = [
        copies.start(x_hbm.at[pl.ds(sz.pixels - edge, edge)], low_ref.at[pl.ds(0, edge)]),
        copies.start(x_hbm.at[pl.ds(0, edge)], high_ref.at[pl.ds(0, edge)]),
    ]
    wait(first, second)
    low_ref[edge : edge + few, :] = index_ref[0].astype(BF16)
    high_ref[edge : edge + few, :] = index_ref[1].astype(BF16)
    wait(*rest)


def kernel_places(sz, kind_ref, domain_ref, limits_ref, member_ref, _):
    m, r = lax.axis_index("maps"), lax.axis_index("rows")
    start = r * sz.rows

    def rows_of(k):
        return jnp.where(kind_ref[k] == 1, sz.height, sz.short_height)

    def cols_of(k):
        return jnp.where(kind_ref[k] == 1, sz.short_width, sz.width)

    own = domain_ref[m]
    area = jnp.int32(0)
    for k in range(sz.maps):
        area = area + jnp.where(domain_ref[k] == own, rows_of(k) * cols_of(k), 0)
    tile = member_ref.shape[1:]
    weight = 1.0 / jnp.full(tile, area.astype(F32))
    for k in range(sz.maps):
        value = jnp.where(domain_ref[k] == own, weight, 0.0)
        for b in range(sz.bands):
            member_ref[k * sz.bands + b] = value
    line = lax.broadcasted_iota(jnp.int32, limits_ref.shape, 0)
    limits_ref[...] = jnp.where(
        line == 0, -start, jnp.where(line == 1, rows_of(m) - start, jnp.where(line == 2, cols_of(m), rows_of(m)))
    )


def kernel_first(sz, limits_ref, up_ref, x_ref, down_ref, head_ref, weights_hbm, stats_ref, conv_ref, x3_ref, buffer_ref, sems):
    weights = Weights(Copies(sems), head_ref, weights_hbm, buffer_ref, 0)
    masks = Masks(sz, limits_ref)
    stats = Stats(sz)

    def prepare(row):
        if row < HALO:
            value = up_ref[line(sz, row), :]
        elif row < HALO + sz.rows:
            value = x_ref[line(sz, row - HALO), :]
        else:
            value = down_ref[line(sz, row - HALO - sz.rows), :]
        put_shifted(sz, masks, x3_ref, row, value.astype(F32))

    def work(first, last):
        conv_rows(sz, x3_ref, weights, conv_ref, last)
        add_conv_rows(sz, masks, stats, conv_ref, HALO - 1, first, last)

    for row in range(sz.rows + 2 * HALO):
        prepare(row)
    work(0, sz.rows + 2 * HALO - 2)
    put_stats(sz, stats.first, stats.second, stats_ref)


def norm_of(sz, gathered_ref, member_ref):
    mean, squares = split_rows(own_sums(gathered_ref, member_ref), sz.channels)
    return mean, lax.rsqrt(squares - mean * mean + norm_epsilon)


def kernel_forward(sz, layer, limits_ref, member_ref, gathered_ref, before_ref, norm_ref, head_ref, weights_hbm, *rest):
    if layer == 1:
        stats_ref, conv_ref, moments_ref, act_hbm, saved_hbm, *shares, normed_ref, x3_ref, buffer_ref, sems = rest
    else:
        stats_ref, conv_ref, moments_ref, act_hbm, saved_hbm, x3_ref, buffer_ref, sems = rest
    copies = Copies(sems)
    weights = Weights(copies, head_ref, weights_hbm, buffer_ref, layer)
    halo = HALO - layer
    rows = sz.rows + 2 * halo
    skip = (halo - layer) * sz.width
    outs = []
    mean, inverse = norm_of(sz, gathered_ref, member_ref)
    moments_ref[...] = join_rows(mean, inverse)
    scale = 0.5 * norm_ref[layer - 1, 0:1, :] * inverse
    offset = 0.5 * norm_ref[layer - 1, 1:2, :] - mean * scale
    masks = Masks(sz, limits_ref)
    stats = Stats(sz)
    c = sz.channels

    def prepare(row):
        value = before_ref[line(sz, row), :]
        act, _ = silu_parts(value * scale + offset)
        put_shifted(sz, masks, x3_ref, row, act * tiled(sz, masks.valid(row - halo)))
        if layer == 1 and halo <= row < halo + sz.rows:
            normed_ref[line(sz, row - halo), :] = ((value - mean) * inverse).astype(BF16)
        if row == halo + sz.rows - 1:
            outs.append(copies.start(x3_ref.at[pl.ds(halo * sz.width, sz.pixels), pl.ds(c, c)], act_hbm))
            if layer == 1:
                outs.extend(send_shares(sz, copies, normed_ref, shares, 0))

    def work(first, last):
        conv_rows(sz, x3_ref, weights, conv_ref, last)
        outs.append(copies.start(before_ref.at[pl.ds(skip, saved_hbm.shape[0])], saved_hbm))
        add_conv_rows(sz, masks, stats, conv_ref, halo - 1, first, last)

    for row in range(rows):
        prepare(row)
    work(0, rows - 2)
    put_stats(sz, stats.first, stats.second, stats_ref)
    wait(*outs)


def kernel_pool(sz, limits_ref, member_ref, gathered_ref, before_ref, norm_ref, index_hbm, up_hbm, down_hbm, *rest):
    cotangents, rest = rest[: sz.bands], rest[sz.bands :]
    (stats_ref, grad_ref, normed_ref, moments_ref), rest = rest[:4], rest[4:]
    shares, rest = rest[: sz.bands], rest[sz.bands :]
    (index_ref, up_ref, down_ref, cotangent_ref, spread_ref, act_ref, pooled_ref, grad16_ref, normed16_ref, sems) = rest
    c, w = sz.channels, sz.width
    half = w // 2
    windows = sz.rows // 2
    edge = HALO * w
    copies = Copies(sems)
    inputs = [
        copies.start(index_hbm, index_ref),
        copies.start(up_hbm.at[pl.ds(edge, w)], up_ref),
        copies.start(down_hbm.at[pl.ds(edge, w)], down_ref),
    ]
    inputs += [
        copies.start(
            ref, cotangent_ref.at[:, band_lanes(sz, n)]
        )
        for n, ref in enumerate(cotangents)
    ]
    mean, inverse = norm_of(sz, gathered_ref, member_ref)
    moments_ref[...] = join_rows(mean, inverse)
    gain = 0.5 * norm_ref[2, 0:1, :]
    shift = 0.5 * norm_ref[2, 1:2, :]
    halo = HALO - 3
    rows = sz.rows + 2 * halo
    lines = sz.pixels // 4
    groups = c // 128
    masks = Masks(sz, limits_ref)
    for row in range(rows):
        normed = (before_ref[line(sz, row), :] - mean) * inverse
        normed_ref[line(sz, row), :] = normed.astype(BF16)
        act, slope = silu_parts(normed * gain + shift)
        valid = tiled(sz, masks.valid(row - halo))
        grad_ref[line(sz, row), :] = slope * valid
        if halo <= row < halo + sz.rows:
            normed16_ref[line(sz, row - halo), :] = normed.astype(BF16)
            act = act * valid
            for g in range(groups):
                act_ref[g, line(sz, row - halo), :] = act[:, g * 128 : (g + 1) * 128]
    outs = send_shares(sz, copies, normed16_ref, shares, lines + sz.pixels)
    wait(*inputs)
    for p in range(windows):
        index = index_ref[p * half : (p + 1) * half, :]
        result = jnp.zeros(index.shape, F32)
        for corner in range(4):
            start = (2 * p + corner // 2) * w + corner % 2
            taken = jnp.concatenate(
                [act_ref[g, pl.ds(start, half, stride=2), :] for g in range(groups)], axis=1
            )
            result = jnp.where(index == corner, taken, result)
        pooled_ref[p * half : (p + 1) * half, :] = result.astype(BF16)
    outs += send_shares(sz, copies, pooled_ref, shares, 0)
    for p in range(windows + 4):
        if p < 2:
            index = up_ref[p * half : (p + 1) * half, :].astype(jnp.int32)
        elif p < windows + 2:
            index = index_ref[(p - 2) * half : (p - 1) * half, :]
        else:
            first = (p - windows - 2) * half
            index = down_ref[first : first + half, :].astype(jnp.int32)
        given = cotangent_ref[p * half : (p + 1) * half, :].astype(F32)
        for corner in range(4):
            start = (2 * p + corner // 2) * w + corner % 2
            placed = jnp.where(index == corner, given, 0.0)
            for g in range(groups):
                spread_ref[g, pl.ds(start, half, stride=2), :] = placed[:, g * 128 : (g + 1) * 128]
    stats = Stats(sz)
    for row in range(rows):
        upstream = jnp.concatenate([spread_ref[g, line(sz, row + 1), :] for g in range(groups)], axis=1)
        grad = upstream * grad_ref[line(sz, row), :]
        grad_ref[line(sz, row), :] = grad
        if halo <= row < halo + sz.rows:
            grad16_ref[line(sz, row - halo), :] = grad.astype(BF16)
            stats.add(grad, grad * normed_ref[line(sz, row), :].astype(F32))
    outs += send_shares(sz, copies, grad16_ref, shares, lines)
    put_stats(sz, stats.first, stats.second, stats_ref)
    wait(*outs)


class ConvGrad:
    def __init__(self, sz, layer, masks, member_ref, moments_ref, gathered_ref, norm_ref):
        self.sz, self.masks = sz, masks
        _, inverse = split_rows(moments_ref[...], sz.channels)
        one, two = split_rows(own_sums(gathered_ref, member_ref), sz.channels)
        self.scale = norm_ref[layer, 0:1, :] * inverse
        self.one, self.two = one, two

    def row(self, row, grad, normed):
        value = self.scale * (grad - self.one - normed * self.two)
        return value * tiled(self.sz, self.masks.valid(row))


def kernel_backward(sz, layer, limits_ref, member_ref, gathered_ref, grad_ref, normed_ref, moments_ref, norm_ref,
                    head_ref, weights_hbm, saved_hbm, moments_below_ref, stats_ref, below_ref, normed_below_ref, totals_ref,
                    *rest):
    shares, (saved_ref, x3_ref, buffer_ref, grad16_ref, normed16_ref, sems) = rest[: sz.bands], rest[sz.bands :]
    copies = Copies(sems)
    weights = Weights(copies, head_ref, weights_hbm, buffer_ref, layer)
    saved = copies.start(saved_hbm, saved_ref)
    halo = layer + 1
    rows = sz.rows + 2 * halo
    masks = Masks(sz, limits_ref)
    conv_grad = ConvGrad(sz, layer, masks, member_ref, moments_ref, gathered_ref, norm_ref)
    below = layer - 1
    mean, inverse = split_rows(moments_below_ref[...], sz.channels)
    gain = 0.5 * norm_ref[below, 0:1, :]
    shift = 0.5 * norm_ref[below, 1:2, :]
    stats = Stats(sz)
    outs = []

    def prepare(row):
        value = conv_grad.row(row - halo, grad_ref[line(sz, row), :], normed_ref[line(sz, row), :].astype(F32))
        put_shifted(sz, masks, x3_ref, row, value, True)

    def work(first, last):
        conv_rows(sz, x3_ref, weights, below_ref, last, True)
        if first == 0:
            wait(saved)
        for row in range(first, last):
            normed = (saved_ref[line(sz, row), :] - mean) * inverse
            normed_below_ref[line(sz, row), :] = normed.astype(BF16)
            _, slope = silu_parts(normed * gain + shift)
            own = row - (halo - 1)
            grad = below_ref[line(sz, row), :] * slope * tiled(sz, masks.valid(own))
            below_ref[line(sz, row), :] = grad
            if 0 <= own < sz.rows:
                grad16_ref[line(sz, own), :] = grad.astype(BF16)
                if below > 0:
                    normed16_ref[line(sz, own), :] = normed.astype(BF16)
                stats.add(grad, grad * normed)

    for row in range(rows):
        prepare(row)
    work(0, rows - 2)
    outs += send_shares(sz, copies, grad16_ref, shares, 0)
    if below > 0:
        outs += send_shares(sz, copies, normed16_ref, shares, sz.pixels)
    put_stats(sz, stats.first, stats.second, stats_ref)
    totals_ref[...] = all_sums(gathered_ref)
    wait(*outs)


def kernel_last(sz, limits_ref, member_ref, gathered_ref, grad_ref, normed_ref, moments_ref, norm_ref, head_ref,
                weights_hbm, *rest):
    parts, (out_hbm, totals_ref, pooled_hbm, x3_ref, buffer_ref, acc_ref, out_ref, sems) = (
        rest[: sz.bands], rest[sz.bands :]
    )
    copies = Copies(sems)
    weights = Weights(copies, head_ref, weights_hbm, buffer_ref, 0)
    lines = sz.pixels // 4
    outs = []
    for n, ref in enumerate(parts):
        target = line_share(pooled_hbm, (lax.axis_index("rows") ^ n) * lines, lines, lines)
        outs.append(copies.start(ref.at[pl.ds(0, lines)], target))
    totals_ref[...] = all_sums(gathered_ref)
    masks = Masks(sz, limits_ref)
    conv_grad = ConvGrad(sz, 0, masks, member_ref, moments_ref, gathered_ref, norm_ref)

    def prepare(row):
        value = conv_grad.row(row - 1, grad_ref[line(sz, row), :], normed_ref[line(sz, row), :].astype(F32))
        put_shifted(sz, masks, x3_ref, row, value, True)

    def work(first, last):
        conv_rows(sz, x3_ref, weights, acc_ref, last, True)
        pixels = slice(first * sz.width, last * sz.width)
        out_ref[pixels, :] = acc_ref[pixels, :].astype(BF16)

    for row in range(sz.rows + 2):
        prepare(row)
    work(0, sz.rows)
    outs.append(copies.start(out_ref, out_hbm))
    wait(*outs)


def kernel_weight_grad(sz, layer, first, limits_ref, member_ref, gathered_ref, moments_ref, norm_ref, *rest):
    w, q, c, bands = sz.width, sz.quarter, sz.channels, sz.bands
    pixels = sz.height * w
    given, rest = rest[:bands], rest[bands:]
    values, rest = rest[:bands], rest[bands:]
    acts, rest = rest[:bands], rest[bands:]
    if layer == 0:
        out_ref, grad_ref, normed_ref, act_ref, x9_ref, sems = rest
    else:
        (keep_hbm, send_hbm, grad_ref, normed_ref, act_ref, x9_ref, keep_ref, send_ref, term_ref,
         sems) = rest
    copies = Copies(sems)
    inputs = []
    for n in range(bands):
        start = (lax.axis_index("rows") ^ n) * sz.pixels
        for source, target, top in ((given[n], grad_ref, first[0]), (values[n], normed_ref, first[1])):
            inputs.append(
                copies.start(source.at[pl.ds(top, sz.pixels)], line_share(target, start, sz.pixels, sz.pixels))
            )
    act_loads = [
        copies.start(
            acts[n], line_share(act_ref, (lax.axis_index("rows") ^ n) * sz.pixels, sz.pixels, sz.pixels)
        )
        for n in range(bands)
    ]
    band = lax.axis_index("rows")
    own = lax.axis_index("maps")
    tile = own_sums(gathered_ref, member_ref)
    one, two, inverse, gain = (jnp.zeros((1, q), F32) for _ in range(4))
    for b in range(bands):
        here = band == b
        one = jnp.where(here, tile[b : b + 1, :], one)
        two = jnp.where(here, tile[b + 4 : b + 5, :], two)
        inverse = jnp.where(here, moments_ref[b + 4 : b + 5, :], inverse)
        gain = jnp.where(here, norm_ref[layer, 0:1, b * q : (b + 1) * q], gain)
    wait(*inputs)
    masks = Masks(sz, limits_ref)
    blank = jnp.zeros((w, q), BF16)
    for row in range(sz.height):
        value = grad_ref[line(sz, row), :].astype(F32) - one - normed_ref[line(sz, row), :].astype(F32) * two
        value = (gain * inverse) * value * masks.valid_of_map(row)
        for j, piece in enumerate((shifted_left(sz, masks, value), value, shifted_right(sz, masks, value))):
            piece = piece.astype(BF16)
            for i in range(3):
                if 0 <= row + i - 1 < sz.height:
                    x9_ref[line(sz, row + i - 1), (3 * i + j) * q : (3 * i + j + 1) * q] = piece
    for j in range(3):
        x9_ref[line(sz, sz.height - 1), j * q : (j + 1) * q] = blank
        x9_ref[line(sz, 0), (6 + j) * q : (7 + j) * q] = blank
    share = c // sz.maps
    wait(*act_loads)
    term = lax.dot_general(
        act_ref[...], x9_ref[...], (((0,), (0,)), ((), ())), preferred_element_type=F32
    )
    if layer == 0:
        for tap in range(9):
            part = term[:, tap * q : (tap + 1) * q].astype(BF16)
            for m in range(sz.maps):
                out_ref[m, tap * share : (tap + 1) * share, :] = part[m * share : (m + 1) * share, :]
        return
    term_ref[...] = term
    for position, relative in enumerate(halving_order(sz.maps)):
        lines = pl.ds(pl.multiple_of((own ^ relative) * share, share), share)
        for tap in range(9):
            place = slice(tap * share, (tap + 1) * share)
            part = term_ref[lines, tap * q : (tap + 1) * q]
            if position < sz.maps // 2:
                keep_ref[position, place, :] = part
            else:
                send_ref[position - sz.maps // 2, place, :] = part.astype(BF16)
    wait(copies.start(keep_ref, keep_hbm), copies.start(send_ref, send_hbm))


def halving_order(maps):
    bits = maps.bit_length() - 1
    return [sum(((place >> (bits - 1 - k)) & 1) << k for k in range(bits)) for place in range(maps)]


def kernel_halve(keep_hbm, received_hbm, next_keep_hbm, next_send_hbm, keep_ref, received_ref, send_ref, sems):
    half = next_keep_hbm.shape[0]
    copies = Copies(sems)
    loads = [
        [
            copies.start(source.at[part], target.at[part])
            for source, target in ((keep_hbm, keep_ref), (received_hbm, received_ref))
        ]
        for part in (pl.ds(half, half), pl.ds(0, half))
    ]
    wait(*loads[0])
    send_ref[...] = (keep_ref[half:] + received_ref[half:].astype(F32)).astype(BF16)
    first = copies.start(send_ref, next_send_hbm)
    wait(*loads[1])
    keep_ref[:half] += received_ref[:half].astype(F32)
    wait(first, copies.start(keep_ref.at[pl.ds(0, half)], next_keep_hbm))


def kernel_squares(sz, received_ref, keep1_ref, last1_ref, keep2_ref, last2_ref, totals2_ref, totals1_ref,
                   totals0_ref, squares_ref, shard_ref, norm_grad_ref, _):
    value = received_ref[0].astype(F32)
    for m in range(1, sz.maps):
        value = value + received_ref[m].astype(F32)
    values = [value, keep1_ref[0] + last1_ref[0].astype(F32), keep2_ref[0] + last2_ref[0].astype(F32)]
    total = jnp.zeros((1, sz.quarter), F32)
    for layer, value in enumerate(values):
        shard_ref[layer] = value
        total = total + jnp.sum(value * value, axis=0, keepdims=True)
    squares_ref[...] = jnp.broadcast_to(total[None], squares_ref.shape)
    for layer, ref in enumerate((totals0_ref, totals1_ref, totals2_ref)):
        shift_row, gain_row = split_rows(ref[...], sz.channels)
        norm_grad_ref[layer, 0:1, :] = gain_row
        norm_grad_ref[layer, 1:2, :] = shift_row


def kernel_adam(sz, rate, every_ref, step_ref, shard_ref, master_hbm, first_hbm, second_hbm, norm_grad_ref, norm_ref,
                norm_first_ref, norm_second_ref, total_hbm, first_out_hbm, second_out_hbm, master_out_hbm,
                norm_first_hbm, norm_second_hbm, norm_hbm,
                total_ref, master_ref, first_ref, second_ref, small_ref, sems):
    copies = Copies(sems)
    loads = [
        [
            copies.start(source.at[layer], target.at[layer])
            for source, target in ((master_hbm, master_ref), (first_hbm, first_ref), (second_hbm, second_ref))
        ]
        for layer in range(3)
    ]
    norm_grad = norm_grad_ref[...]
    square = jnp.sum(jnp.sum(every_ref[...], axis=0)) + jnp.sum(norm_grad * norm_grad)
    total = jnp.sqrt(jnp.full((1, 128), square, F32))
    total_ref[...] = total
    outs = [copies.start(total_ref, total_hbm)]
    scale = jnp.minimum(1.0, clip_limit / total)
    count = jnp.full((1, 128), step_ref[0].astype(F32), F32)
    first_fix = 1.0 - jnp.exp(count * math.log(first_decay))
    second_fix = 1.0 - jnp.exp(count * math.log(second_decay))
    for layer in range(3):
        wait(*loads[layer])
        first_ref[layer], second_ref[layer], master_ref[layer] = adam(
            master_ref[layer], shard_ref[layer], first_ref[layer], second_ref[layer], rate, weight_decay,
            scale, first_fix, second_fix,
        )
        for source, target in (
            (first_ref, first_out_hbm), (second_ref, second_out_hbm), (master_ref, master_out_hbm)
        ):
            outs.append(copies.start(source.at[layer], target.at[layer]))
    wide = [jnp.concatenate([v] * (sz.channels // 128), axis=1) for v in (scale, first_fix, second_fix)]
    for layer in range(3):
        small_ref[0, layer], small_ref[1, layer], small_ref[2, layer] = adam(
            norm_ref[layer], norm_grad[layer], norm_first_ref[layer], norm_second_ref[layer], norm_rate, 0.0, *wide
        )
    for k, target in enumerate((norm_first_hbm, norm_second_hbm, norm_hbm)):
        outs.append(copies.start(small_ref.at[k], target))
    wait(*outs)


def adam(param, grad, first, second, rate, decay, scale, first_fix, second_fix):
    clipped = scale * grad
    first_new = first_decay * first + (1.0 - first_decay) * clipped
    second_new = second_decay * second + (1.0 - second_decay) * clipped * clipped
    update = first_new / first_fix / (jnp.sqrt(second_new / second_fix) + adam_epsilon)
    return first_new, second_new, param - rate * (update + decay * param)


def call(kernel, name, outs, ins, scratch=(), flops=0, moved=0, hbm_ins=(), hbm_outs=(), smem_ins=()):
    spaces_in = [
        pltpu.SMEM if k in smem_ins else pltpu.HBM if k in hbm_ins else pltpu.VMEM for k in range(len(ins))
    ]
    spaces_out = [pltpu.HBM if k in hbm_outs else pltpu.VMEM for k in range(len(outs))]
    return pl.pallas_call(
        kernel,
        out_shape=tuple(space(out.shape, out.dtype) for space, out in zip(spaces_out, outs)),
        in_specs=[spec(space) for space in spaces_in],
        out_specs=tuple(spec(space) for space in spaces_out),
        scratch_shapes=list(scratch) + [pltpu.SemaphoreType.DMA((32,))],
        compiler_params=params(SPACE),
        cost_estimate=pl.CostEstimate(flops=flops // 8, bytes_accessed=moved, transcendentals=0),
        name=name,
    )(*[v if k in smem_ins else pltpu.with_memory_space_constraint(v, spaces_in[k]) for k, v in enumerate(ins)])


def local(sz, block_input, conv_weights, norm_params, pool_index, task_mask, map_kind, map_domain, out_grad, step,
          conv_master, conv_moment1, conv_moment2, norm_moment1, norm_moment2):
    w, c, q = sz.width, sz.channels, sz.quarter
    half = w // 2
    n_maps, bands = sz.maps, sz.bands
    forward = [(i, i + 1) for i in range(bands - 1)]
    backward = [(i + 1, i) for i in range(bands - 1)]
    x = block_input.reshape(sz.pixels, c)
    index = pool_index.reshape(sz.pixels // 4, c)
    norms, norm_first, norm_second = (v.transpose(1, 0, 2) for v in (norm_params, norm_moment1, norm_moment2))
    edge = HALO * w
    lines = sz.pixels // 4

    def shape(dims, dtype):
        return jax.ShapeDtypeStruct(dims, dtype)

    def pixel_shape(rows, dtype):
        return shape((rows * w, c), dtype)

    def pixel_space(rows, dtype, times=1):
        return pltpu.VMEM((rows * w, times * c), dtype)

    def share_shapes(count):
        return [shape((count, q), BF16)] * bands

    stats_shape = shape((sz.devices, 8, c // 4), F32)
    tile_shape = shape((8, c // 4), F32)
    weight_space = pltpu.VMEM((9 - HEAD, c, c), BF16)


    def conv_flops(rows):
        return rows * w * 9 * c * c * 2

    def spread(stats):
        return lax.all_to_all(stats, AXES, 0, 0, tiled=True)

    def trade(shares):
        return [shares[0]] + [
            lax.ppermute(shares[n], "rows", [(i, i ^ n) for i in range(bands)]) for n in range(1, bands)
        ]

    def swap(act, n):
        return lax.ppermute(act, "rows", [(i, i ^ n) for i in range(bands)])

    tie = lax.optimization_barrier

    low, high = call(
        functools.partial(kernel_edges, sz), "edges",
        [shape((edge + 2 * half, c), BF16)] * 2, [x, index],
        [pltpu.VMEM((2, 2 * half, c), jnp.int32)], hbm_ins=(0, 1),
    )
    up = lax.ppermute(low, "rows", forward)
    down = lax.ppermute(high, "rows", backward)

    limits, member = call(
        functools.partial(kernel_places, sz), "places", [shape((8, 128), jnp.int32), stats_shape],
        [map_kind, map_domain], smem_ins=(0, 1),
    )
    labelled = (out_grad * task_mask[..., None].astype(BF16)).reshape(sz.height // 2 * half, q)
    labelled = jnp.pad(labelled, ((2 * half, 2 * half), (0, 0)))
    consts = [limits, member]

    rows = sz.rows + 2 * HALO
    stats, conv = call(
        functools.partial(kernel_first, sz), "first",
        [stats_shape, pixel_shape(rows - 2, F32)], [limits, up, x, down, conv_weights[0, :HEAD], conv_weights],
        [pixel_space(rows, BF16, 3), weight_space], conv_flops(rows - 2), hbm_ins=(5,),
    )
    def head(layer, weights):
        return weights[layer, :HEAD]

    cot_lines = (sz.rows // 2 + 4) * half
    cots = call(functools.partial(kernel_spans, sz), "spans", share_shapes(cot_lines), [labelled])
    stats, kept, weights, *cots = tie((stats, x, conv_weights, *cots))
    gathered = spread(stats)
    cots = trade(cots)
    acts = [[kept, swap(kept, 1), swap(kept, 2)]]
    moments = []
    saves = []
    for layer in (1, 2):
        rows = sz.rows + 2 * (HALO - layer)
        outs = [
            stats_shape, pixel_shape(rows - 2, F32), tile_shape, pixel_shape(sz.rows, BF16),
            pixel_shape(sz.rows + 2 * layer, F32),
        ]
        scratch = [pixel_space(rows, BF16, 3), weight_space]
        if layer == 1:
            outs += share_shapes(sz.pixels)
            scratch = [pixel_space(sz.rows, BF16)] + scratch
        stats, conv, moment, act, saved, *shares = call(
            functools.partial(kernel_forward, sz, layer), "forward", outs,
            consts + [gathered, conv, norms, head(layer, weights), conv_weights], scratch,
            conv_flops(rows - 2), hbm_ins=(6,), hbm_outs=range(3, 9),
        )
        moments.append(moment)
        saves.append(saved)
        if layer == 1:
            stats, weights = tie((stats, conv_weights))
            gathered = spread(stats)
            given0 = trade(shares)
        else:
            stats, *rest = tie((stats, *cots, *acts[0]))
            cots, acts[0] = rest[:bands], rest[bands:]
            gathered = spread(stats)
            acts[0].append(swap(acts[0][2], 1))
        acts.append([act, swap(act, 1), swap(act, 2)])

    rows = sz.rows + 2 * (HALO - 3)
    stats, grad, normed, moment, *shares = call(
        functools.partial(kernel_pool, sz), "pool",
        [stats_shape, pixel_shape(rows, F32), pixel_shape(rows, BF16), tile_shape]
        + share_shapes(lines + 2 * sz.pixels),
        consts + [gathered, conv, norms, index, up, down] + cots,
        [
            pltpu.VMEM((lines, c), jnp.int32), pltpu.VMEM((2 * half, c), BF16), pltpu.VMEM((2 * half, c), BF16),
            pltpu.VMEM((cot_lines, c), BF16),
            pltpu.VMEM((c // 128, (rows + 2) * w, 128), F32), pltpu.VMEM((c // 128, sz.pixels, 128), F32),
            pltpu.VMEM((lines, c), BF16), pixel_space(sz.rows, BF16), pixel_space(sz.rows, BF16),
        ],
        conv_flops(4), hbm_ins=range(5, 12), hbm_outs=range(4, 8),
    )
    moments.append(moment)
    stats, weights, *rest = tie((stats, conv_weights, *given0, *acts[1]))
    given0, acts[1] = rest[:bands], rest[bands:]
    gathered = spread(stats)
    exchanged = trade(shares)
    acts[1].append(swap(acts[1][2], 1))
    pooled_parts = exchanged

    totals = [None, None, None]
    share = 9 * (c // n_maps)
    steps = n_maps.bit_length() - 1

    def part_shape(parts, dtype):
        return shape((parts, share, q), dtype)

    def part_space(parts, dtype):
        return pltpu.VMEM((parts, share, q), dtype)

    def weight_grad(layer, gathered, given, first, normed=None):
        scratch = [
            pltpu.VMEM((sz.height * w, q), BF16),
            pltpu.VMEM((sz.height * w, q), BF16),
            pltpu.VMEM((sz.height * w, c), BF16),
            pltpu.VMEM((sz.height * w, 9 * q), BF16),
        ]
        if layer == 0:
            outs = [part_shape(n_maps, BF16)]
        else:
            outs = [part_shape(n_maps // 2, dtype) for dtype in (F32, BF16)]
            scratch += [part_space(n_maps // 2, dtype) for dtype in (F32, BF16)]
            scratch.append(pltpu.VMEM((c, 9 * q), F32))
        return call(
            functools.partial(kernel_weight_grad, sz, layer, first), "weight_grad", outs,
            consts + [gathered, moments[layer], norms] + given + (normed or given) + acts[layer], scratch, conv_flops(sz.rows),
            hbm_ins=range(5, 17), hbm_outs=() if layer == 0 else (0, 1),
        )

    def halve(keep, send):
        for k in range(steps):
            received = lax.ppermute(send, "maps", [(m, m ^ (1 << k)) for m in range(n_maps)])
            if k == steps - 1:
                return keep, received
            size = keep.shape[0] // 2
            keep, send = call(
                kernel_halve, "halve", [part_shape(size, dtype) for dtype in (F32, BF16)], [keep, received],
                [part_space(2 * size, F32), part_space(2 * size, BF16), part_space(size, BF16)],
                hbm_ins=(0, 1), hbm_outs=(0, 1),
            )

    shards = [None, None, None]
    for layer in (2, 1):
        halo = layer + 1
        rows = sz.rows + 2 * halo
        received, gathered_here = exchanged, gathered
        stats, grad, normed, totals[layer], *shares = call(
            functools.partial(kernel_backward, sz, layer), "backward",
            [stats_shape, pixel_shape(rows - 2, F32), pixel_shape(rows - 2, BF16), tile_shape]
            + share_shapes(sz.pixels * (2 if layer == 2 else 1)),
            consts + [
                gathered, grad, normed, moments[layer], norms, head(layer, weights), conv_weights, saves[layer - 1],
                moments[layer - 1],
            ],
            [
                pixel_space(rows - 2, F32), pixel_space(rows, BF16, 3), weight_space, pixel_space(sz.rows, BF16),
                pixel_space(sz.rows, BF16),
            ],
            conv_flops(rows - 2), hbm_ins=(8, 9), hbm_outs=range(4, 8),
        )
        if layer == 2:
            stats, weights, acts[0][3], acts[1][3], *acts[2] = tie(
                (stats, conv_weights, acts[0][3], acts[1][3], *acts[2])
            )
            gathered = spread(stats)
            exchanged = trade(shares)
            acts[2].append(swap(acts[2][2], 1))
            keep2, send2 = weight_grad(2, gathered_here, received, (lines, lines + sz.pixels))
        else:
            stats, weights, send2 = tie((stats, conv_weights, send2))
            gathered = spread(stats)
            exchanged = trade(shares)
            keep1, send1 = weight_grad(1, gathered_here, received, (0, sz.pixels))

    send1, late = tie((send1, exchanged))
    (partial,) = weight_grad(0, gathered, late, (0, 0), given0)
    received = lax.all_to_all(partial, "maps", 0, 0, tiled=True)
    shards[2] = halve(keep2, send2)
    shards[1] = halve(keep1, send1)
    input_grad, totals[0], pooled = call(
        functools.partial(kernel_last, sz), "last",
        [pixel_shape(sz.rows, BF16), tile_shape, shape((sz.height // 2 * half, q), BF16)],
        consts + [gathered, grad, normed, moments[0], norms, head(0, weights), conv_weights] + pooled_parts,
        [pixel_space(sz.rows + 2, BF16, 3), weight_space, pixel_space(sz.rows, F32), pixel_space(sz.rows, BF16)],
        conv_flops(sz.rows), hbm_ins=range(8, 13), hbm_outs=(0, 2),
    )

    norm_shape = shape((3, 2, c), F32)
    squares, shard, norm_grad = call(
        functools.partial(kernel_squares, sz), "squares",
        [shape((sz.devices, 1, q), F32), part_shape(3, F32), norm_shape],
        [received, *shards[1], *shards[2], totals[2], totals[1], totals[0]],
    )
    every = lax.all_to_all(squares, AXES, 0, 0, tiled=True)
    rate = 2.0 / math.sqrt(9.0 * c)
    total, conv_first, conv_second, conv_new, norm_first, norm_second, norm_new = call(
        functools.partial(kernel_adam, sz, rate), "adam",
        [shape((1, 128), F32)] + [part_shape(3, F32)] * 3 + [norm_shape] * 3,
        [every, step, shard]
        + [v.reshape(3, share, q) for v in (conv_master, conv_moment1, conv_moment2)]
        + [norm_grad, norms, norm_first, norm_second],
        [pltpu.VMEM((1, 128), F32)] + [part_space(3, F32)] * 3 + [pltpu.VMEM((3, 3, 2, c), F32)],
        hbm_ins=(3, 4, 5), hbm_outs=range(7), smem_ins=(1,),
    )
    return (
        pooled.reshape(1, sz.height // 2, half, q),
        input_grad.reshape(block_input.shape),
        total[0, :1],
        conv_first.reshape(conv_master.shape),
        conv_second.reshape(conv_master.shape),
        conv_new.reshape(conv_master.shape),
        norm_first.transpose(1, 0, 2),
        norm_second.transpose(1, 0, 2),
        norm_new.transpose(1, 0, 2),
    )


def solution(mesh):
    def run(*args):
        bands = mesh.shape["rows"]
        maps = mesh.shape["maps"]
        shape = args[0].shape
        sz = Sizes(maps, bands, shape[1] // bands, shape[2], shape[3])
        return jax.shard_map(
            functools.partial(local, sz),
            mesh=mesh,
            in_specs=(
                P("maps", "rows", None, None),
                P(),
                P(),
                P("maps", "rows", None, None),
                P("maps", None, None),
                P(),
                P(),
                P("maps", None, None, "rows"),
                P(),
                P(None, None, "maps", "rows"),
                P(None, None, "maps", "rows"),
                P(None, None, "maps", "rows"),
                P(),
                P(),
            ),
            out_specs=(
                P("maps", None, None, "rows"),
                P("maps", "rows", None, None),
                P(),
                P(None, None, "maps", "rows"),
                P(None, None, "maps", "rows"),
                P(None, None, "maps", "rows"),
                P(),
                P(),
                P(),
            ),
            check_vma=False,
        )(*args)

    return run
```

```python
import functools
import math

import jax
import jax.numpy as jnp
from jax import lax
from jax.experimental import pallas as pl
from jax.experimental.pallas import tpu as pltpu
from jax.sharding import PartitionSpec as P

DOMAINS = 4
norm_epsilon = 1e-05
clip_limit = 1.0
first_decay = 0.9
second_decay = 0.999
adam_epsilon = 1e-08
norm_rate = 0.5
weight_decay = 0.01

HALO = 6
SPACE = 28
AXES = ("maps", "rows")
F32 = jnp.float32
BF16 = jnp.bfloat16


class Sizes:
    def __init__(self, maps, bands, rows, width, channels):
        self.maps = maps
        self.bands = bands
        self.devices = maps * bands
        self.rows = rows
        self.width = width
        self.channels = channels
        self.height = rows * bands
        self.short_height = 2 * (self.height * 7 // 16)
        self.short_width = 2 * (width * 13 // 32)
        self.pixels = rows * width
        self.quarter = channels // bands


def spec(space):
    return pl.BlockSpec(memory_space=space)


def params(megabytes):
    return pltpu.CompilerParams(vmem_limit_bytes=megabytes << 20)


class Copies:
    def __init__(self, sems):
        self.sems = sems
        self.used = 0

    def start(self, source, target):
        copy = pltpu.make_async_copy(source, target, self.sems.at[self.used])
        self.used += 1
        copy.start()
        return copy


def wait(*copies):
    for copy in copies:
        copy.wait()


def line_share(ref, start, step, size):
    return ref.at[pl.ds(pl.multiple_of(start, step), size)]


def own_sums(gathered_ref, weights_ref):
    return jnp.sum(gathered_ref[...] * weights_ref[...], axis=0)


def all_sums(gathered_ref):
    return jnp.sum(gathered_ref[...], axis=0)


def split_rows(tile, channels):
    first = jnp.concatenate([tile[k : k + 1, :] for k in range(4)], axis=1)
    second = jnp.concatenate([tile[k : k + 1, :] for k in range(4, 8)], axis=1)
    return first, second


def join_rows(first, second):
    lanes = first.shape[1] // 4
    return jnp.concatenate(
        [row[:, k * lanes : (k + 1) * lanes] for row in (first, second) for k in range(4)], axis=0
    )


def tiled(sz, value):
    return jnp.concatenate([value] * (sz.channels // value.shape[1]), axis=1)


class Masks:
    def __init__(self, sz, limits_ref):
        self.col = lax.broadcasted_iota(jnp.int32, (sz.width, 128), 0)
        self.wide = jnp.where(self.col < limits_ref[2:3, :], 1.0, 0.0)
        self.inner_left = jnp.where(self.col > 0, 1.0, 0.0)
        self.inner_right = jnp.where(self.col < sz.width - 1, 1.0, 0.0)
        self.limits_ref = limits_ref

    def valid(self, row):
        inside = (self.limits_ref[0:1, :] <= row) & (self.limits_ref[1:2, :] > row)
        return self.wide * jnp.where(inside, 1.0, 0.0)

    def valid_of_map(self, row):
        return self.wide * jnp.where(self.limits_ref[3:4, :] > row, 1.0, 0.0)


def line(sz, row):
    return slice(row * sz.width, (row + 1) * sz.width)


def shifted_right(sz, masks, value):
    mask = masks.inner_left
    return pltpu.roll(value, 1, 0) * (mask if value.shape[1] == 128 else tiled(sz, mask))


def shifted_left(sz, masks, value):
    mask = masks.inner_right
    return pltpu.roll(value, sz.width - 1, 0) * (mask if value.shape[1] == 128 else tiled(sz, mask))


def put_shifted(sz, masks, x3_ref, row, value, reverse=False):
    before = shifted_right(sz, masks, value)
    after = shifted_left(sz, masks, value)
    if reverse:
        before, after = after, before
    c = sz.channels
    x3_ref[line(sz, row), 0:c] = before.astype(BF16)
    x3_ref[line(sz, row), c : 2 * c] = value.astype(BF16)
    x3_ref[line(sz, row), 2 * c : 3 * c] = after.astype(BF16)


def fold(value):
    total = value[0:8, :]
    for k in range(1, value.shape[0] // 8):
        total = total + value[8 * k : 8 * (k + 1), :]
    return total


HEAD = 1


class Weights:
    def __init__(self, copies, head_ref, weights_hbm, buffer_ref, layer):
        self.head_ref, self.buffer_ref = head_ref, buffer_ref
        self.loads = {
            first: copies.start(
                weights_hbm.at[layer, pl.ds(first, 3 - first % 3)],
                buffer_ref.at[pl.ds(first - HEAD, 3 - first % 3)],
            )
            for first in (HEAD, 3, 6)
        }

    def wait(self, tap):
        if tap in self.loads:
            wait(self.loads[tap])

    def taps(self, first, last):
        if first < HEAD:
            part = self.head_ref[first:last]
        else:
            part = self.buffer_ref[first - HEAD : last - HEAD]
        return part.reshape(-1, part.shape[-1])


def conv_rows(sz, x3_ref, weights, out_ref, rows, reverse=False):
    c, w = sz.channels, sz.width
    n = rows * w
    spans = [(0, HEAD), (HEAD, 3), (3, 6), (6, 9)]
    if reverse:
        spans = [(tap, tap + 1) for tap in range(9)]
    for first, last in spans:
        weights.wait(first)
        i = first // 3
        start = (2 - i if reverse else i) * w
        lhs = x3_ref[start : start + n, (first - 3 * i) * c : (last - 3 * i) * c]
        across = 1 if reverse else 0
        term = lax.dot_general(
            lhs, weights.taps(first, last), (((1,), (across,)), ((), ())), preferred_element_type=F32
        )
        if first == 0:
            out_ref[...] = term
        else:
            out_ref[...] += term


def put_stats(sz, first, second, out_ref):
    tile = join_rows(jnp.sum(first, axis=0, keepdims=True), jnp.sum(second, axis=0, keepdims=True))
    out_ref[...] = jnp.broadcast_to(tile[None], out_ref.shape)


def silu_parts(half):
    t = jnp.tanh(half)
    product = half * t
    return half + product, (0.5 + 0.5 * t) * (1.0 + (half - product))


class Stats:
    def __init__(self, sz):
        self.first = jnp.zeros((8, sz.channels), F32)
        self.second = jnp.zeros((8, sz.channels), F32)

    def add(self, first, second):
        self.first = self.first + fold(first)
        self.second = self.second + fold(second)


def add_conv_rows(sz, masks, stats, conv_ref, skip, first, last):
    for row in range(max(first, skip), min(last, skip + sz.rows)):
        value = conv_ref[line(sz, row), :]
        masked = value * tiled(sz, masks.valid(row - skip))
        stats.add(masked, masked * value)


def band_lanes(sz, n):
    return pl.ds(pl.multiple_of((lax.axis_index("rows") ^ n) * sz.quarter, sz.quarter), sz.quarter)


def send_shares(sz, copies, source_ref, targets, first):
    lines = source_ref.shape[0]
    return [
        copies.start(source_ref.at[:, band_lanes(sz, n)], target.at[pl.ds(first, lines)])
        for n, target in enumerate(targets)
    ]


def kernel_spans(sz, given_ref, *rest):
    shares, sems = rest[: sz.bands], rest[sz.bands]
    copies = Copies(sems)
    span = sz.rows // 2 * (sz.width // 2)
    wait(*[
        copies.start(line_share(given_ref, (lax.axis_index("rows") ^ n) * span, span, share.shape[0]), share)
        for n, share in enumerate(shares)
    ])


def kernel_edges(sz, x_hbm, index_hbm, low_ref, high_ref, x_ref, index_ref, sems):
    copies = Copies(sems)
    edge = HALO * sz.width
    few = sz.width
    lines = index_hbm.shape[0]
    first = copies.start(index_hbm.at[pl.ds(lines - few, few)], index_ref.at[0])
    second = copies.start(index_hbm.at[pl.ds(0, few)], index_ref.at[1])
    rest = [
        copies.start(x_hbm.at[pl.ds(sz.pixels - edge, edge)], low_ref.at[pl.ds(0, edge)]),
        copies.start(x_hbm.at[pl.ds(0, edge)], high_ref.at[pl.ds(0, edge)]),
        copies.start(x_hbm, x_ref),
    ]
    wait(first, second)
    low_ref[edge : edge + few, :] = index_ref[0].astype(BF16)
    high_ref[edge : edge + few, :] = index_ref[1].astype(BF16)
    wait(*rest)


def kernel_places(sz, kind_ref, domain_ref, limits_ref, member_ref, _):
    m, r = lax.axis_index("maps"), lax.axis_index("rows")
    start = r * sz.rows

    def rows_of(k):
        return jnp.where(kind_ref[k] == 1, sz.height, sz.short_height)

    def cols_of(k):
        return jnp.where(kind_ref[k] == 1, sz.short_width, sz.width)

    own = domain_ref[m]
    area = jnp.int32(0)
    for k in range(sz.maps):
        area = area + jnp.where(domain_ref[k] == own, rows_of(k) * cols_of(k), 0)
    tile = member_ref.shape[1:]
    weight = 1.0 / jnp.full(tile, area.astype(F32))
    for k in range(sz.maps):
        value = jnp.where(domain_ref[k] == own, weight, 0.0)
        for b in range(sz.bands):
            member_ref[k * sz.bands + b] = value
    line = lax.broadcasted_iota(jnp.int32, limits_ref.shape, 0)
    limits_ref[...] = jnp.where(
        line == 0, -start, jnp.where(line == 1, rows_of(m) - start, jnp.where(line == 2, cols_of(m), rows_of(m)))
    )


def kernel_first(sz, limits_ref, up_ref, x_ref, down_ref, head_ref, weights_hbm, stats_ref, conv_ref, act_hbm, x3_ref,
                 buffer_ref, sems):
    copies = Copies(sems)
    weights = Weights(copies, head_ref, weights_hbm, buffer_ref, 0)
    masks = Masks(sz, limits_ref)
    stats = Stats(sz)

    def prepare(row):
        if row < HALO:
            value = up_ref[line(sz, row), :]
        elif row < HALO + sz.rows:
            value = x_ref[line(sz, row - HALO), :]
        else:
            value = down_ref[line(sz, row - HALO - sz.rows), :]
        put_shifted(sz, masks, x3_ref, row, value.astype(F32))

    def work(first, last):
        conv_rows(sz, x3_ref, weights, conv_ref, last)
        add_conv_rows(sz, masks, stats, conv_ref, HALO - 1, first, last)

    for row in range(sz.rows + 2 * HALO):
        prepare(row)
    work(0, sz.rows + 2 * HALO - 2)
    out = copies.start(x_ref, act_hbm)
    put_stats(sz, stats.first, stats.second, stats_ref)
    wait(out)


def norm_of(sz, gathered_ref, member_ref):
    mean, squares = split_rows(own_sums(gathered_ref, member_ref), sz.channels)
    return mean, lax.rsqrt(squares - mean * mean + norm_epsilon)


def kernel_forward(sz, layer, limits_ref, member_ref, gathered_ref, before_ref, norm_ref, head_ref, weights_hbm, *rest):
    stats_ref, conv_ref, moments_ref, act_hbm, saved_hbm, x3_ref, buffer_ref, sems = rest
    copies = Copies(sems)
    weights = Weights(copies, head_ref, weights_hbm, buffer_ref, layer)
    halo = HALO - layer
    rows = sz.rows + 2 * halo
    skip = (halo - layer) * sz.width
    outs = []
    mean, inverse = norm_of(sz, gathered_ref, member_ref)
    moments_ref[...] = join_rows(mean, inverse)
    scale = 0.5 * norm_ref[layer - 1, 0:1, :] * inverse
    offset = 0.5 * norm_ref[layer - 1, 1:2, :] - mean * scale
    masks = Masks(sz, limits_ref)
    stats = Stats(sz)
    c = sz.channels

    def prepare(row):
        value = before_ref[line(sz, row), :]
        act, _ = silu_parts(value * scale + offset)
        put_shifted(sz, masks, x3_ref, row, act * tiled(sz, masks.valid(row - halo)))
        if row == halo + sz.rows - 1:
            outs.append(copies.start(x3_ref.at[pl.ds(halo * sz.width, sz.pixels), pl.ds(c, c)], act_hbm))

    def work(first, last):
        conv_rows(sz, x3_ref, weights, conv_ref, last)
        outs.append(copies.start(before_ref.at[pl.ds(skip, saved_hbm.shape[0])], saved_hbm))
        add_conv_rows(sz, masks, stats, conv_ref, halo - 1, first, last)

    for row in range(rows):
        prepare(row)
    work(0, rows - 2)
    put_stats(sz, stats.first, stats.second, stats_ref)
    wait(*outs)


def kernel_pool(sz, limits_ref, member_ref, gathered_ref, before_ref, norm_ref, index_hbm, up_hbm, down_hbm, *rest):
    cotangents, rest = rest[: sz.bands], rest[sz.bands :]
    (stats_ref, grad_ref, normed_ref, moments_ref), rest = rest[:4], rest[4:]
    shares, rest = rest[: sz.bands], rest[sz.bands :]
    (index_ref, up_ref, down_ref, cotangent_ref, spread_ref, act_ref, pooled_ref, grad16_ref, normed16_ref, sems) = rest
    c, w = sz.channels, sz.width
    half = w // 2
    windows = sz.rows // 2
    edge = HALO * w
    copies = Copies(sems)
    inputs = [
        copies.start(index_hbm, index_ref),
        copies.start(up_hbm.at[pl.ds(edge, w)], up_ref),
        copies.start(down_hbm.at[pl.ds(edge, w)], down_ref),
    ]
    inputs += [
        copies.start(
            ref, cotangent_ref.at[:, band_lanes(sz, n)]
        )
        for n, ref in enumerate(cotangents)
    ]
    mean, inverse = norm_of(sz, gathered_ref, member_ref)
    moments_ref[...] = join_rows(mean, inverse)
    gain = 0.5 * norm_ref[2, 0:1, :]
    shift = 0.5 * norm_ref[2, 1:2, :]
    halo = HALO - 3
    rows = sz.rows + 2 * halo
    lines = sz.pixels // 4
    groups = c // 128
    masks = Masks(sz, limits_ref)
    for row in range(rows):
        normed = (before_ref[line(sz, row), :] - mean) * inverse
        normed_ref[line(sz, row), :] = normed.astype(BF16)
        act, slope = silu_parts(normed * gain + shift)
        valid = tiled(sz, masks.valid(row - halo))
        grad_ref[line(sz, row), :] = slope * valid
        if halo <= row < halo + sz.rows:
            normed16_ref[line(sz, row - halo), :] = normed.astype(BF16)
            act = act * valid
            for g in range(groups):
                act_ref[g, line(sz, row - halo), :] = act[:, g * 128 : (g + 1) * 128]
    outs = send_shares(sz, copies, normed16_ref, shares, lines + sz.pixels)
    wait(*inputs)
    for p in range(windows):
        index = index_ref[p * half : (p + 1) * half, :]
        result = jnp.zeros(index.shape, F32)
        for corner in range(4):
            start = (2 * p + corner // 2) * w + corner % 2
            taken = jnp.concatenate(
                [act_ref[g, pl.ds(start, half, stride=2), :] for g in range(groups)], axis=1
            )
            result = jnp.where(index == corner, taken, result)
        pooled_ref[p * half : (p + 1) * half, :] = result.astype(BF16)
    outs += send_shares(sz, copies, pooled_ref, shares, 0)
    for p in range(windows + 4):
        if p < 2:
            index = up_ref[p * half : (p + 1) * half, :].astype(jnp.int32)
        elif p < windows + 2:
            index = index_ref[(p - 2) * half : (p - 1) * half, :]
        else:
            first = (p - windows - 2) * half
            index = down_ref[first : first + half, :].astype(jnp.int32)
        given = cotangent_ref[p * half : (p + 1) * half, :].astype(F32)
        for corner in range(4):
            start = (2 * p + corner // 2) * w + corner % 2
            placed = jnp.where(index == corner, given, 0.0)
            for g in range(groups):
                spread_ref[g, pl.ds(start, half, stride=2), :] = placed[:, g * 128 : (g + 1) * 128]
    stats = Stats(sz)
    for row in range(rows):
        upstream = jnp.concatenate([spread_ref[g, line(sz, row + 1), :] for g in range(groups)], axis=1)
        grad = upstream * grad_ref[line(sz, row), :]
        grad_ref[line(sz, row), :] = grad
        if halo <= row < halo + sz.rows:
            grad16_ref[line(sz, row - halo), :] = grad.astype(BF16)
            stats.add(grad, grad * normed_ref[line(sz, row), :].astype(F32))
    outs += send_shares(sz, copies, grad16_ref, shares, lines)
    put_stats(sz, stats.first, stats.second, stats_ref)
    wait(*outs)


class ConvGrad:
    def __init__(self, sz, layer, masks, member_ref, moments_ref, gathered_ref, norm_ref):
        self.sz, self.masks = sz, masks
        _, inverse = split_rows(moments_ref[...], sz.channels)
        one, two = split_rows(own_sums(gathered_ref, member_ref), sz.channels)
        self.scale = norm_ref[layer, 0:1, :] * inverse
        self.one, self.two = one, two

    def row(self, row, grad, normed):
        value = self.scale * (grad - self.one - normed * self.two)
        return value * tiled(self.sz, self.masks.valid(row))


def kernel_backward(sz, layer, limits_ref, member_ref, gathered_ref, grad_ref, normed_ref, moments_ref, norm_ref,
                    head_ref, weights_hbm, saved_hbm, moments_below_ref, stats_ref, below_ref, normed_below_ref, totals_ref,
                    *rest):
    shares, (saved_ref, x3_ref, buffer_ref, grad16_ref, normed16_ref, sems) = rest[: sz.bands], rest[sz.bands :]
    copies = Copies(sems)
    weights = Weights(copies, head_ref, weights_hbm, buffer_ref, layer)
    saved = copies.start(saved_hbm, saved_ref)
    halo = layer + 1
    rows = sz.rows + 2 * halo
    masks = Masks(sz, limits_ref)
    conv_grad = ConvGrad(sz, layer, masks, member_ref, moments_ref, gathered_ref, norm_ref)
    below = layer - 1
    mean, inverse = split_rows(moments_below_ref[...], sz.channels)
    gain = 0.5 * norm_ref[below, 0:1, :]
    shift = 0.5 * norm_ref[below, 1:2, :]
    stats = Stats(sz)
    outs = []

    def prepare(row):
        value = conv_grad.row(row - halo, grad_ref[line(sz, row), :], normed_ref[line(sz, row), :].astype(F32))
        put_shifted(sz, masks, x3_ref, row, value, True)

    def work(first, last):
        conv_rows(sz, x3_ref, weights, below_ref, last, True)
        if first == 0:
            wait(saved)
        for row in range(first, last):
            normed = (saved_ref[line(sz, row), :] - mean) * inverse
            normed_below_ref[line(sz, row), :] = normed.astype(BF16)
            _, slope = silu_parts(normed * gain + shift)
            own = row - (halo - 1)
            grad = below_ref[line(sz, row), :] * slope * tiled(sz, masks.valid(own))
            below_ref[line(sz, row), :] = grad
            if 0 <= own < sz.rows:
                grad16_ref[line(sz, own), :] = grad.astype(BF16)
                normed16_ref[line(sz, own), :] = normed.astype(BF16)
                stats.add(grad, grad * normed)

    for row in range(rows):
        prepare(row)
    work(0, rows - 2)
    outs += send_shares(sz, copies, grad16_ref, shares, 0)
    outs += send_shares(sz, copies, normed16_ref, shares, sz.pixels)
    put_stats(sz, stats.first, stats.second, stats_ref)
    totals_ref[...] = all_sums(gathered_ref)
    wait(*outs)


def kernel_last(sz, limits_ref, member_ref, gathered_ref, grad_ref, normed_ref, moments_ref, norm_ref, head_ref,
                weights_hbm, *rest):
    parts, (out_hbm, totals_ref, pooled_hbm, x3_ref, buffer_ref, acc_ref, out_ref, sems) = (
        rest[: sz.bands], rest[sz.bands :]
    )
    copies = Copies(sems)
    weights = Weights(copies, head_ref, weights_hbm, buffer_ref, 0)
    lines = sz.pixels // 4
    outs = []
    for n, ref in enumerate(parts):
        target = line_share(pooled_hbm, (lax.axis_index("rows") ^ n) * lines, lines, lines)
        outs.append(copies.start(ref.at[pl.ds(0, lines)], target))
    totals_ref[...] = all_sums(gathered_ref)
    masks = Masks(sz, limits_ref)
    conv_grad = ConvGrad(sz, 0, masks, member_ref, moments_ref, gathered_ref, norm_ref)

    def prepare(row):
        value = conv_grad.row(row - 1, grad_ref[line(sz, row), :], normed_ref[line(sz, row), :].astype(F32))
        put_shifted(sz, masks, x3_ref, row, value, True)

    def work(first, last):
        conv_rows(sz, x3_ref, weights, acc_ref, last, True)
        pixels = slice(first * sz.width, last * sz.width)
        out_ref[pixels, :] = acc_ref[pixels, :].astype(BF16)

    for row in range(sz.rows + 2):
        prepare(row)
    work(0, sz.rows)
    outs.append(copies.start(out_ref, out_hbm))
    wait(*outs)


def kernel_weight_grad(sz, layer, first, limits_ref, member_ref, gathered_ref, moments_ref, norm_ref, *rest):
    w, q, c, bands = sz.width, sz.quarter, sz.channels, sz.bands
    pixels = sz.height * w
    given, rest = rest[:bands], rest[bands:]
    acts, rest = rest[:bands], rest[bands:]
    if layer == 0:
        out_ref, grad_ref, normed_ref, act_ref, x9_ref, sems = rest
    else:
        (keep_hbm, send_hbm, grad_ref, normed_ref, act_ref, x9_ref, keep_ref, send_ref, term_ref,
         sems) = rest
    copies = Copies(sems)
    inputs = []
    for n in range(bands):
        start = (lax.axis_index("rows") ^ n) * sz.pixels
        for source, target, top in ((given[n], grad_ref, first[0]), (given[n], normed_ref, first[1])):
            inputs.append(
                copies.start(source.at[pl.ds(top, sz.pixels)], line_share(target, start, sz.pixels, sz.pixels))
            )
    act_loads = [
        copies.start(
            acts[n], line_share(act_ref, (lax.axis_index("rows") ^ n) * sz.pixels, sz.pixels, sz.pixels)
        )
        for n in range(bands)
    ]
    band = lax.axis_index("rows")
    own = lax.axis_index("maps")
    tile = own_sums(gathered_ref, member_ref)
    one, two, inverse, gain = (jnp.zeros((1, q), F32) for _ in range(4))
    for b in range(bands):
        here = band == b
        one = jnp.where(here, tile[b : b + 1, :], one)
        two = jnp.where(here, tile[b + 4 : b + 5, :], two)
        inverse = jnp.where(here, moments_ref[b + 4 : b + 5, :], inverse)
        gain = jnp.where(here, norm_ref[layer, 0:1, b * q : (b + 1) * q], gain)
    wait(*inputs)
    masks = Masks(sz, limits_ref)
    blank = jnp.zeros((w, q), BF16)
    for row in range(sz.height):
        value = grad_ref[line(sz, row), :].astype(F32) - one - normed_ref[line(sz, row), :].astype(F32) * two
        value = (gain * inverse) * value * masks.valid_of_map(row)
        for j, piece in enumerate((shifted_left(sz, masks, value), value, shifted_right(sz, masks, value))):
            piece = piece.astype(BF16)
            for i in range(3):
                if 0 <= row + i - 1 < sz.height:
                    x9_ref[line(sz, row + i - 1), (3 * i + j) * q : (3 * i + j + 1) * q] = piece
    for j in range(3):
        x9_ref[line(sz, sz.height - 1), j * q : (j + 1) * q] = blank
        x9_ref[line(sz, 0), (6 + j) * q : (7 + j) * q] = blank
    share = c // sz.maps
    wait(*act_loads)
    term = lax.dot_general(
        act_ref[...], x9_ref[...], (((0,), (0,)), ((), ())), preferred_element_type=F32
    )
    if layer == 0:
        for tap in range(9):
            part = term[:, tap * q : (tap + 1) * q].astype(BF16)
            for m in range(sz.maps):
                out_ref[m, tap * share : (tap + 1) * share, :] = part[m * share : (m + 1) * share, :]
        return
    term_ref[...] = term
    for position, relative in enumerate(halving_order(sz.maps)):
        lines = pl.ds(pl.multiple_of((own ^ relative) * share, share), share)
        for tap in range(9):
            place = slice(tap * share, (tap + 1) * share)
            part = term_ref[lines, tap * q : (tap + 1) * q]
            if position < sz.maps // 2:
                keep_ref[position, place, :] = part
            else:
                send_ref[position - sz.maps // 2, place, :] = part.astype(BF16)
    wait(copies.start(keep_ref, keep_hbm), copies.start(send_ref, send_hbm))


def halving_order(maps):
    bits = maps.bit_length() - 1
    return [sum(((place >> (bits - 1 - k)) & 1) << k for k in range(bits)) for place in range(maps)]


def kernel_halve(keep_hbm, received_hbm, next_keep_hbm, next_send_hbm, keep_ref, received_ref, send_ref, sems):
    half = next_keep_hbm.shape[0]
    copies = Copies(sems)
    loads = [
        [
            copies.start(source.at[part], target.at[part])
            for source, target in ((keep_hbm, keep_ref), (received_hbm, received_ref))
        ]
        for part in (pl.ds(half, half), pl.ds(0, half))
    ]
    wait(*loads[0])
    send_ref[...] = (keep_ref[half:] + received_ref[half:].astype(F32)).astype(BF16)
    first = copies.start(send_ref, next_send_hbm)
    wait(*loads[1])
    keep_ref[:half] += received_ref[:half].astype(F32)
    wait(first, copies.start(keep_ref.at[pl.ds(0, half)], next_keep_hbm))


def kernel_squares(sz, received_ref, keep1_hbm, last1_hbm, keep2_hbm, last2_hbm, totals2_ref, totals1_ref,
                   totals0_ref, squares_ref, shard_ref, norm_grad_ref, keep_ref, last_ref, sems):
    copies = Copies(sems)
    loads = [
        copies.start(source.at[0], target.at[k])
        for k, pair in enumerate(((keep1_hbm, last1_hbm), (keep2_hbm, last2_hbm)))
        for source, target in zip(pair, (keep_ref, last_ref))
    ]
    for layer, ref in enumerate((totals0_ref, totals1_ref, totals2_ref)):
        shift_row, gain_row = split_rows(ref[...], sz.channels)
        norm_grad_ref[layer, 0:1, :] = gain_row
        norm_grad_ref[layer, 1:2, :] = shift_row
    value = received_ref[0].astype(F32)
    for m in range(1, sz.maps):
        value = value + received_ref[m].astype(F32)
    shard_ref[0] = value
    total = jnp.sum(value * value, axis=0, keepdims=True)
    wait(*loads)
    for layer in (1, 2):
        value = keep_ref[layer - 1] + last_ref[layer - 1].astype(F32)
        shard_ref[layer] = value
        total = total + jnp.sum(value * value, axis=0, keepdims=True)
    squares_ref[...] = jnp.broadcast_to(total[None], squares_ref.shape)


def kernel_adam(sz, rate, every_ref, step_ref, shard_ref, master_hbm, first_hbm, second_hbm, norm_grad_ref, norm_ref,
                norm_first_ref, norm_second_ref, total_hbm, first_out_hbm, second_out_hbm, master_out_hbm,
                norm_first_hbm, norm_second_hbm, norm_hbm,
                total_ref, master_ref, first_ref, second_ref, small_ref, sems):
    copies = Copies(sems)
    loads = [
        [
            copies.start(source.at[layer], target.at[layer])
            for source, target in ((master_hbm, master_ref), (first_hbm, first_ref), (second_hbm, second_ref))
        ]
        for layer in range(3)
    ]
    norm_grad = norm_grad_ref[...]
    square = jnp.sum(jnp.sum(every_ref[...], axis=0)) + jnp.sum(norm_grad * norm_grad)
    total = jnp.sqrt(jnp.full((1, 128), square, F32))
    total_ref[...] = total
    outs = [copies.start(total_ref, total_hbm)]
    scale = jnp.minimum(1.0, clip_limit / total)
    count = jnp.full((1, 128), step_ref[0].astype(F32), F32)
    first_fix = 1.0 - jnp.exp(count * math.log(first_decay))
    second_fix = 1.0 - jnp.exp(count * math.log(second_decay))
    for layer in range(3):
        wait(*loads[layer])
        first_ref[layer], second_ref[layer], master_ref[layer] = adam(
            master_ref[layer], shard_ref[layer], first_ref[layer], second_ref[layer], rate, weight_decay,
            scale, first_fix, second_fix,
        )
        for source, target in (
            (first_ref, first_out_hbm), (second_ref, second_out_hbm), (master_ref, master_out_hbm)
        ):
            outs.append(copies.start(source.at[layer], target.at[layer]))
    wide = [jnp.concatenate([v] * (sz.channels // 128), axis=1) for v in (scale, first_fix, second_fix)]
    for layer in range(3):
        small_ref[0, layer], small_ref[1, layer], small_ref[2, layer] = adam(
            norm_ref[layer], norm_grad[layer], norm_first_ref[layer], norm_second_ref[layer], norm_rate, 0.0, *wide
        )
    for k, target in enumerate((norm_first_hbm, norm_second_hbm, norm_hbm)):
        outs.append(copies.start(small_ref.at[k], target))
    wait(*outs)


def adam(param, grad, first, second, rate, decay, scale, first_fix, second_fix):
    clipped = scale * grad
    first_new = first_decay * first + (1.0 - first_decay) * clipped
    second_new = second_decay * second + (1.0 - second_decay) * clipped * clipped
    update = first_new / first_fix / (jnp.sqrt(second_new / second_fix) + adam_epsilon)
    return first_new, second_new, param - rate * (update + decay * param)


def call(kernel, name, outs, ins, scratch=(), flops=0, moved=0, hbm_ins=(), hbm_outs=(), smem_ins=(), sems=1):
    spaces_in = [
        pltpu.SMEM if k in smem_ins else pltpu.HBM if k in hbm_ins else pltpu.VMEM for k in range(len(ins))
    ]
    spaces_out = [pltpu.HBM if k in hbm_outs else pltpu.VMEM for k in range(len(outs))]
    return pl.pallas_call(
        kernel,
        out_shape=tuple(space(out.shape, out.dtype) for space, out in zip(spaces_out, outs)),
        in_specs=[spec(space) for space in spaces_in],
        out_specs=tuple(spec(space) for space in spaces_out),
        scratch_shapes=list(scratch) + [pltpu.SemaphoreType.DMA((sems,))],
        compiler_params=params(SPACE),
        cost_estimate=pl.CostEstimate(flops=flops, bytes_accessed=moved, transcendentals=0),
        name=name,
    )(*[v if k in smem_ins else pltpu.with_memory_space_constraint(v, spaces_in[k]) for k, v in enumerate(ins)])


def local(sz, block_input, conv_weights, norm_params, pool_index, task_mask, map_kind, map_domain, out_grad, step,
          conv_master, conv_moment1, conv_moment2, norm_moment1, norm_moment2):
    w, c, q = sz.width, sz.channels, sz.quarter
    half = w // 2
    n_maps, bands = sz.maps, sz.bands
    forward = [(i, i + 1) for i in range(bands - 1)]
    backward = [(i + 1, i) for i in range(bands - 1)]
    x = block_input.reshape(sz.pixels, c)
    index = pool_index.reshape(sz.pixels // 4, c)
    norms, norm_first, norm_second = (v.transpose(1, 0, 2) for v in (norm_params, norm_moment1, norm_moment2))
    edge = HALO * w
    lines = sz.pixels // 4

    def shape(dims, dtype):
        return jax.ShapeDtypeStruct(dims, dtype)

    def pixel_shape(rows, dtype):
        return shape((rows * w, c), dtype)

    def pixel_space(rows, dtype, times=1):
        return pltpu.VMEM((rows * w, times * c), dtype)

    def share_shapes(count):
        return [shape((count, q), BF16)] * bands

    stats_shape = shape((sz.devices, 8, c // 4), F32)
    tile_shape = shape((8, c // 4), F32)
    weight_space = pltpu.VMEM((9 - HEAD, c, c), BF16)


    def conv_flops(rows):
        return rows * w * 9 * c * c * 2

    def spread(stats):
        return lax.all_to_all(stats, AXES, 0, 0, tiled=True)

    def trade(shares):
        return [shares[0]] + [
            lax.ppermute(shares[n], "rows", [(i, i ^ n) for i in range(bands)]) for n in range(1, bands)
        ]

    def swap(act, n):
        return lax.ppermute(act, "rows", [(i, i ^ n) for i in range(bands)])

    tie = lax.optimization_barrier

    low, high, near = call(
        functools.partial(kernel_edges, sz), "edges",
        [shape((edge + 2 * half, c), BF16)] * 2 + [pixel_shape(sz.rows, BF16)], [x, index],
        [pltpu.VMEM((2, 2 * half, c), jnp.int32)], hbm_ins=(0, 1), sems=5,
    )
    up = lax.ppermute(low, "rows", forward)
    down = lax.ppermute(high, "rows", backward)

    limits, member = call(
        functools.partial(kernel_places, sz), "places", [shape((8, 128), jnp.int32), stats_shape],
        [map_kind, map_domain], smem_ins=(0, 1),
    )
    labelled = (out_grad * task_mask[..., None].astype(BF16)).reshape(sz.height // 2 * half, q)
    labelled = jnp.pad(labelled, ((2 * half, 2 * half), (0, 0)))
    consts = [limits, member]

    rows = sz.rows + 2 * HALO
    stats, conv, kept = call(
        functools.partial(kernel_first, sz), "first",
        [stats_shape, pixel_shape(rows - 2, F32), pixel_shape(sz.rows, BF16)], [limits, up, near, down, conv_weights[0, :HEAD], conv_weights],
        [pixel_space(rows, BF16, 3), weight_space], conv_flops(rows - 2), hbm_ins=(5,), hbm_outs=(2,), sems=4,
    )
    def head(layer, weights):
        return weights[layer, :HEAD]

    cot_lines = (sz.rows // 2 + 4) * half
    cots = call(functools.partial(kernel_spans, sz), "spans", share_shapes(cot_lines), [labelled], hbm_outs=range(bands), sems=bands)
    stats, weights, *cots = tie((stats, conv_weights, *cots))
    gathered = spread(stats)
    cots = trade(cots)
    acts = [[kept, swap(kept, 1), swap(kept, 2)]]
    moments = []
    saves = []
    for layer in (1, 2):
        rows = sz.rows + 2 * (HALO - layer)
        outs = [
            stats_shape, pixel_shape(rows - 2, F32), tile_shape, pixel_shape(sz.rows, BF16),
            pixel_shape(sz.rows + 2 * layer, F32),
        ]
        scratch = [pixel_space(rows, BF16, 3), weight_space]
        stats, conv, moment, act, saved = call(
            functools.partial(kernel_forward, sz, layer), "forward", outs,
            consts + [gathered, conv, norms, head(layer, weights), conv_weights], scratch,
            conv_flops(rows - 2), hbm_ins=(6,), hbm_outs=(3, 4), sems=5,
        )
        moments.append(moment)
        saves.append(saved)
        if layer == 1:
            stats, weights, *rest = tie((stats, conv_weights, *cots, *acts[0]))
            cots, acts[0] = rest[:bands], rest[bands:]
            gathered = spread(stats)
        else:
            stats, *acts[1] = tie((stats, *acts[1]))
            gathered = spread(stats)
        acts[layer - 1].append(swap(acts[layer - 1][2], 1))
        acts.append([act, swap(act, 1), swap(act, 2)])

    rows = sz.rows + 2 * (HALO - 3)
    stats, grad, normed, moment, *shares = call(
        functools.partial(kernel_pool, sz), "pool",
        [stats_shape, pixel_shape(rows, F32), pixel_shape(rows, BF16), tile_shape]
        + share_shapes(lines + 2 * sz.pixels),
        consts + [gathered, conv, norms, index, up, down] + cots,
        [
            pltpu.VMEM((lines, c), jnp.int32), pltpu.VMEM((2 * half, c), BF16), pltpu.VMEM((2 * half, c), BF16),
            pltpu.VMEM((cot_lines, c), BF16),
            pltpu.VMEM((c // 128, (rows + 2) * w, 128), F32), pltpu.VMEM((c // 128, sz.pixels, 128), F32),
            pltpu.VMEM((lines, c), BF16), pixel_space(sz.rows, BF16), pixel_space(sz.rows, BF16),
        ],
        conv_flops(4), hbm_ins=range(5, 8 + bands), hbm_outs=range(4, 4 + bands), sems=3 + 4 * bands,
    )
    moments.append(moment)
    stats, weights, acts[0][3], *acts[2] = tie((stats, conv_weights, acts[0][3], *acts[2]))
    gathered = spread(stats)
    exchanged = trade(shares)
    acts[2].append(swap(acts[2][2], 1))
    pooled_parts = exchanged

    totals = [None, None, None]
    share = 9 * (c // n_maps)
    steps = n_maps.bit_length() - 1

    def part_shape(parts, dtype):
        return shape((parts, share, q), dtype)

    def part_space(parts, dtype):
        return pltpu.VMEM((parts, share, q), dtype)

    def weight_grad(layer, gathered, given, first):
        scratch = [
            pltpu.VMEM((sz.height * w, q), BF16),
            pltpu.VMEM((sz.height * w, q), BF16),
            pltpu.VMEM((sz.height * w, c), BF16),
            pltpu.VMEM((sz.height * w, 9 * q), BF16),
        ]
        if layer == 0:
            outs = [part_shape(n_maps, BF16)]
        else:
            outs = [part_shape(n_maps // 2, dtype) for dtype in (F32, BF16)]
            scratch += [part_space(n_maps // 2, dtype) for dtype in (F32, BF16)]
            scratch.append(pltpu.VMEM((c, 9 * q), F32))
        return call(
            functools.partial(kernel_weight_grad, sz, layer, first), "weight_grad", outs,
            consts + [gathered, moments[layer], norms] + given + acts[layer], scratch, conv_flops(sz.rows),
            hbm_ins=range(5, 5 + 2 * bands), hbm_outs=() if layer == 0 else (0, 1), sems=3 * bands + 2,
        )

    def step_of(send, k):
        return lax.ppermute(send, "maps", [(m, m ^ (1 << k)) for m in range(n_maps)])

    def halved(keep, received):
        size = keep.shape[0] // 2
        return call(
            kernel_halve, "halve", [part_shape(size, dtype) for dtype in (F32, BF16)], [keep, received],
            [part_space(2 * size, F32), part_space(2 * size, BF16), part_space(size, BF16)],
            hbm_ins=(0, 1), hbm_outs=(0, 1), sems=6,
        )

    def halve(keep, received, k):
        while k < steps - 1:
            k += 1
            keep, send = halved(keep, received)
            received = step_of(send, k)
        return keep, received

    shards = [None, None, None]
    for layer in (2, 1):
        halo = layer + 1
        rows = sz.rows + 2 * halo
        received, gathered_here = exchanged, gathered
        stats, grad, normed, totals[layer], *shares = call(
            functools.partial(kernel_backward, sz, layer), "backward",
            [stats_shape, pixel_shape(rows - 2, F32), pixel_shape(rows - 2, BF16), tile_shape]
            + share_shapes(2 * sz.pixels),
            consts + [
                gathered, grad, normed, moments[layer], norms, head(layer, weights), conv_weights, saves[layer - 1],
                moments[layer - 1],
            ],
            [
                pixel_space(rows - 2, F32), pixel_space(rows, BF16, 3), weight_space, pixel_space(sz.rows, BF16),
                pixel_space(sz.rows, BF16),
            ],
            conv_flops(rows - 2), hbm_ins=(8, 9), hbm_outs=range(4, 4 + bands), sems=4 + 2 * bands,
        )
        if layer == 2:
            stats, weights, acts[1][3], acts[2][3], *received = tie(
                (stats, conv_weights, acts[1][3], acts[2][3], *received)
            )
            gathered = spread(stats)
            exchanged = trade(shares)
            keep2, send2 = weight_grad(2, gathered_here, received, (lines, lines + sz.pixels))
            gathered, send2 = tie((gathered, send2))
            arrived2 = step_of(send2, 0)
        else:
            stats, weights, *received = tie((stats, conv_weights, *received))
            gathered = spread(stats)
            exchanged = trade(shares)
            keep1, send1 = weight_grad(1, gathered_here, received, (0, sz.pixels))
            gathered, send1, arrived2 = tie((gathered, send1, arrived2))
            arrived1 = step_of(send1, 0)
            keep2, send2 = halved(keep2, arrived2)

    arrived2 = step_of(send2, 1)
    (partial,) = weight_grad(0, gathered, exchanged, (0, sz.pixels))
    partial, arrived1, arrived2 = tie((partial, arrived1, arrived2))
    received = lax.all_to_all(partial, "maps", 0, 0, tiled=True)
    shards[2] = halve(keep2, arrived2, 1)
    shards[1] = halve(keep1, arrived1, 0)
    input_grad, totals[0], pooled = call(
        functools.partial(kernel_last, sz), "last",
        [pixel_shape(sz.rows, BF16), tile_shape, shape((sz.height // 2 * half, q), BF16)],
        consts + [gathered, grad, normed, moments[0], norms, head(0, weights), conv_weights] + pooled_parts,
        [pixel_space(sz.rows + 2, BF16, 3), weight_space, pixel_space(sz.rows, F32), pixel_space(sz.rows, BF16)],
        conv_flops(sz.rows), hbm_ins=range(8, 9 + bands), hbm_outs=(0, 2), sems=4 + bands,
    )

    norm_shape = shape((3, 2, c), F32)
    squares, shard, norm_grad = call(
        functools.partial(kernel_squares, sz), "squares",
        [shape((sz.devices, 1, q), F32), part_shape(3, F32), norm_shape],
        [received, *shards[1], *shards[2], totals[2], totals[1], totals[0]],
        [part_space(2, F32), part_space(2, BF16)], hbm_ins=range(1, 5), sems=4,
    )
    every = lax.all_to_all(squares, AXES, 0, 0, tiled=True)
    rate = 2.0 / math.sqrt(9.0 * c)
    total, conv_first, conv_second, conv_new, norm_first, norm_second, norm_new = call(
        functools.partial(kernel_adam, sz, rate), "adam",
        [shape((1, 128), F32)] + [part_shape(3, F32)] * 3 + [norm_shape] * 3,
        [every, step, shard]
        + [v.reshape(3, share, q) for v in (conv_master, conv_moment1, conv_moment2)]
        + [norm_grad, norms, norm_first, norm_second],
        [pltpu.VMEM((1, 128), F32)] + [part_space(3, F32)] * 3 + [pltpu.VMEM((3, 3, 2, c), F32)],
        hbm_ins=(3, 4, 5), hbm_outs=range(7), smem_ins=(1,), sems=22,
    )
    return (
        pooled.reshape(1, sz.height // 2, half, q),
        input_grad.reshape(block_input.shape),
        total[0, :1],
        conv_first.reshape(conv_master.shape),
        conv_second.reshape(conv_master.shape),
        conv_new.reshape(conv_master.shape),
        norm_first.transpose(1, 0, 2),
        norm_second.transpose(1, 0, 2),
        norm_new.transpose(1, 0, 2),
    )


def solution(mesh):
    def run(*args):
        bands = mesh.shape["rows"]
        maps = mesh.shape["maps"]
        shape = args[0].shape
        sz = Sizes(maps, bands, shape[1] // bands, shape[2], shape[3])
        return jax.shard_map(
            functools.partial(local, sz),
            mesh=mesh,
            in_specs=(
                P("maps", "rows", None, None),
                P(),
                P(),
                P("maps", "rows", None, None),
                P("maps", None, None),
                P(),
                P(),
                P("maps", None, None, "rows"),
                P(),
                P(None, None, "maps", "rows"),
                P(None, None, "maps", "rows"),
                P(None, None, "maps", "rows"),
                P(),
                P(),
            ),
            out_specs=(
                P("maps", None, None, "rows"),
                P("maps", "rows", None, None),
                P(),
                P(None, None, "maps", "rows"),
                P(None, None, "maps", "rows"),
                P(None, None, "maps", "rows"),
                P(),
                P(),
                P(),
            ),
            check_vma=False,
        )(*args)

    return run
```

```python
import functools
import math

import jax
import jax.numpy as jnp
from jax import lax
from jax.experimental import pallas as pl
from jax.experimental.pallas import tpu as pltpu
from jax.sharding import PartitionSpec as P

DOMAINS = 4
norm_epsilon = 1e-05
clip_limit = 1.0
first_decay = 0.9
second_decay = 0.999
adam_epsilon = 1e-08
norm_rate = 0.5
weight_decay = 0.01

HALO = 6
SPACE = 28
AXES = ("maps", "rows")
F32 = jnp.float32
BF16 = jnp.bfloat16


class Sizes:
    def __init__(self, maps, bands, rows, width, channels):
        self.maps = maps
        self.bands = bands
        self.devices = maps * bands
        self.rows = rows
        self.width = width
        self.channels = channels
        self.height = rows * bands
        self.short_height = 2 * (self.height * 7 // 16)
        self.short_width = 2 * (width * 13 // 32)
        self.pixels = rows * width
        self.quarter = channels // bands


def spec(space):
    return pl.BlockSpec(memory_space=space)


def params(megabytes):
    return pltpu.CompilerParams(vmem_limit_bytes=megabytes << 20)


class Copies:
    def __init__(self, sems):
        self.sems = sems
        self.used = 0

    def start(self, source, target):
        copy = pltpu.make_async_copy(source, target, self.sems.at[self.used])
        self.used += 1
        copy.start()
        return copy


def wait(*copies):
    for copy in copies:
        copy.wait()


def line_share(ref, start, step, size):
    return ref.at[pl.ds(pl.multiple_of(start, step), size)]


def own_sums(gathered_ref, weights_ref):
    return jnp.sum(gathered_ref[...] * weights_ref[...], axis=0)


def all_sums(gathered_ref):
    return jnp.sum(gathered_ref[...], axis=0)


def split_rows(tile, channels):
    first = jnp.concatenate([tile[k : k + 1, :] for k in range(4)], axis=1)
    second = jnp.concatenate([tile[k : k + 1, :] for k in range(4, 8)], axis=1)
    return first, second


def join_rows(first, second):
    lanes = first.shape[1] // 4
    return jnp.concatenate(
        [row[:, k * lanes : (k + 1) * lanes] for row in (first, second) for k in range(4)], axis=0
    )


def tiled(sz, value):
    return jnp.concatenate([value] * (sz.channels // value.shape[1]), axis=1)


class Masks:
    def __init__(self, sz, limits_ref):
        self.col = lax.broadcasted_iota(jnp.int32, (sz.width, 128), 0)
        self.wide = jnp.where(self.col < limits_ref[2:3, :], 1.0, 0.0)
        self.inner_left = jnp.where(self.col > 0, 1.0, 0.0)
        self.inner_right = jnp.where(self.col < sz.width - 1, 1.0, 0.0)
        self.limits_ref = limits_ref

    def valid(self, row):
        inside = (self.limits_ref[0:1, :] <= row) & (self.limits_ref[1:2, :] > row)
        return self.wide * jnp.where(inside, 1.0, 0.0)

    def valid_of_map(self, row):
        return self.wide * jnp.where(self.limits_ref[3:4, :] > row, 1.0, 0.0)


def line(sz, row):
    return slice(row * sz.width, (row + 1) * sz.width)


def shifted_right(sz, masks, value):
    mask = masks.inner_left
    return pltpu.roll(value, 1, 0) * (mask if value.shape[1] == 128 else tiled(sz, mask))


def shifted_left(sz, masks, value):
    mask = masks.inner_right
    return pltpu.roll(value, sz.width - 1, 0) * (mask if value.shape[1] == 128 else tiled(sz, mask))


def put_shifted(sz, masks, x3_ref, row, value, reverse=False):
    before = shifted_right(sz, masks, value)
    after = shifted_left(sz, masks, value)
    if reverse:
        before, after = after, before
    c = sz.channels
    x3_ref[line(sz, row), 0:c] = before.astype(BF16)
    x3_ref[line(sz, row), c : 2 * c] = value.astype(BF16)
    x3_ref[line(sz, row), 2 * c : 3 * c] = after.astype(BF16)


def fold(value):
    total = value[0:8, :]
    for k in range(1, value.shape[0] // 8):
        total = total + value[8 * k : 8 * (k + 1), :]
    return total


HEAD = 1


class Weights:
    def __init__(self, copies, head_ref, weights_hbm, buffer_ref, layer):
        self.head_ref, self.buffer_ref = head_ref, buffer_ref
        self.loads = {
            first: copies.start(
                weights_hbm.at[layer, pl.ds(first, 3 - first % 3)],
                buffer_ref.at[pl.ds(first - HEAD, 3 - first % 3)],
            )
            for first in (HEAD, 3, 6)
        }

    def wait(self, tap):
        if tap in self.loads:
            wait(self.loads[tap])

    def taps(self, first, last):
        if first < HEAD:
            part = self.head_ref[first:last]
        else:
            part = self.buffer_ref[first - HEAD : last - HEAD]
        return part.reshape(-1, part.shape[-1])


def conv_rows(sz, x3_ref, weights, out_ref, rows, reverse=False):
    c, w = sz.channels, sz.width
    n = rows * w
    spans = [(0, HEAD), (HEAD, 3), (3, 6), (6, 9)]
    if reverse:
        spans = [(tap, tap + 1) for tap in range(9)]
    for first, last in spans:
        weights.wait(first)
        i = first // 3
        start = (2 - i if reverse else i) * w
        lhs = x3_ref[start : start + n, (first - 3 * i) * c : (last - 3 * i) * c]
        across = 1 if reverse else 0
        term = lax.dot_general(
            lhs, weights.taps(first, last), (((1,), (across,)), ((), ())), preferred_element_type=F32
        )
        if first == 0:
            out_ref[...] = term
        else:
            out_ref[...] += term


def put_stats(sz, first, second, out_ref):
    tile = join_rows(jnp.sum(first, axis=0, keepdims=True), jnp.sum(second, axis=0, keepdims=True))
    out_ref[...] = jnp.broadcast_to(tile[None], out_ref.shape)


def silu_parts(half):
    t = jnp.tanh(half)
    product = half * t
    return half + product, (0.5 + 0.5 * t) * (1.0 + (half - product))


class Stats:
    def __init__(self, sz):
        self.first = jnp.zeros((8, sz.channels), F32)
        self.second = jnp.zeros((8, sz.channels), F32)

    def add(self, first, second):
        self.first = self.first + fold(first)
        self.second = self.second + fold(second)


def add_conv_rows(sz, masks, stats, conv_ref, skip, first, last):
    for row in range(max(first, skip), min(last, skip + sz.rows)):
        value = conv_ref[line(sz, row), :]
        masked = value * tiled(sz, masks.valid(row - skip))
        stats.add(masked, masked * value)


def band_lanes(sz, n):
    return pl.ds(pl.multiple_of((lax.axis_index("rows") ^ n) * sz.quarter, sz.quarter), sz.quarter)


def send_shares(sz, copies, source_ref, targets, first):
    lines = source_ref.shape[0]
    return [
        copies.start(source_ref.at[:, band_lanes(sz, n)], target.at[pl.ds(first, lines)])
        for n, target in enumerate(targets)
    ]


def kernel_spans(sz, given_ref, *rest):
    shares, sems = rest[: sz.bands], rest[sz.bands]
    copies = Copies(sems)
    span = sz.rows // 2 * (sz.width // 2)
    wait(*[
        copies.start(line_share(given_ref, (lax.axis_index("rows") ^ n) * span, span, share.shape[0]), share)
        for n, share in enumerate(shares)
    ])


def kernel_edges(sz, x_hbm, index_hbm, near_ref, far_ref, x_ref, index_ref, sems):
    copies = Copies(sems)
    edge = HALO * sz.width
    few = sz.width
    odd = lax.axis_index("rows") % 2
    last = index_hbm.shape[0] - few
    loads = []
    rest = []
    for k, (first, target) in enumerate(((1 - odd, near_ref), (odd, far_ref))):
        loads.append(copies.start(line_share(index_hbm, first * last, few, few), index_ref.at[k]))
        rest.append(copies.start(line_share(x_hbm, first * (sz.pixels - edge), edge, edge), target.at[pl.ds(0, edge)]))
    rest.append(copies.start(x_hbm, x_ref))
    wait(*loads)
    near_ref[edge : edge + few, :] = index_ref[0].astype(BF16)
    far_ref[edge : edge + few, :] = index_ref[1].astype(BF16)
    wait(*rest)


def kernel_places(sz, kind_ref, domain_ref, limits_ref, member_ref, _):
    m, r = lax.axis_index("maps"), lax.axis_index("rows")
    start = r * sz.rows

    def rows_of(k):
        return jnp.where(kind_ref[k] == 1, sz.height, sz.short_height)

    def cols_of(k):
        return jnp.where(kind_ref[k] == 1, sz.short_width, sz.width)

    own = domain_ref[m]
    area = jnp.int32(0)
    for k in range(sz.maps):
        area = area + jnp.where(domain_ref[k] == own, rows_of(k) * cols_of(k), 0)
    tile = member_ref.shape[1:]
    weight = 1.0 / jnp.full(tile, area.astype(F32))
    for k in range(sz.maps):
        value = jnp.where(domain_ref[k] == own, weight, 0.0)
        for b in range(sz.bands):
            member_ref[k * sz.bands + b] = value
    line = lax.broadcasted_iota(jnp.int32, limits_ref.shape, 0)
    limits_ref[...] = jnp.where(
        line == 0, -start, jnp.where(line == 1, rows_of(m) - start, jnp.where(line == 2, cols_of(m), rows_of(m)))
    )


def kernel_first(sz, limits_ref, near_ref, x_ref, far_ref, head_ref, weights_hbm, stats_ref, conv_ref, act_hbm, x3_ref,
                 buffer_ref, sems):
    copies = Copies(sems)
    weights = Weights(copies, head_ref, weights_hbm, buffer_ref, 0)
    masks = Masks(sz, limits_ref)
    stats = Stats(sz)

    odd = lax.axis_index("rows") % 2 == 1

    def prepare(row):
        if row < HALO:
            value = jnp.where(odd, near_ref[line(sz, row), :], far_ref[line(sz, row), :])
        elif row < HALO + sz.rows:
            value = x_ref[line(sz, row - HALO), :]
        else:
            below = line(sz, row - HALO - sz.rows)
            value = jnp.where(odd, far_ref[below, :], near_ref[below, :])
        put_shifted(sz, masks, x3_ref, row, value.astype(F32))

    def work(first, last):
        conv_rows(sz, x3_ref, weights, conv_ref, last)
        add_conv_rows(sz, masks, stats, conv_ref, HALO - 1, first, last)

    for row in range(sz.rows + 2 * HALO):
        prepare(row)
    work(0, sz.rows + 2 * HALO - 2)
    out = copies.start(x_ref, act_hbm)
    put_stats(sz, stats.first, stats.second, stats_ref)
    wait(out)


def norm_of(sz, gathered_ref, member_ref):
    mean, squares = split_rows(own_sums(gathered_ref, member_ref), sz.channels)
    return mean, lax.rsqrt(squares - mean * mean + norm_epsilon)


def kernel_forward(sz, layer, limits_ref, member_ref, gathered_ref, before_ref, norm_ref, head_ref, weights_hbm, *rest):
    stats_ref, conv_ref, moments_ref, act_hbm, saved_hbm, x3_ref, buffer_ref, sems = rest
    copies = Copies(sems)
    weights = Weights(copies, head_ref, weights_hbm, buffer_ref, layer)
    halo = HALO - layer
    rows = sz.rows + 2 * halo
    skip = (halo - layer) * sz.width
    outs = []
    mean, inverse = norm_of(sz, gathered_ref, member_ref)
    moments_ref[...] = join_rows(mean, inverse)
    scale = 0.5 * norm_ref[layer - 1, 0:1, :] * inverse
    offset = 0.5 * norm_ref[layer - 1, 1:2, :] - mean * scale
    masks = Masks(sz, limits_ref)
    stats = Stats(sz)
    c = sz.channels

    def prepare(row):
        value = before_ref[line(sz, row), :]
        act, _ = silu_parts(value * scale + offset)
        put_shifted(sz, masks, x3_ref, row, act * tiled(sz, masks.valid(row - halo)))
        if row == halo + sz.rows - 1:
            outs.append(copies.start(x3_ref.at[pl.ds(halo * sz.width, sz.pixels), pl.ds(c, c)], act_hbm))

    def work(first, last):
        conv_rows(sz, x3_ref, weights, conv_ref, last)
        outs.append(copies.start(before_ref.at[pl.ds(skip, saved_hbm.shape[0])], saved_hbm))
        add_conv_rows(sz, masks, stats, conv_ref, halo - 1, first, last)

    for row in range(rows):
        prepare(row)
    work(0, rows - 2)
    put_stats(sz, stats.first, stats.second, stats_ref)
    wait(*outs)


def kernel_pool(sz, limits_ref, member_ref, gathered_ref, before_ref, norm_ref, index_hbm, near_hbm, far_hbm, *rest):
    cotangents, rest = rest[: sz.bands], rest[sz.bands :]
    (stats_ref, grad_ref, normed_ref, moments_ref), rest = rest[:4], rest[4:]
    shares, rest = rest[: sz.bands], rest[sz.bands :]
    (index_ref, near_ref, far_ref, cotangent_ref, spread_ref, act_ref, pooled_ref, grad16_ref, normed16_ref, sems) = rest
    c, w = sz.channels, sz.width
    half = w // 2
    windows = sz.rows // 2
    edge = HALO * w
    copies = Copies(sems)
    inputs = [
        copies.start(index_hbm, index_ref),
        copies.start(near_hbm.at[pl.ds(edge, w)], near_ref),
        copies.start(far_hbm.at[pl.ds(edge, w)], far_ref),
    ]
    inputs += [
        copies.start(
            ref, cotangent_ref.at[:, band_lanes(sz, n)]
        )
        for n, ref in enumerate(cotangents)
    ]
    mean, inverse = norm_of(sz, gathered_ref, member_ref)
    moments_ref[...] = join_rows(mean, inverse)
    gain = 0.5 * norm_ref[2, 0:1, :]
    shift = 0.5 * norm_ref[2, 1:2, :]
    halo = HALO - 3
    rows = sz.rows + 2 * halo
    lines = sz.pixels // 4
    groups = c // 128
    masks = Masks(sz, limits_ref)
    for row in range(rows):
        normed = (before_ref[line(sz, row), :] - mean) * inverse
        normed_ref[line(sz, row), :] = normed.astype(BF16)
        act, slope = silu_parts(normed * gain + shift)
        valid = tiled(sz, masks.valid(row - halo))
        grad_ref[line(sz, row), :] = slope * valid
        if halo <= row < halo + sz.rows:
            normed16_ref[line(sz, row - halo), :] = normed.astype(BF16)
            act = act * valid
            for g in range(groups):
                act_ref[g, line(sz, row - halo), :] = act[:, g * 128 : (g + 1) * 128]
    outs = send_shares(sz, copies, normed16_ref, shares, lines + sz.pixels)
    wait(*inputs)
    for p in range(windows):
        index = index_ref[p * half : (p + 1) * half, :]
        result = jnp.zeros(index.shape, F32)
        for corner in range(4):
            start = (2 * p + corner // 2) * w + corner % 2
            taken = jnp.concatenate(
                [act_ref[g, pl.ds(start, half, stride=2), :] for g in range(groups)], axis=1
            )
            result = jnp.where(index == corner, taken, result)
        pooled_ref[p * half : (p + 1) * half, :] = result.astype(BF16)
    outs += send_shares(sz, copies, pooled_ref, shares, 0)
    odd = lax.axis_index("rows") % 2 == 1
    for p in range(windows + 4):
        if p < 2:
            place = slice(p * half, (p + 1) * half)
            index = jnp.where(odd, near_ref[place, :].astype(jnp.int32), far_ref[place, :].astype(jnp.int32))
        elif p < windows + 2:
            index = index_ref[(p - 2) * half : (p - 1) * half, :]
        else:
            place = slice((p - windows - 2) * half, (p - windows - 1) * half)
            index = jnp.where(odd, far_ref[place, :].astype(jnp.int32), near_ref[place, :].astype(jnp.int32))
        given = cotangent_ref[p * half : (p + 1) * half, :].astype(F32)
        for corner in range(4):
            start = (2 * p + corner // 2) * w + corner % 2
            placed = jnp.where(index == corner, given, 0.0)
            for g in range(groups):
                spread_ref[g, pl.ds(start, half, stride=2), :] = placed[:, g * 128 : (g + 1) * 128]
    stats = Stats(sz)
    for row in range(rows):
        upstream = jnp.concatenate([spread_ref[g, line(sz, row + 1), :] for g in range(groups)], axis=1)
        grad = upstream * grad_ref[line(sz, row), :]
        grad_ref[line(sz, row), :] = grad
        if halo <= row < halo + sz.rows:
            grad16_ref[line(sz, row - halo), :] = grad.astype(BF16)
            stats.add(grad, grad * normed_ref[line(sz, row), :].astype(F32))
    outs += send_shares(sz, copies, grad16_ref, shares, lines)
    put_stats(sz, stats.first, stats.second, stats_ref)
    wait(*outs)


class ConvGrad:
    def __init__(self, sz, layer, masks, member_ref, moments_ref, gathered_ref, norm_ref):
        self.sz, self.masks = sz, masks
        _, inverse = split_rows(moments_ref[...], sz.channels)
        one, two = split_rows(own_sums(gathered_ref, member_ref), sz.channels)
        self.scale = norm_ref[layer, 0:1, :] * inverse
        self.one, self.two = one, two

    def row(self, row, grad, normed):
        value = self.scale * (grad - self.one - normed * self.two)
        return value * tiled(self.sz, self.masks.valid(row))


def kernel_backward(sz, layer, limits_ref, member_ref, gathered_ref, grad_ref, normed_ref, moments_ref, norm_ref,
                    head_ref, weights_hbm, saved_hbm, moments_below_ref, stats_ref, below_ref, normed_below_ref, totals_ref,
                    *rest):
    shares, (saved_ref, x3_ref, buffer_ref, grad16_ref, normed16_ref, sems) = rest[: sz.bands], rest[sz.bands :]
    copies = Copies(sems)
    weights = Weights(copies, head_ref, weights_hbm, buffer_ref, layer)
    saved = copies.start(saved_hbm, saved_ref)
    halo = layer + 1
    rows = sz.rows + 2 * halo
    masks = Masks(sz, limits_ref)
    conv_grad = ConvGrad(sz, layer, masks, member_ref, moments_ref, gathered_ref, norm_ref)
    below = layer - 1
    mean, inverse = split_rows(moments_below_ref[...], sz.channels)
    gain = 0.5 * norm_ref[below, 0:1, :]
    shift = 0.5 * norm_ref[below, 1:2, :]
    stats = Stats(sz)
    outs = []

    def prepare(row):
        value = conv_grad.row(row - halo, grad_ref[line(sz, row), :], normed_ref[line(sz, row), :].astype(F32))
        put_shifted(sz, masks, x3_ref, row, value, True)

    def work(first, last):
        conv_rows(sz, x3_ref, weights, below_ref, last, True)
        if first == 0:
            wait(saved)
        for row in range(first, last):
            normed = (saved_ref[line(sz, row), :] - mean) * inverse
            normed_below_ref[line(sz, row), :] = normed.astype(BF16)
            _, slope = silu_parts(normed * gain + shift)
            own = row - (halo - 1)
            grad = below_ref[line(sz, row), :] * slope * tiled(sz, masks.valid(own))
            below_ref[line(sz, row), :] = grad
            if 0 <= own < sz.rows:
                grad16_ref[line(sz, own), :] = grad.astype(BF16)
                normed16_ref[line(sz, own), :] = normed.astype(BF16)
                stats.add(grad, grad * normed)

    for row in range(rows):
        prepare(row)
    work(0, rows - 2)
    outs += send_shares(sz, copies, grad16_ref, shares, 0)
    outs += send_shares(sz, copies, normed16_ref, shares, sz.pixels)
    put_stats(sz, stats.first, stats.second, stats_ref)
    totals_ref[...] = all_sums(gathered_ref)
    wait(*outs)


def kernel_last(sz, limits_ref, member_ref, gathered_ref, grad_ref, normed_ref, moments_ref, norm_ref, head_ref,
                weights_hbm, *rest):
    parts, (out_hbm, totals_ref, pooled_hbm, x3_ref, buffer_ref, acc_ref, out_ref, sems) = (
        rest[: sz.bands], rest[sz.bands :]
    )
    copies = Copies(sems)
    weights = Weights(copies, head_ref, weights_hbm, buffer_ref, 0)
    lines = sz.pixels // 4
    outs = []
    for n, ref in enumerate(parts):
        target = line_share(pooled_hbm, (lax.axis_index("rows") ^ n) * lines, lines, lines)
        outs.append(copies.start(ref.at[pl.ds(0, lines)], target))
    totals_ref[...] = all_sums(gathered_ref)
    masks = Masks(sz, limits_ref)
    conv_grad = ConvGrad(sz, 0, masks, member_ref, moments_ref, gathered_ref, norm_ref)

    def prepare(row):
        value = conv_grad.row(row - 1, grad_ref[line(sz, row), :], normed_ref[line(sz, row), :].astype(F32))
        put_shifted(sz, masks, x3_ref, row, value, True)

    def work(first, last):
        conv_rows(sz, x3_ref, weights, acc_ref, last, True)
        pixels = slice(first * sz.width, last * sz.width)
        out_ref[pixels, :] = acc_ref[pixels, :].astype(BF16)

    for row in range(sz.rows + 2):
        prepare(row)
    work(0, sz.rows)
    outs.append(copies.start(out_ref, out_hbm))
    wait(*outs)


def kernel_weight_grad(sz, layer, first, limits_ref, member_ref, gathered_ref, moments_ref, norm_ref, *rest):
    w, q, c, bands = sz.width, sz.quarter, sz.channels, sz.bands
    pixels = sz.height * w
    given, rest = rest[:bands], rest[bands:]
    acts, rest = rest[:bands], rest[bands:]
    keep_hbm, send_hbm, grad_ref, normed_ref, act_ref, x9_ref, keep_ref, send_ref, term_ref, sems = rest
    copies = Copies(sems)
    inputs = []
    for n in range(bands):
        start = (lax.axis_index("rows") ^ n) * sz.pixels
        for source, target, top in ((given[n], grad_ref, first[0]), (given[n], normed_ref, first[1])):
            inputs.append(
                copies.start(source.at[pl.ds(top, sz.pixels)], line_share(target, start, sz.pixels, sz.pixels))
            )
    act_loads = [
        copies.start(
            acts[n], line_share(act_ref, (lax.axis_index("rows") ^ n) * sz.pixels, sz.pixels, sz.pixels)
        )
        for n in range(bands)
    ]
    band = lax.axis_index("rows")
    own = lax.axis_index("maps")
    tile = own_sums(gathered_ref, member_ref)
    one, two, inverse, gain = (jnp.zeros((1, q), F32) for _ in range(4))
    for b in range(bands):
        here = band == b
        one = jnp.where(here, tile[b : b + 1, :], one)
        two = jnp.where(here, tile[b + 4 : b + 5, :], two)
        inverse = jnp.where(here, moments_ref[b + 4 : b + 5, :], inverse)
        gain = jnp.where(here, norm_ref[layer, 0:1, b * q : (b + 1) * q], gain)
    wait(*inputs)
    masks = Masks(sz, limits_ref)
    blank = jnp.zeros((w, q), BF16)
    for row in range(sz.height):
        value = grad_ref[line(sz, row), :].astype(F32) - one - normed_ref[line(sz, row), :].astype(F32) * two
        value = (gain * inverse) * value * masks.valid_of_map(row)
        for j, piece in enumerate((shifted_left(sz, masks, value), value, shifted_right(sz, masks, value))):
            piece = piece.astype(BF16)
            for i in range(3):
                if 0 <= row + i - 1 < sz.height:
                    x9_ref[line(sz, row + i - 1), (3 * i + j) * q : (3 * i + j + 1) * q] = piece
    for j in range(3):
        x9_ref[line(sz, sz.height - 1), j * q : (j + 1) * q] = blank
        x9_ref[line(sz, 0), (6 + j) * q : (7 + j) * q] = blank
    share = c // sz.maps
    wait(*act_loads)
    term = lax.dot_general(
        act_ref[...], x9_ref[...], (((0,), (0,)), ((), ())), preferred_element_type=F32
    )
    term_ref[...] = term
    if layer == 0:
        others = [2 * place + (own & 1) for place in range(sz.maps // 2)]
        order = others + [other ^ 1 for other in others]
    else:
        order = [own ^ relative for relative in halving_order(sz.maps)]
    for position, other in enumerate(order):
        lines = pl.ds(pl.multiple_of(other * share, share), share)
        for tap in range(9):
            place = slice(tap * share, (tap + 1) * share)
            part = term_ref[lines, tap * q : (tap + 1) * q]
            if position < sz.maps // 2:
                keep_ref[position, place, :] = part
            else:
                send_ref[position - sz.maps // 2, place, :] = part.astype(BF16)
    wait(copies.start(keep_ref, keep_hbm), copies.start(send_ref, send_hbm))


def halving_order(maps):
    bits = maps.bit_length() - 1
    return [sum(((place >> (bits - 1 - k)) & 1) << k for k in range(bits)) for place in range(maps)]


def kernel_add(keep_hbm, received_hbm, out_ref, keep_ref, received_ref, sems):
    copies = Copies(sems)
    loads = [
        (copies.start(keep_hbm.at[k], keep_ref.at[k]), copies.start(received_hbm.at[k], received_ref.at[k]))
        for k in range(keep_ref.shape[0])
    ]
    for k, load in enumerate(loads):
        wait(*load)
        out_ref[k] = (keep_ref[k] + received_ref[k].astype(F32)).astype(BF16)


def kernel_halve(keep_hbm, received_hbm, next_keep_hbm, next_send_hbm, keep_ref, received_ref, send_ref, sems):
    half = next_keep_hbm.shape[0]
    copies = Copies(sems)
    loads = [
        [
            copies.start(source.at[part], target.at[part])
            for source, target in ((keep_hbm, keep_ref), (received_hbm, received_ref))
        ]
        for part in (pl.ds(half, half), pl.ds(0, half))
    ]
    wait(*loads[0])
    send_ref[...] = (keep_ref[half:] + received_ref[half:].astype(F32)).astype(BF16)
    first = copies.start(send_ref, next_send_hbm)
    wait(*loads[1])
    keep_ref[:half] += received_ref[:half].astype(F32)
    wait(first, copies.start(keep_ref.at[pl.ds(0, half)], next_keep_hbm))


def kernel_squares(sz, received_ref, keep1_hbm, last1_hbm, keep2_hbm, last2_hbm, totals2_ref, totals1_ref,
                   totals0_ref, squares_ref, shard_ref, norm_grad_ref, keep_ref, last_ref, sems):
    copies = Copies(sems)
    loads = [
        copies.start(source.at[0], target.at[k])
        for k, pair in enumerate(((keep1_hbm, last1_hbm), (keep2_hbm, last2_hbm)))
        for source, target in zip(pair, (keep_ref, last_ref))
    ]
    for layer, ref in enumerate((totals0_ref, totals1_ref, totals2_ref)):
        shift_row, gain_row = split_rows(ref[...], sz.channels)
        norm_grad_ref[layer, 0:1, :] = gain_row
        norm_grad_ref[layer, 1:2, :] = shift_row
    value = received_ref[0].astype(F32)
    for m in range(1, received_ref.shape[0]):
        value = value + received_ref[m].astype(F32)
    shard_ref[0] = value
    total = jnp.sum(value * value, axis=0, keepdims=True)
    wait(*loads)
    for layer in (1, 2):
        value = keep_ref[layer - 1] + last_ref[layer - 1].astype(F32)
        shard_ref[layer] = value
        total = total + jnp.sum(value * value, axis=0, keepdims=True)
    squares_ref[...] = jnp.broadcast_to(total[None], squares_ref.shape)


def kernel_adam(sz, rate, every_ref, step_ref, shard_ref, master_hbm, first_hbm, second_hbm, norm_grad_ref, norm_ref,
                norm_first_ref, norm_second_ref, total_hbm, first_out_hbm, second_out_hbm, master_out_hbm,
                norm_first_hbm, norm_second_hbm, norm_hbm,
                total_ref, master_ref, first_ref, second_ref, small_ref, sems):
    copies = Copies(sems)
    loads = [
        [
            copies.start(source.at[layer], target.at[layer])
            for source, target in ((master_hbm, master_ref), (first_hbm, first_ref), (second_hbm, second_ref))
        ]
        for layer in range(3)
    ]
    norm_grad = norm_grad_ref[...]
    square = jnp.sum(jnp.sum(every_ref[...], axis=0)) + jnp.sum(norm_grad * norm_grad)
    total = jnp.sqrt(jnp.full((1, 128), square, F32))
    total_ref[...] = total
    outs = [copies.start(total_ref, total_hbm)]
    scale = jnp.minimum(1.0, clip_limit / total)
    count = jnp.full((1, 128), step_ref[0].astype(F32), F32)
    first_fix = 1.0 - jnp.exp(count * math.log(first_decay))
    second_fix = 1.0 - jnp.exp(count * math.log(second_decay))
    for layer in range(3):
        wait(*loads[layer])
        first_ref[layer], second_ref[layer], master_ref[layer] = adam(
            master_ref[layer], shard_ref[layer], first_ref[layer], second_ref[layer], rate, weight_decay,
            scale, first_fix, second_fix,
        )
        for source, target in (
            (first_ref, first_out_hbm), (second_ref, second_out_hbm), (master_ref, master_out_hbm)
        ):
            outs.append(copies.start(source.at[layer], target.at[layer]))
    wide = [jnp.concatenate([v] * (sz.channels // 128), axis=1) for v in (scale, first_fix, second_fix)]
    for layer in range(3):
        small_ref[0, layer], small_ref[1, layer], small_ref[2, layer] = adam(
            norm_ref[layer], norm_grad[layer], norm_first_ref[layer], norm_second_ref[layer], norm_rate, 0.0, *wide
        )
    for k, target in enumerate((norm_first_hbm, norm_second_hbm, norm_hbm)):
        outs.append(copies.start(small_ref.at[k], target))
    wait(*outs)


def adam(param, grad, first, second, rate, decay, scale, first_fix, second_fix):
    clipped = scale * grad
    first_new = first_decay * first + (1.0 - first_decay) * clipped
    second_new = second_decay * second + (1.0 - second_decay) * clipped * clipped
    update = first_new / first_fix / (jnp.sqrt(second_new / second_fix) + adam_epsilon)
    return first_new, second_new, param - rate * (update + decay * param)


def call(kernel, name, outs, ins, scratch=(), flops=0, moved=0, hbm_ins=(), hbm_outs=(), smem_ins=(), sems=1):
    spaces_in = [
        pltpu.SMEM if k in smem_ins else pltpu.HBM if k in hbm_ins else pltpu.VMEM for k in range(len(ins))
    ]
    spaces_out = [pltpu.HBM if k in hbm_outs else pltpu.VMEM for k in range(len(outs))]
    return pl.pallas_call(
        kernel,
        out_shape=tuple(space(out.shape, out.dtype) for space, out in zip(spaces_out, outs)),
        in_specs=[spec(space) for space in spaces_in],
        out_specs=tuple(spec(space) for space in spaces_out),
        scratch_shapes=list(scratch) + [pltpu.SemaphoreType.DMA((sems,))],
        compiler_params=params(SPACE),
        cost_estimate=pl.CostEstimate(flops=flops, bytes_accessed=moved, transcendentals=0),
        name=name,
    )(*[v if k in smem_ins else pltpu.with_memory_space_constraint(v, spaces_in[k]) for k, v in enumerate(ins)])


def local(sz, block_input, conv_weights, norm_params, pool_index, task_mask, map_kind, map_domain, out_grad, step,
          conv_master, conv_moment1, conv_moment2, norm_moment1, norm_moment2):
    w, c, q = sz.width, sz.channels, sz.quarter
    half = w // 2
    n_maps, bands = sz.maps, sz.bands
    x = block_input.reshape(sz.pixels, c)
    index = pool_index.reshape(sz.pixels // 4, c)
    norms, norm_first, norm_second = (v.transpose(1, 0, 2) for v in (norm_params, norm_moment1, norm_moment2))
    edge = HALO * w
    lines = sz.pixels // 4

    def shape(dims, dtype):
        return jax.ShapeDtypeStruct(dims, dtype)

    def pixel_shape(rows, dtype):
        return shape((rows * w, c), dtype)

    def pixel_space(rows, dtype, times=1):
        return pltpu.VMEM((rows * w, times * c), dtype)

    def share_shapes(count):
        return [shape((count, q), BF16)] * bands

    stats_shape = shape((sz.devices, 8, c // 4), F32)
    tile_shape = shape((8, c // 4), F32)
    weight_space = pltpu.VMEM((9 - HEAD, c, c), BF16)


    def conv_flops(rows):
        return rows * w * 9 * c * c * 2

    def spread(stats):
        return lax.all_to_all(stats, AXES, 0, 0, tiled=True)

    def trade(shares):
        return [shares[0]] + [
            lax.ppermute(shares[n], "rows", [(i, i ^ n) for i in range(bands)]) for n in range(1, bands)
        ]

    def swap(act, n):
        return lax.ppermute(act, "rows", [(i, i ^ n) for i in range(bands)])

    tie = lax.optimization_barrier

    to_near, to_far, own_x = call(
        functools.partial(kernel_edges, sz), "edges",
        [shape((edge + 2 * half, c), BF16)] * 2 + [pixel_shape(sz.rows, BF16)], [x, index],
        [pltpu.VMEM((2, 2 * half, c), jnp.int32)], hbm_ins=(0, 1), sems=5,
    )
    far = lax.ppermute(to_far, "rows", [(i + 1 - k, i + k) for i in range(1, bands - 1, 2) for k in (0, 1)])
    near = swap(to_near, 1)

    limits, member = call(
        functools.partial(kernel_places, sz), "places", [shape((8, 128), jnp.int32), stats_shape],
        [map_kind, map_domain], smem_ins=(0, 1),
    )
    labelled = (out_grad * task_mask[..., None].astype(BF16)).reshape(sz.height // 2 * half, q)
    labelled = jnp.pad(labelled, ((2 * half, 2 * half), (0, 0)))
    consts = [limits, member]

    rows = sz.rows + 2 * HALO
    stats, conv, kept = call(
        functools.partial(kernel_first, sz), "first",
        [stats_shape, pixel_shape(rows - 2, F32), pixel_shape(sz.rows, BF16)], [limits, near, own_x, far, conv_weights[0, :HEAD], conv_weights],
        [pixel_space(rows, BF16, 3), weight_space], conv_flops(rows - 2), hbm_ins=(5,), hbm_outs=(2,), sems=4,
    )
    def head(layer, weights):
        return weights[layer, :HEAD]

    cot_lines = (sz.rows // 2 + 4) * half
    cots = call(functools.partial(kernel_spans, sz), "spans", share_shapes(cot_lines), [labelled], hbm_outs=range(bands), sems=bands)
    stats, weights, *cots = tie((stats, conv_weights, *cots))
    gathered = spread(stats)
    cots = trade(cots)
    acts = [[kept, swap(kept, 1), swap(kept, 2)]]
    moments = []
    saves = []
    for layer in (1, 2):
        rows = sz.rows + 2 * (HALO - layer)
        outs = [
            stats_shape, pixel_shape(rows - 2, F32), tile_shape, pixel_shape(sz.rows, BF16),
            pixel_shape(sz.rows + 2 * layer, F32),
        ]
        scratch = [pixel_space(rows, BF16, 3), weight_space]
        stats, conv, moment, act, saved = call(
            functools.partial(kernel_forward, sz, layer), "forward", outs,
            consts + [gathered, conv, norms, head(layer, weights), conv_weights], scratch,
            conv_flops(rows - 2), hbm_ins=(6,), hbm_outs=(3, 4), sems=5,
        )
        moments.append(moment)
        saves.append(saved)
        if layer == 1:
            stats, weights, *acts[0] = tie((stats, conv_weights, *acts[0]))
            gathered = spread(stats)
        else:
            stats, *rest = tie((stats, *cots, *acts[1]))
            cots, acts[1] = rest[:bands], rest[bands:]
            gathered = spread(stats)
        acts[layer - 1].append(swap(acts[layer - 1][2], 1))
        acts.append([act, swap(act, 1), swap(act, 2)])

    rows = sz.rows + 2 * (HALO - 3)
    stats, grad, normed, moment, *shares = call(
        functools.partial(kernel_pool, sz), "pool",
        [stats_shape, pixel_shape(rows, F32), pixel_shape(rows, BF16), tile_shape]
        + share_shapes(lines + 2 * sz.pixels),
        consts + [gathered, conv, norms, index, near, far] + cots,
        [
            pltpu.VMEM((lines, c), jnp.int32), pltpu.VMEM((2 * half, c), BF16), pltpu.VMEM((2 * half, c), BF16),
            pltpu.VMEM((cot_lines, c), BF16),
            pltpu.VMEM((c // 128, (rows + 2) * w, 128), F32), pltpu.VMEM((c // 128, sz.pixels, 128), F32),
            pltpu.VMEM((lines, c), BF16), pixel_space(sz.rows, BF16), pixel_space(sz.rows, BF16),
        ],
        conv_flops(4), hbm_ins=range(5, 8 + bands), hbm_outs=range(4, 4 + bands), sems=3 + 4 * bands,
    )
    moments.append(moment)
    stats, weights, acts[0][3], *acts[2] = tie((stats, conv_weights, acts[0][3], *acts[2]))
    gathered = spread(stats)
    exchanged = trade(shares)
    acts[2].append(swap(acts[2][2], 1))
    pooled_parts = exchanged

    totals = [None, None, None]
    share = 9 * (c // n_maps)
    steps = n_maps.bit_length() - 1

    def part_shape(parts, dtype):
        return shape((parts, share, q), dtype)

    def part_space(parts, dtype):
        return pltpu.VMEM((parts, share, q), dtype)

    def weight_grad(layer, gathered, given, first):
        scratch = [
            pltpu.VMEM((sz.height * w, q), BF16),
            pltpu.VMEM((sz.height * w, q), BF16),
            pltpu.VMEM((sz.height * w, c), BF16),
            pltpu.VMEM((sz.height * w, 9 * q), BF16),
        ]
        outs = [part_shape(n_maps // 2, dtype) for dtype in (F32, BF16)]
        scratch += [part_space(n_maps // 2, dtype) for dtype in (F32, BF16)]
        scratch.append(pltpu.VMEM((c, 9 * q), F32))
        return call(
            functools.partial(kernel_weight_grad, sz, layer, first), "weight_grad", outs,
            consts + [gathered, moments[layer], norms] + given + acts[layer], scratch, conv_flops(sz.rows),
            hbm_ins=range(5, 5 + 2 * bands), hbm_outs=(0, 1), sems=3 * bands + 2,
        )

    def step_of(send, k):
        return lax.ppermute(send, "maps", [(m, m ^ (1 << k)) for m in range(n_maps)])

    def halved(keep, received):
        size = keep.shape[0] // 2
        return call(
            kernel_halve, "halve", [part_shape(size, dtype) for dtype in (F32, BF16)], [keep, received],
            [part_space(2 * size, F32), part_space(2 * size, BF16), part_space(size, BF16)],
            hbm_ins=(0, 1), hbm_outs=(0, 1), sems=6,
        )

    def halve(keep, received, k):
        while k < steps - 1:
            k += 1
            keep, send = halved(keep, received)
            received = step_of(send, k)
        return keep, received

    shards = [None, None, None]
    for layer in (2, 1):
        halo = layer + 1
        rows = sz.rows + 2 * halo
        received, gathered_here = exchanged, gathered
        stats, grad, normed, totals[layer], *shares = call(
            functools.partial(kernel_backward, sz, layer), "backward",
            [stats_shape, pixel_shape(rows - 2, F32), pixel_shape(rows - 2, BF16), tile_shape]
            + share_shapes(2 * sz.pixels),
            consts + [
                gathered, grad, normed, moments[layer], norms, head(layer, weights), conv_weights, saves[layer - 1],
                moments[layer - 1],
            ],
            [
                pixel_space(rows - 2, F32), pixel_space(rows, BF16, 3), weight_space, pixel_space(sz.rows, BF16),
                pixel_space(sz.rows, BF16),
            ],
            conv_flops(rows - 2), hbm_ins=(8, 9), hbm_outs=range(4, 4 + bands), sems=4 + 2 * bands,
        )
        if layer == 2:
            stats, weights, acts[1][3], acts[2][3], *received = tie(
                (stats, conv_weights, acts[1][3], acts[2][3], *received)
            )
            gathered = spread(stats)
            exchanged = trade(shares)
            keep2, send2 = weight_grad(2, gathered_here, received, (lines, lines + sz.pixels))
            gathered, send2 = tie((gathered, send2))
            arrived2 = step_of(send2, 0)
        else:
            stats, weights, *received = tie((stats, conv_weights, *received))
            gathered = spread(stats)
            exchanged = trade(shares)
            keep1, send1 = weight_grad(1, gathered_here, received, (0, sz.pixels))
            gathered, send1, arrived2 = tie((gathered, send1, arrived2))
            arrived1 = step_of(send1, 0)
            keep2, send2 = halved(keep2, arrived2)

    arrived2 = step_of(send2, 1)
    keep0, send0 = weight_grad(0, gathered, exchanged, (0, sz.pixels))
    send0, arrived2 = tie((send0, arrived2))
    arrived0 = step_of(send0, 0)
    keep1, send1 = halved(keep1, arrived1)
    keep2, send2 = halved(keep2, arrived2)
    arrived1 = step_of(send1, 1)
    arrived2 = step_of(send2, 2)
    arrived0, arrived1, arrived2 = tie((arrived0, arrived1, arrived2))
    half_maps = n_maps // 2
    (partial,) = call(
        kernel_add, "add", [part_shape(half_maps, BF16)], [keep0, arrived0],
        [part_space(half_maps, dtype) for dtype in (F32, BF16)], hbm_ins=(0, 1), sems=2 * half_maps,
    )
    alike = [[m for m in range(n_maps) if m & 1 == bit] for bit in (0, 1)]
    received = lax.all_to_all(partial, "maps", 0, 0, tiled=True, axis_index_groups=alike)
    shards[2] = halve(keep2, arrived2, 2)
    shards[1] = halve(keep1, arrived1, 1)
    input_grad, totals[0], pooled = call(
        functools.partial(kernel_last, sz), "last",
        [pixel_shape(sz.rows, BF16), tile_shape, shape((sz.height // 2 * half, q), BF16)],
        consts + [gathered, grad, normed, moments[0], norms, head(0, weights), conv_weights] + pooled_parts,
        [pixel_space(sz.rows + 2, BF16, 3), weight_space, pixel_space(sz.rows, F32), pixel_space(sz.rows, BF16)],
        conv_flops(sz.rows), hbm_ins=range(8, 9 + bands), hbm_outs=(0, 2), sems=4 + bands,
    )

    norm_shape = shape((3, 2, c), F32)
    squares, shard, norm_grad = call(
        functools.partial(kernel_squares, sz), "squares",
        [shape((sz.devices, 1, q), F32), part_shape(3, F32), norm_shape],
        [received, *shards[1], *shards[2], totals[2], totals[1], totals[0]],
        [part_space(2, F32), part_space(2, BF16)], hbm_ins=range(1, 5), sems=4,
    )
    every = lax.all_to_all(squares, AXES, 0, 0, tiled=True)
    rate = 2.0 / math.sqrt(9.0 * c)
    total, conv_first, conv_second, conv_new, norm_first, norm_second, norm_new = call(
        functools.partial(kernel_adam, sz, rate), "adam",
        [shape((1, 128), F32)] + [part_shape(3, F32)] * 3 + [norm_shape] * 3,
        [every, step, shard]
        + [v.reshape(3, share, q) for v in (conv_master, conv_moment1, conv_moment2)]
        + [norm_grad, norms, norm_first, norm_second],
        [pltpu.VMEM((1, 128), F32)] + [part_space(3, F32)] * 3 + [pltpu.VMEM((3, 3, 2, c), F32)],
        hbm_ins=(3, 4, 5), hbm_outs=range(7), smem_ins=(1,), sems=22,
    )
    return (
        pooled.reshape(1, sz.height // 2, half, q),
        input_grad.reshape(block_input.shape),
        total[0, :1],
        conv_first.reshape(conv_master.shape),
        conv_second.reshape(conv_master.shape),
        conv_new.reshape(conv_master.shape),
        norm_first.transpose(1, 0, 2),
        norm_second.transpose(1, 0, 2),
        norm_new.transpose(1, 0, 2),
    )


def solution(mesh):
    def run(*args):
        bands = mesh.shape["rows"]
        maps = mesh.shape["maps"]
        shape = args[0].shape
        sz = Sizes(maps, bands, shape[1] // bands, shape[2], shape[3])
        return jax.shard_map(
            functools.partial(local, sz),
            mesh=mesh,
            in_specs=(
                P("maps", "rows", None, None),
                P(),
                P(),
                P("maps", "rows", None, None),
                P("maps", None, None),
                P(),
                P(),
                P("maps", None, None, "rows"),
                P(),
                P(None, None, "maps", "rows"),
                P(None, None, "maps", "rows"),
                P(None, None, "maps", "rows"),
                P(),
                P(),
            ),
            out_specs=(
                P("maps", None, None, "rows"),
                P("maps", "rows", None, None),
                P(),
                P(None, None, "maps", "rows"),
                P(None, None, "maps", "rows"),
                P(None, None, "maps", "rows"),
                P(),
                P(),
                P(),
            ),
            check_vma=False,
        )(*args)

    return run
```

```python
import functools
import math

import jax
import jax.numpy as jnp
from jax import lax
from jax.experimental import pallas as pl
from jax.experimental.pallas import tpu as pltpu
from jax.sharding import PartitionSpec as P

DOMAINS = 4
norm_epsilon = 1e-05
clip_limit = 1.0
first_decay = 0.9
second_decay = 0.999
adam_epsilon = 1e-08
norm_rate = 0.5
weight_decay = 0.01

HALO = 6
SPACE = 28
AXES = ("maps", "rows")
F32 = jnp.float32
BF16 = jnp.bfloat16


class Sizes:
    def __init__(self, maps, bands, rows, width, channels):
        self.maps = maps
        self.bands = bands
        self.devices = maps * bands
        self.rows = rows
        self.width = width
        self.channels = channels
        self.height = rows * bands
        self.short_height = 2 * (self.height * 7 // 16)
        self.short_width = 2 * (width * 13 // 32)
        self.pixels = rows * width
        self.quarter = channels // bands


def spec(space):
    return pl.BlockSpec(memory_space=space)


def params(megabytes):
    return pltpu.CompilerParams(vmem_limit_bytes=megabytes << 20)


class Copies:
    def __init__(self, sems):
        self.sems = sems
        self.used = 0

    def start(self, source, target):
        copy = pltpu.make_async_copy(source, target, self.sems.at[self.used])
        self.used += 1
        copy.start()
        return copy


def wait(*copies):
    for copy in copies:
        copy.wait()


def line_share(ref, start, step, size):
    return ref.at[pl.ds(pl.multiple_of(start, step), size)]


def own_sums(gathered_ref, weights_ref):
    return jnp.sum(gathered_ref[...] * weights_ref[...], axis=0)


def all_sums(gathered_ref):
    return jnp.sum(gathered_ref[...], axis=0)


def split_rows(tile, channels):
    first = jnp.concatenate([tile[k : k + 1, :] for k in range(4)], axis=1)
    second = jnp.concatenate([tile[k : k + 1, :] for k in range(4, 8)], axis=1)
    return first, second


def join_rows(first, second):
    lanes = first.shape[1] // 4
    return jnp.concatenate(
        [row[:, k * lanes : (k + 1) * lanes] for row in (first, second) for k in range(4)], axis=0
    )


def tiled(sz, value):
    return jnp.concatenate([value] * (sz.channels // value.shape[1]), axis=1)


class Masks:
    def __init__(self, sz, limits_ref):
        self.col = lax.broadcasted_iota(jnp.int32, (sz.width, 128), 0)
        self.wide = jnp.where(self.col < limits_ref[2:3, :], 1.0, 0.0)
        self.inner_left = jnp.where(self.col > 0, 1.0, 0.0)
        self.inner_right = jnp.where(self.col < sz.width - 1, 1.0, 0.0)
        self.limits_ref = limits_ref

    def valid(self, row):
        inside = (self.limits_ref[0:1, :] <= row) & (self.limits_ref[1:2, :] > row)
        return self.wide * jnp.where(inside, 1.0, 0.0)

    def valid_of_map(self, row):
        return self.wide * jnp.where(self.limits_ref[3:4, :] > row, 1.0, 0.0)


def line(sz, row):
    return slice(row * sz.width, (row + 1) * sz.width)


def shifted_right(sz, masks, value):
    mask = masks.inner_left
    return pltpu.roll(value, 1, 0) * (mask if value.shape[1] == 128 else tiled(sz, mask))


def shifted_left(sz, masks, value):
    mask = masks.inner_right
    return pltpu.roll(value, sz.width - 1, 0) * (mask if value.shape[1] == 128 else tiled(sz, mask))


def put_shifted(sz, masks, x3_ref, row, value, reverse=False):
    before = shifted_right(sz, masks, value)
    after = shifted_left(sz, masks, value)
    if reverse:
        before, after = after, before
    c = sz.channels
    x3_ref[line(sz, row), 0:c] = before.astype(BF16)
    x3_ref[line(sz, row), c : 2 * c] = value.astype(BF16)
    x3_ref[line(sz, row), 2 * c : 3 * c] = after.astype(BF16)


def fold(value):
    total = value[0:8, :]
    for k in range(1, value.shape[0] // 8):
        total = total + value[8 * k : 8 * (k + 1), :]
    return total


HEAD = 1


class Weights:
    def __init__(self, copies, head_ref, weights_hbm, buffer_ref, layer):
        self.head_ref, self.buffer_ref = head_ref, buffer_ref
        self.loads = {
            first: copies.start(
                weights_hbm.at[layer, pl.ds(first, 3 - first % 3)],
                buffer_ref.at[pl.ds(first - HEAD, 3 - first % 3)],
            )
            for first in (HEAD, 3, 6)
        }

    def wait(self, tap):
        if tap in self.loads:
            wait(self.loads[tap])

    def taps(self, first, last):
        if first < HEAD:
            part = self.head_ref[first:last]
        else:
            part = self.buffer_ref[first - HEAD : last - HEAD]
        return part.reshape(-1, part.shape[-1])


def conv_rows(sz, x3_ref, weights, out_ref, rows, reverse=False):
    c, w = sz.channels, sz.width
    n = rows * w
    spans = [(0, HEAD), (HEAD, 3), (3, 6), (6, 9)]
    if reverse:
        spans = [(tap, tap + 1) for tap in range(9)]
    for first, last in spans:
        weights.wait(first)
        i = first // 3
        start = (2 - i if reverse else i) * w
        lhs = x3_ref[start : start + n, (first - 3 * i) * c : (last - 3 * i) * c]
        across = 1 if reverse else 0
        term = lax.dot_general(
            lhs, weights.taps(first, last), (((1,), (across,)), ((), ())), preferred_element_type=F32
        )
        if first == 0:
            out_ref[...] = term
        else:
            out_ref[...] += term


def put_stats(sz, first, second, out_ref):
    tile = join_rows(jnp.sum(first, axis=0, keepdims=True), jnp.sum(second, axis=0, keepdims=True))
    out_ref[...] = jnp.broadcast_to(tile[None], out_ref.shape)


def silu_parts(half):
    t = jnp.tanh(half)
    product = half * t
    return half + product, (0.5 + 0.5 * t) * (1.0 + (half - product))


class Stats:
    def __init__(self, sz):
        self.first = jnp.zeros((8, sz.channels), F32)
        self.second = jnp.zeros((8, sz.channels), F32)

    def add(self, first, second):
        self.first = self.first + fold(first)
        self.second = self.second + fold(second)


def add_conv_rows(sz, masks, stats, conv_ref, skip, first, last):
    for row in range(max(first, skip), min(last, skip + sz.rows)):
        value = conv_ref[line(sz, row), :]
        masked = value * tiled(sz, masks.valid(row - skip))
        stats.add(masked, masked * value)


def band_lanes(sz, n):
    return pl.ds(pl.multiple_of((lax.axis_index("rows") ^ n) * sz.quarter, sz.quarter), sz.quarter)


def send_shares(sz, copies, source_ref, targets, first):
    lines = source_ref.shape[0]
    return [
        copies.start(source_ref.at[:, band_lanes(sz, n)], target.at[pl.ds(first, lines)])
        for n, target in enumerate(targets)
    ]


def kernel_spans(sz, given_ref, *rest):
    shares, sems = rest[: sz.bands], rest[sz.bands]
    copies = Copies(sems)
    span = sz.rows // 2 * (sz.width // 2)
    wait(*[
        copies.start(line_share(given_ref, (lax.axis_index("rows") ^ n) * span, span, share.shape[0]), share)
        for n, share in enumerate(shares)
    ])


def kernel_edges(sz, x_hbm, index_hbm, near_ref, far_ref, x_ref, index_ref, sems):
    copies = Copies(sems)
    edge = HALO * sz.width
    few = sz.width
    odd = lax.axis_index("rows") % 2
    last = index_hbm.shape[0] - few
    loads = []
    rest = []
    for k, (first, target) in enumerate(((1 - odd, near_ref), (odd, far_ref))):
        loads.append(copies.start(line_share(index_hbm, first * last, few, few), index_ref.at[k]))
        rest.append(copies.start(line_share(x_hbm, first * (sz.pixels - edge), edge, edge), target.at[pl.ds(0, edge)]))
    rest.append(copies.start(x_hbm, x_ref))
    wait(*loads)
    near_ref[edge : edge + few, :] = index_ref[0].astype(BF16)
    far_ref[edge : edge + few, :] = index_ref[1].astype(BF16)
    wait(*rest)


def kernel_places(sz, kind_ref, domain_ref, limits_ref, member_ref, _):
    m, r = lax.axis_index("maps"), lax.axis_index("rows")
    start = r * sz.rows

    def rows_of(k):
        return jnp.where(kind_ref[k] == 1, sz.height, sz.short_height)

    def cols_of(k):
        return jnp.where(kind_ref[k] == 1, sz.short_width, sz.width)

    own = domain_ref[m]
    area = jnp.int32(0)
    for k in range(sz.maps):
        area = area + jnp.where(domain_ref[k] == own, rows_of(k) * cols_of(k), 0)
    tile = member_ref.shape[1:]
    weight = 1.0 / jnp.full(tile, area.astype(F32))
    for k in range(sz.maps):
        value = jnp.where(domain_ref[k] == own, weight, 0.0)
        for b in range(sz.bands):
            member_ref[k * sz.bands + b] = value
    line = lax.broadcasted_iota(jnp.int32, limits_ref.shape, 0)
    limits_ref[...] = jnp.where(
        line == 0, -start, jnp.where(line == 1, rows_of(m) - start, jnp.where(line == 2, cols_of(m), rows_of(m)))
    )


def kernel_first(sz, limits_ref, near_ref, x_ref, far_ref, head_ref, weights_hbm, stats_ref, conv_ref, act_hbm, x3_ref,
                 buffer_ref, sems):
    copies = Copies(sems)
    weights = Weights(copies, head_ref, weights_hbm, buffer_ref, 0)
    masks = Masks(sz, limits_ref)
    stats = Stats(sz)

    odd = lax.axis_index("rows") % 2 == 1

    def prepare(row):
        if row < HALO:
            value = jnp.where(odd, near_ref[line(sz, row), :], far_ref[line(sz, row), :])
        elif row < HALO + sz.rows:
            value = x_ref[line(sz, row - HALO), :]
        else:
            below = line(sz, row - HALO - sz.rows)
            value = jnp.where(odd, far_ref[below, :], near_ref[below, :])
        put_shifted(sz, masks, x3_ref, row, value.astype(F32))

    def work(first, last):
        conv_rows(sz, x3_ref, weights, conv_ref, last)
        add_conv_rows(sz, masks, stats, conv_ref, HALO - 1, first, last)

    for row in range(sz.rows + 2 * HALO):
        prepare(row)
    work(0, sz.rows + 2 * HALO - 2)
    out = copies.start(x_ref, act_hbm)
    put_stats(sz, stats.first, stats.second, stats_ref)
    wait(out)


def norm_of(sz, gathered_ref, member_ref):
    mean, squares = split_rows(own_sums(gathered_ref, member_ref), sz.channels)
    return mean, lax.rsqrt(squares - mean * mean + norm_epsilon)


def kernel_forward(sz, layer, limits_ref, member_ref, gathered_ref, before_ref, norm_ref, head_ref, weights_hbm, *rest):
    stats_ref, conv_ref, moments_ref, act_hbm, saved_hbm, x3_ref, buffer_ref, sems = rest
    copies = Copies(sems)
    weights = Weights(copies, head_ref, weights_hbm, buffer_ref, layer)
    halo = HALO - layer
    rows = sz.rows + 2 * halo
    skip = (halo - layer) * sz.width
    outs = []
    mean, inverse = norm_of(sz, gathered_ref, member_ref)
    moments_ref[...] = join_rows(mean, inverse)
    scale = 0.5 * norm_ref[layer - 1, 0:1, :] * inverse
    offset = 0.5 * norm_ref[layer - 1, 1:2, :] - mean * scale
    masks = Masks(sz, limits_ref)
    stats = Stats(sz)
    c = sz.channels

    def prepare(row):
        value = before_ref[line(sz, row), :]
        act, _ = silu_parts(value * scale + offset)
        put_shifted(sz, masks, x3_ref, row, act * tiled(sz, masks.valid(row - halo)))
        if row == halo + sz.rows - 1:
            outs.append(copies.start(x3_ref.at[pl.ds(halo * sz.width, sz.pixels), pl.ds(c, c)], act_hbm))

    def work(first, last):
        conv_rows(sz, x3_ref, weights, conv_ref, last)
        outs.append(copies.start(before_ref.at[pl.ds(skip, saved_hbm.shape[0])], saved_hbm))
        add_conv_rows(sz, masks, stats, conv_ref, halo - 1, first, last)

    for row in range(rows):
        prepare(row)
    work(0, rows - 2)
    put_stats(sz, stats.first, stats.second, stats_ref)
    wait(*outs)


def kernel_pool(sz, limits_ref, member_ref, gathered_ref, before_ref, norm_ref, index_hbm, near_hbm, far_hbm, *rest):
    cotangents, rest = rest[: sz.bands], rest[sz.bands :]
    (stats_ref, grad_ref, normed_ref, moments_ref), rest = rest[:4], rest[4:]
    shares, rest = rest[: sz.bands], rest[sz.bands :]
    (index_ref, near_ref, far_ref, cotangent_ref, spread_ref, act_ref, pooled_ref, grad16_ref, normed16_ref, sems) = rest
    c, w = sz.channels, sz.width
    half = w // 2
    windows = sz.rows // 2
    edge = HALO * w
    copies = Copies(sems)
    inputs = [
        copies.start(index_hbm, index_ref),
        copies.start(near_hbm.at[pl.ds(edge, w)], near_ref),
        copies.start(far_hbm.at[pl.ds(edge, w)], far_ref),
    ]
    inputs += [
        copies.start(
            ref, cotangent_ref.at[:, band_lanes(sz, n)]
        )
        for n, ref in enumerate(cotangents)
    ]
    mean, inverse = norm_of(sz, gathered_ref, member_ref)
    moments_ref[...] = join_rows(mean, inverse)
    gain = 0.5 * norm_ref[2, 0:1, :]
    shift = 0.5 * norm_ref[2, 1:2, :]
    halo = HALO - 3
    rows = sz.rows + 2 * halo
    lines = sz.pixels // 4
    groups = c // 128
    masks = Masks(sz, limits_ref)
    for row in range(rows):
        normed = (before_ref[line(sz, row), :] - mean) * inverse
        normed_ref[line(sz, row), :] = normed.astype(BF16)
        act, slope = silu_parts(normed * gain + shift)
        valid = tiled(sz, masks.valid(row - halo))
        grad_ref[line(sz, row), :] = slope * valid
        if halo <= row < halo + sz.rows:
            normed16_ref[line(sz, row - halo), :] = normed.astype(BF16)
            act = act * valid
            for g in range(groups):
                act_ref[g, line(sz, row - halo), :] = act[:, g * 128 : (g + 1) * 128]
    outs = send_shares(sz, copies, normed16_ref, shares, lines + sz.pixels)
    wait(*inputs)
    for p in range(windows):
        index = index_ref[p * half : (p + 1) * half, :]
        result = jnp.zeros(index.shape, F32)
        for corner in range(4):
            start = (2 * p + corner // 2) * w + corner % 2
            taken = jnp.concatenate(
                [act_ref[g, pl.ds(start, half, stride=2), :] for g in range(groups)], axis=1
            )
            result = jnp.where(index == corner, taken, result)
        pooled_ref[p * half : (p + 1) * half, :] = result.astype(BF16)
    outs += send_shares(sz, copies, pooled_ref, shares, 0)
    odd = lax.axis_index("rows") % 2 == 1
    for p in range(windows + 4):
        if p < 2:
            place = slice(p * half, (p + 1) * half)
            index = jnp.where(odd, near_ref[place, :].astype(jnp.int32), far_ref[place, :].astype(jnp.int32))
        elif p < windows + 2:
            index = index_ref[(p - 2) * half : (p - 1) * half, :]
        else:
            place = slice((p - windows - 2) * half, (p - windows - 1) * half)
            index = jnp.where(odd, far_ref[place, :].astype(jnp.int32), near_ref[place, :].astype(jnp.int32))
        given = cotangent_ref[p * half : (p + 1) * half, :].astype(F32)
        for corner in range(4):
            start = (2 * p + corner // 2) * w + corner % 2
            placed = jnp.where(index == corner, given, 0.0)
            for g in range(groups):
                spread_ref[g, pl.ds(start, half, stride=2), :] = placed[:, g * 128 : (g + 1) * 128]
    stats = Stats(sz)
    for row in range(rows):
        upstream = jnp.concatenate([spread_ref[g, line(sz, row + 1), :] for g in range(groups)], axis=1)
        grad = upstream * grad_ref[line(sz, row), :]
        grad_ref[line(sz, row), :] = grad
        if halo <= row < halo + sz.rows:
            grad16_ref[line(sz, row - halo), :] = grad.astype(BF16)
            stats.add(grad, grad * normed_ref[line(sz, row), :].astype(F32))
    outs += send_shares(sz, copies, grad16_ref, shares, lines)
    put_stats(sz, stats.first, stats.second, stats_ref)
    wait(*outs)


class ConvGrad:
    def __init__(self, sz, layer, masks, member_ref, moments_ref, gathered_ref, norm_ref):
        self.sz, self.masks = sz, masks
        _, inverse = split_rows(moments_ref[...], sz.channels)
        one, two = split_rows(own_sums(gathered_ref, member_ref), sz.channels)
        self.scale = norm_ref[layer, 0:1, :] * inverse
        self.one, self.two = one, two

    def row(self, row, grad, normed):
        value = self.scale * (grad - self.one - normed * self.two)
        return value * tiled(self.sz, self.masks.valid(row))


def kernel_backward(sz, layer, limits_ref, member_ref, gathered_ref, grad_ref, normed_ref, moments_ref, norm_ref,
                    head_ref, weights_hbm, saved_hbm, moments_below_ref, stats_ref, below_ref, normed_below_ref, totals_ref,
                    *rest):
    shares, (saved_ref, x3_ref, buffer_ref, grad16_ref, normed16_ref, sems) = rest[: sz.bands], rest[sz.bands :]
    copies = Copies(sems)
    weights = Weights(copies, head_ref, weights_hbm, buffer_ref, layer)
    saved = copies.start(saved_hbm, saved_ref)
    halo = layer + 1
    rows = sz.rows + 2 * halo
    masks = Masks(sz, limits_ref)
    conv_grad = ConvGrad(sz, layer, masks, member_ref, moments_ref, gathered_ref, norm_ref)
    below = layer - 1
    mean, inverse = split_rows(moments_below_ref[...], sz.channels)
    gain = 0.5 * norm_ref[below, 0:1, :]
    shift = 0.5 * norm_ref[below, 1:2, :]
    stats = Stats(sz)
    outs = []

    def prepare(row):
        value = conv_grad.row(row - halo, grad_ref[line(sz, row), :], normed_ref[line(sz, row), :].astype(F32))
        put_shifted(sz, masks, x3_ref, row, value, True)

    def work(first, last):
        conv_rows(sz, x3_ref, weights, below_ref, last, True)
        if first == 0:
            wait(saved)
        for row in range(first, last):
            normed = (saved_ref[line(sz, row), :] - mean) * inverse
            normed_below_ref[line(sz, row), :] = normed.astype(BF16)
            _, slope = silu_parts(normed * gain + shift)
            own = row - (halo - 1)
            grad = below_ref[line(sz, row), :] * slope * tiled(sz, masks.valid(own))
            below_ref[line(sz, row), :] = grad
            if 0 <= own < sz.rows:
                grad16_ref[line(sz, own), :] = grad.astype(BF16)
                normed16_ref[line(sz, own), :] = normed.astype(BF16)
                stats.add(grad, grad * normed)

    for row in range(rows):
        prepare(row)
    work(0, rows - 2)
    outs += send_shares(sz, copies, grad16_ref, shares, 0)
    outs += send_shares(sz, copies, normed16_ref, shares, sz.pixels)
    put_stats(sz, stats.first, stats.second, stats_ref)
    totals_ref[...] = all_sums(gathered_ref)
    wait(*outs)


def kernel_last(sz, limits_ref, member_ref, gathered_ref, grad_ref, normed_ref, moments_ref, norm_ref, head_ref,
                weights_hbm, *rest):
    parts, (out_hbm, totals_ref, pooled_hbm, x3_ref, buffer_ref, acc_ref, out_ref, sems) = (
        rest[: sz.bands], rest[sz.bands :]
    )
    copies = Copies(sems)
    weights = Weights(copies, head_ref, weights_hbm, buffer_ref, 0)
    lines = sz.pixels // 4
    outs = []
    for n, ref in enumerate(parts):
        target = line_share(pooled_hbm, (lax.axis_index("rows") ^ n) * lines, lines, lines)
        outs.append(copies.start(ref.at[pl.ds(0, lines)], target))
    totals_ref[...] = all_sums(gathered_ref)
    masks = Masks(sz, limits_ref)
    conv_grad = ConvGrad(sz, 0, masks, member_ref, moments_ref, gathered_ref, norm_ref)

    def prepare(row):
        value = conv_grad.row(row - 1, grad_ref[line(sz, row), :], normed_ref[line(sz, row), :].astype(F32))
        put_shifted(sz, masks, x3_ref, row, value, True)

    def work(first, last):
        conv_rows(sz, x3_ref, weights, acc_ref, last, True)
        pixels = slice(first * sz.width, last * sz.width)
        out_ref[pixels, :] = acc_ref[pixels, :].astype(BF16)

    for row in range(sz.rows + 2):
        prepare(row)
    work(0, sz.rows)
    outs.append(copies.start(out_ref, out_hbm))
    wait(*outs)


def kernel_weight_grad(sz, layer, first, limits_ref, member_ref, gathered_ref, moments_ref, norm_ref, *rest):
    w, q, c, bands = sz.width, sz.quarter, sz.channels, sz.bands
    pixels = sz.height * w
    given, rest = rest[:bands], rest[bands:]
    acts, rest = rest[:bands], rest[bands:]
    keep_hbm, send_hbm, grad_ref, normed_ref, act_ref, x9_ref, term_ref, *spaces, sems = rest
    keep_ref, send_ref = spaces or (keep_hbm, send_hbm)
    copies = Copies(sems)
    inputs = []
    for n in range(bands):
        start = (lax.axis_index("rows") ^ n) * sz.pixels
        for source, target, top in ((given[n], grad_ref, first[0]), (given[n], normed_ref, first[1])):
            inputs.append(
                copies.start(source.at[pl.ds(top, sz.pixels)], line_share(target, start, sz.pixels, sz.pixels))
            )
    act_loads = [
        copies.start(
            acts[n], line_share(act_ref, (lax.axis_index("rows") ^ n) * sz.pixels, sz.pixels, sz.pixels)
        )
        for n in range(bands)
    ]
    band = lax.axis_index("rows")
    own = lax.axis_index("maps")
    tile = own_sums(gathered_ref, member_ref)
    one, two, inverse, gain = (jnp.zeros((1, q), F32) for _ in range(4))
    for b in range(bands):
        here = band == b
        one = jnp.where(here, tile[b : b + 1, :], one)
        two = jnp.where(here, tile[b + 4 : b + 5, :], two)
        inverse = jnp.where(here, moments_ref[b + 4 : b + 5, :], inverse)
        gain = jnp.where(here, norm_ref[layer, 0:1, b * q : (b + 1) * q], gain)
    wait(*inputs)
    masks = Masks(sz, limits_ref)
    blank = jnp.zeros((w, q), BF16)
    for row in range(sz.height):
        value = grad_ref[line(sz, row), :].astype(F32) - one - normed_ref[line(sz, row), :].astype(F32) * two
        value = (gain * inverse) * value * masks.valid_of_map(row)
        for j, piece in enumerate((shifted_left(sz, masks, value), value, shifted_right(sz, masks, value))):
            piece = piece.astype(BF16)
            for i in range(3):
                if 0 <= row + i - 1 < sz.height:
                    x9_ref[line(sz, row + i - 1), (3 * i + j) * q : (3 * i + j + 1) * q] = piece
    for j in range(3):
        x9_ref[line(sz, sz.height - 1), j * q : (j + 1) * q] = blank
        x9_ref[line(sz, 0), (6 + j) * q : (7 + j) * q] = blank
    share = c // sz.maps
    wait(*act_loads)
    term = lax.dot_general(
        act_ref[...], x9_ref[...], (((0,), (0,)), ((), ())), preferred_element_type=F32
    )
    term_ref[...] = term
    if layer == 0:
        others = [2 * place + (own & 1) for place in range(sz.maps // 2)]
        order = others + [other ^ 1 for other in others]
    else:
        order = [own ^ relative for relative in halving_order(sz.maps)]
    for position, other in enumerate(order):
        lines = pl.ds(pl.multiple_of(other * share, share), share)
        for tap in range(9):
            place = slice(tap * share, (tap + 1) * share)
            part = term_ref[lines, tap * q : (tap + 1) * q]
            if position < sz.maps // 2:
                keep_ref[position, place, :] = part
            else:
                send_ref[position - sz.maps // 2, place, :] = part.astype(BF16)
    if spaces:
        wait(copies.start(keep_ref, keep_hbm), copies.start(send_ref, send_hbm))


def halving_order(maps):
    bits = maps.bit_length() - 1
    return [sum(((place >> (bits - 1 - k)) & 1) << k for k in range(bits)) for place in range(maps)]


def kernel_add(keep_hbm, received_ref, out_ref, keep_ref, sems):
    copies = Copies(sems)
    loads = [copies.start(keep_hbm.at[k], keep_ref.at[k]) for k in range(keep_ref.shape[0])]
    for k, load in enumerate(loads):
        wait(load)
        out_ref[k] = (keep_ref[k] + received_ref[k].astype(F32)).astype(BF16)


def kernel_halve(keep_hbm, received_ref, next_keep_hbm, next_send_hbm, keep_ref, send_ref, sems):
    half = next_keep_hbm.shape[0]
    copies = Copies(sems)
    loads = [copies.start(keep_hbm.at[part], keep_ref.at[part]) for part in (pl.ds(half, half), pl.ds(0, half))]
    wait(loads[0])
    send_ref[...] = (keep_ref[half:] + received_ref[half:].astype(F32)).astype(BF16)
    first = copies.start(send_ref, next_send_hbm)
    wait(loads[1])
    keep_ref[:half] += received_ref[:half].astype(F32)
    wait(first, copies.start(keep_ref.at[pl.ds(0, half)], next_keep_hbm))


def kernel_squares(sz, received_ref, keep1_hbm, last1_hbm, keep2_hbm, last2_hbm, totals2_ref, totals1_ref,
                   totals0_ref, squares_ref, shard_ref, norm_grad_ref, keep_ref, last_ref, sems):
    copies = Copies(sems)
    loads = [
        copies.start(source.at[0], target.at[k])
        for k, pair in enumerate(((keep1_hbm, last1_hbm), (keep2_hbm, last2_hbm)))
        for source, target in zip(pair, (keep_ref, last_ref))
    ]
    for layer, ref in enumerate((totals0_ref, totals1_ref, totals2_ref)):
        shift_row, gain_row = split_rows(ref[...], sz.channels)
        norm_grad_ref[layer, 0:1, :] = gain_row
        norm_grad_ref[layer, 1:2, :] = shift_row
    value = received_ref[0].astype(F32)
    for m in range(1, received_ref.shape[0]):
        value = value + received_ref[m].astype(F32)
    shard_ref[0] = value
    total = jnp.sum(value * value, axis=0, keepdims=True)
    wait(*loads)
    for layer in (1, 2):
        value = keep_ref[layer - 1] + last_ref[layer - 1].astype(F32)
        shard_ref[layer] = value
        total = total + jnp.sum(value * value, axis=0, keepdims=True)
    squares_ref[...] = jnp.broadcast_to(total[None], squares_ref.shape)


def kernel_adam(sz, rate, every_ref, step_ref, shard_ref, master_hbm, first_hbm, second_hbm, norm_grad_ref, norm_ref,
                norm_first_ref, norm_second_ref, total_hbm, first_out_hbm, second_out_hbm, master_out_hbm,
                norm_first_hbm, norm_second_hbm, norm_hbm,
                total_ref, master_ref, first_ref, second_ref, small_ref, sems):
    copies = Copies(sems)
    loads = [
        [
            copies.start(source.at[layer], target.at[layer])
            for source, target in ((master_hbm, master_ref), (first_hbm, first_ref), (second_hbm, second_ref))
        ]
        for layer in range(3)
    ]
    norm_grad = norm_grad_ref[...]
    square = jnp.sum(jnp.sum(every_ref[...], axis=0)) + jnp.sum(norm_grad * norm_grad)
    total = jnp.sqrt(jnp.full((1, 128), square, F32))
    total_ref[...] = total
    outs = [copies.start(total_ref, total_hbm)]
    scale = jnp.minimum(1.0, clip_limit / total)
    count = jnp.full((1, 128), step_ref[0].astype(F32), F32)
    first_fix = 1.0 - jnp.exp(count * math.log(first_decay))
    second_fix = 1.0 - jnp.exp(count * math.log(second_decay))
    for layer in range(3):
        wait(*loads[layer])
        first_ref[layer], second_ref[layer], master_ref[layer] = adam(
            master_ref[layer], shard_ref[layer], first_ref[layer], second_ref[layer], rate, weight_decay,
            scale, first_fix, second_fix,
        )
        for source, target in (
            (first_ref, first_out_hbm), (second_ref, second_out_hbm), (master_ref, master_out_hbm)
        ):
            outs.append(copies.start(source.at[layer], target.at[layer]))
    wide = [jnp.concatenate([v] * (sz.channels // 128), axis=1) for v in (scale, first_fix, second_fix)]
    for layer in range(3):
        small_ref[0, layer], small_ref[1, layer], small_ref[2, layer] = adam(
            norm_ref[layer], norm_grad[layer], norm_first_ref[layer], norm_second_ref[layer], norm_rate, 0.0, *wide
        )
    for k, target in enumerate((norm_first_hbm, norm_second_hbm, norm_hbm)):
        outs.append(copies.start(small_ref.at[k], target))
    wait(*outs)


def adam(param, grad, first, second, rate, decay, scale, first_fix, second_fix):
    clipped = scale * grad
    first_new = first_decay * first + (1.0 - first_decay) * clipped
    second_new = second_decay * second + (1.0 - second_decay) * clipped * clipped
    update = first_new / first_fix / (jnp.sqrt(second_new / second_fix) + adam_epsilon)
    return first_new, second_new, param - rate * (update + decay * param)


def call(kernel, name, outs, ins, scratch=(), flops=0, moved=0, hbm_ins=(), hbm_outs=(), smem_ins=(), sems=1):
    spaces_in = [
        pltpu.SMEM if k in smem_ins else pltpu.HBM if k in hbm_ins else pltpu.VMEM for k in range(len(ins))
    ]
    spaces_out = [pltpu.HBM if k in hbm_outs else pltpu.VMEM for k in range(len(outs))]
    return pl.pallas_call(
        kernel,
        out_shape=tuple(space(out.shape, out.dtype) for space, out in zip(spaces_out, outs)),
        in_specs=[spec(space) for space in spaces_in],
        out_specs=tuple(spec(space) for space in spaces_out),
        scratch_shapes=list(scratch) + [pltpu.SemaphoreType.DMA((sems,))],
        compiler_params=params(SPACE),
        cost_estimate=pl.CostEstimate(flops=flops, bytes_accessed=moved, transcendentals=0),
        name=name,
    )(*[v if k in smem_ins else pltpu.with_memory_space_constraint(v, spaces_in[k]) for k, v in enumerate(ins)])


def local(sz, block_input, conv_weights, norm_params, pool_index, task_mask, map_kind, map_domain, out_grad, step,
          conv_master, conv_moment1, conv_moment2, norm_moment1, norm_moment2):
    w, c, q = sz.width, sz.channels, sz.quarter
    half = w // 2
    n_maps, bands = sz.maps, sz.bands
    x = block_input.reshape(sz.pixels, c)
    index = pool_index.reshape(sz.pixels // 4, c)
    norms, norm_first, norm_second = (v.transpose(1, 0, 2) for v in (norm_params, norm_moment1, norm_moment2))
    edge = HALO * w
    lines = sz.pixels // 4

    def shape(dims, dtype):
        return jax.ShapeDtypeStruct(dims, dtype)

    def pixel_shape(rows, dtype):
        return shape((rows * w, c), dtype)

    def pixel_space(rows, dtype, times=1):
        return pltpu.VMEM((rows * w, times * c), dtype)

    def share_shapes(count):
        return [shape((count, q), BF16)] * bands

    stats_shape = shape((sz.devices, 8, c // 4), F32)
    tile_shape = shape((8, c // 4), F32)
    weight_space = pltpu.VMEM((9 - HEAD, c, c), BF16)


    def conv_flops(rows):
        return rows * w * 9 * c * c * 2

    def spread(stats):
        return lax.all_to_all(stats, AXES, 0, 0, tiled=True)

    def trade(shares):
        return [shares[0]] + [
            lax.ppermute(shares[n], "rows", [(i, i ^ n) for i in range(bands)]) for n in range(1, bands)
        ]

    def swap(act, n):
        return lax.ppermute(act, "rows", [(i, i ^ n) for i in range(bands)])

    tie = lax.optimization_barrier

    to_near, to_far, own_x = call(
        functools.partial(kernel_edges, sz), "edges",
        [shape((edge + 2 * half, c), BF16)] * 2 + [pixel_shape(sz.rows, BF16)], [x, index],
        [pltpu.VMEM((2, 2 * half, c), jnp.int32)], hbm_ins=(0, 1), sems=5,
    )
    far = lax.ppermute(to_far, "rows", [(i + 1 - k, i + k) for i in range(1, bands - 1, 2) for k in (0, 1)])
    near = swap(to_near, 1)

    limits, member = call(
        functools.partial(kernel_places, sz), "places", [shape((8, 128), jnp.int32), stats_shape],
        [map_kind, map_domain], smem_ins=(0, 1),
    )
    labelled = (out_grad * task_mask[..., None].astype(BF16)).reshape(sz.height // 2 * half, q)
    labelled = jnp.pad(labelled, ((2 * half, 2 * half), (0, 0)))
    consts = [limits, member]

    rows = sz.rows + 2 * HALO
    stats, conv, kept = call(
        functools.partial(kernel_first, sz), "first",
        [stats_shape, pixel_shape(rows - 2, F32), pixel_shape(sz.rows, BF16)], [limits, near, own_x, far, conv_weights[0, :HEAD], conv_weights],
        [pixel_space(rows, BF16, 3), weight_space], conv_flops(rows - 2), hbm_ins=(5,), hbm_outs=(2,), sems=4,
    )
    def head(layer, weights):
        return weights[layer, :HEAD]

    cot_lines = (sz.rows // 2 + 4) * half
    cots = call(functools.partial(kernel_spans, sz), "spans", share_shapes(cot_lines), [labelled], hbm_outs=range(bands), sems=bands)
    stats, weights, *cots = tie((stats, conv_weights, *cots))
    gathered = spread(stats)
    cots = trade(cots)
    acts = [[kept, swap(kept, 1), swap(kept, 2)]]
    moments = []
    saves = []
    for layer in (1, 2):
        rows = sz.rows + 2 * (HALO - layer)
        outs = [
            stats_shape, pixel_shape(rows - 2, F32), tile_shape, pixel_shape(sz.rows, BF16),
            pixel_shape(sz.rows + 2 * layer, F32),
        ]
        scratch = [pixel_space(rows, BF16, 3), weight_space]
        stats, conv, moment, act, saved = call(
            functools.partial(kernel_forward, sz, layer), "forward", outs,
            consts + [gathered, conv, norms, head(layer, weights), conv_weights], scratch,
            conv_flops(rows - 2), hbm_ins=(6,), hbm_outs=(3, 4), sems=5,
        )
        moments.append(moment)
        saves.append(saved)
        if layer == 1:
            stats, weights, *acts[0] = tie((stats, conv_weights, *acts[0]))
            gathered = spread(stats)
        else:
            stats, *rest = tie((stats, *cots, *acts[1]))
            cots, acts[1] = rest[:bands], rest[bands:]
            gathered = spread(stats)
        acts[layer - 1].append(swap(acts[layer - 1][2], 1))
        acts.append([act, swap(act, 1), swap(act, 2)])

    rows = sz.rows + 2 * (HALO - 3)
    stats, grad, normed, moment, *shares = call(
        functools.partial(kernel_pool, sz), "pool",
        [stats_shape, pixel_shape(rows, F32), pixel_shape(rows, BF16), tile_shape]
        + share_shapes(lines + 2 * sz.pixels),
        consts + [gathered, conv, norms, index, near, far] + cots,
        [
            pltpu.VMEM((lines, c), jnp.int32), pltpu.VMEM((2 * half, c), BF16), pltpu.VMEM((2 * half, c), BF16),
            pltpu.VMEM((cot_lines, c), BF16),
            pltpu.VMEM((c // 128, (rows + 2) * w, 128), F32), pltpu.VMEM((c // 128, sz.pixels, 128), F32),
            pltpu.VMEM((lines, c), BF16), pixel_space(sz.rows, BF16), pixel_space(sz.rows, BF16),
        ],
        conv_flops(4), hbm_ins=range(5, 8 + bands), hbm_outs=range(4, 4 + bands), sems=3 + 4 * bands,
    )
    moments.append(moment)
    stats, weights, acts[0][3], *acts[2] = tie((stats, conv_weights, acts[0][3], *acts[2]))
    gathered = spread(stats)
    exchanged = trade(shares)
    acts[2].append(swap(acts[2][2], 1))
    pooled_parts = exchanged

    totals = [None, None, None]
    share = 9 * (c // n_maps)
    steps = n_maps.bit_length() - 1

    def part_shape(parts, dtype):
        return shape((parts, share, q), dtype)

    def part_space(parts, dtype):
        return pltpu.VMEM((parts, share, q), dtype)

    def weight_grad(layer, gathered, given, first):
        scratch = [
            pltpu.VMEM((sz.height * w, q), BF16),
            pltpu.VMEM((sz.height * w, q), BF16),
            pltpu.VMEM((sz.height * w, c), BF16),
            pltpu.VMEM((sz.height * w, 9 * q), BF16),
        ]
        outs = [part_shape(n_maps // 2, dtype) for dtype in (F32, BF16)]
        scratch.append(pltpu.VMEM((c, 9 * q), F32))
        if layer > 0:
            scratch += [part_space(n_maps // 2, dtype) for dtype in (F32, BF16)]
        return call(
            functools.partial(kernel_weight_grad, sz, layer, first), "weight_grad", outs,
            consts + [gathered, moments[layer], norms] + given + acts[layer], scratch, conv_flops(sz.rows),
            hbm_ins=range(5, 5 + 2 * bands), hbm_outs=() if layer == 0 else (0, 1), sems=3 * bands + 2,
        )

    def step_of(send, k):
        return lax.ppermute(send, "maps", [(m, m ^ (1 << k)) for m in range(n_maps)])

    def halved(keep, received):
        size = keep.shape[0] // 2
        return call(
            kernel_halve, "halve", [part_shape(size, dtype) for dtype in (F32, BF16)], [keep, received],
            [part_space(2 * size, F32), part_space(size, BF16)],
            hbm_ins=(0,), hbm_outs=(0, 1), sems=4,
        )

    def halve(keep, received, k):
        while k < steps - 1:
            k += 1
            keep, send = halved(keep, received)
            received = step_of(send, k)
        return keep, received

    shards = [None, None, None]
    for layer in (2, 1):
        halo = layer + 1
        rows = sz.rows + 2 * halo
        received, gathered_here = exchanged, gathered
        stats, grad, normed, totals[layer], *shares = call(
            functools.partial(kernel_backward, sz, layer), "backward",
            [stats_shape, pixel_shape(rows - 2, F32), pixel_shape(rows - 2, BF16), tile_shape]
            + share_shapes(2 * sz.pixels),
            consts + [
                gathered, grad, normed, moments[layer], norms, head(layer, weights), conv_weights, saves[layer - 1],
                moments[layer - 1],
            ],
            [
                pixel_space(rows - 2, F32), pixel_space(rows, BF16, 3), weight_space, pixel_space(sz.rows, BF16),
                pixel_space(sz.rows, BF16),
            ],
            conv_flops(rows - 2), hbm_ins=(8, 9), hbm_outs=range(4, 4 + bands), sems=4 + 2 * bands,
        )
        if layer == 2:
            stats, weights, acts[1][3], acts[2][3], *received = tie(
                (stats, conv_weights, acts[1][3], acts[2][3], *received)
            )
            gathered = spread(stats)
            exchanged = trade(shares)
            keep2, send2 = weight_grad(2, gathered_here, received, (lines, lines + sz.pixels))
            gathered, send2 = tie((gathered, send2))
            arrived2 = step_of(send2, 0)
        else:
            stats, weights, *received = tie((stats, conv_weights, *received))
            gathered = spread(stats)
            exchanged = trade(shares)
            keep1, send1 = weight_grad(1, gathered_here, received, (0, sz.pixels))
            gathered, send1, arrived2 = tie((gathered, send1, arrived2))
            arrived1 = step_of(send1, 0)
            keep2, send2 = halved(keep2, arrived2)

    arrived2 = step_of(send2, 1)
    keep0, send0 = weight_grad(0, gathered, exchanged, (0, sz.pixels))
    send0, arrived2 = tie((send0, arrived2))
    arrived0 = step_of(send0, 0)
    keep1, send1 = halved(keep1, arrived1)
    keep2, send2 = halved(keep2, arrived2)
    arrived1 = step_of(send1, 1)
    arrived2 = step_of(send2, 2)
    arrived0, arrived1, arrived2 = tie((arrived0, arrived1, arrived2))
    half_maps = n_maps // 2
    (partial,) = call(
        kernel_add, "add", [part_shape(half_maps, BF16)], [keep0, arrived0],
        [part_space(half_maps, F32)], hbm_ins=(0,), sems=half_maps,
    )
    alike = [[m for m in range(n_maps) if m & 1 == bit] for bit in (0, 1)]
    received = lax.all_to_all(partial, "maps", 0, 0, tiled=True, axis_index_groups=alike)
    shards[2] = halve(keep2, arrived2, 2)
    shards[1] = halve(keep1, arrived1, 1)
    input_grad, totals[0], pooled = call(
        functools.partial(kernel_last, sz), "last",
        [pixel_shape(sz.rows, BF16), tile_shape, shape((sz.height // 2 * half, q), BF16)],
        consts + [gathered, grad, normed, moments[0], norms, head(0, weights), conv_weights] + pooled_parts,
        [pixel_space(sz.rows + 2, BF16, 3), weight_space, pixel_space(sz.rows, F32), pixel_space(sz.rows, BF16)],
        conv_flops(sz.rows), hbm_ins=range(8, 9 + bands), hbm_outs=(0, 2), sems=4 + bands,
    )

    norm_shape = shape((3, 2, c), F32)
    squares, shard, norm_grad = call(
        functools.partial(kernel_squares, sz), "squares",
        [shape((sz.devices, 1, q), F32), part_shape(3, F32), norm_shape],
        [received, *shards[1], *shards[2], totals[2], totals[1], totals[0]],
        [part_space(2, F32), part_space(2, BF16)], hbm_ins=range(1, 5), sems=4,
    )
    every = lax.all_to_all(squares, AXES, 0, 0, tiled=True)
    rate = 2.0 / math.sqrt(9.0 * c)
    total, conv_first, conv_second, conv_new, norm_first, norm_second, norm_new = call(
        functools.partial(kernel_adam, sz, rate), "adam",
        [shape((1, 128), F32)] + [part_shape(3, F32)] * 3 + [norm_shape] * 3,
        [every, step, shard]
        + [v.reshape(3, share, q) for v in (conv_master, conv_moment1, conv_moment2)]
        + [norm_grad, norms, norm_first, norm_second],
        [pltpu.VMEM((1, 128), F32)] + [part_space(3, F32)] * 3 + [pltpu.VMEM((3, 3, 2, c), F32)],
        hbm_ins=(3, 4, 5), hbm_outs=range(7), smem_ins=(1,), sems=22,
    )
    return (
        pooled.reshape(1, sz.height // 2, half, q),
        input_grad.reshape(block_input.shape),
        total[0, :1],
        conv_first.reshape(conv_master.shape),
        conv_second.reshape(conv_master.shape),
        conv_new.reshape(conv_master.shape),
        norm_first.transpose(1, 0, 2),
        norm_second.transpose(1, 0, 2),
        norm_new.transpose(1, 0, 2),
    )


def solution(mesh):
    def run(*args):
        bands = mesh.shape["rows"]
        maps = mesh.shape["maps"]
        shape = args[0].shape
        sz = Sizes(maps, bands, shape[1] // bands, shape[2], shape[3])
        return jax.shard_map(
            functools.partial(local, sz),
            mesh=mesh,
            in_specs=(
                P("maps", "rows", None, None),
                P(),
                P(),
                P("maps", "rows", None, None),
                P("maps", None, None),
                P(),
                P(),
                P("maps", None, None, "rows"),
                P(),
                P(None, None, "maps", "rows"),
                P(None, None, "maps", "rows"),
                P(None, None, "maps", "rows"),
                P(),
                P(),
            ),
            out_specs=(
                P("maps", None, None, "rows"),
                P("maps", "rows", None, None),
                P(),
                P(None, None, "maps", "rows"),
                P(None, None, "maps", "rows"),
                P(None, None, "maps", "rows"),
                P(),
                P(),
                P(),
            ),
            check_vma=False,
        )(*args)

    return run
```

```python
import functools
import math

import jax
import jax.numpy as jnp
from jax import lax
from jax.experimental import pallas as pl
from jax.experimental.pallas import tpu as pltpu
from jax.sharding import PartitionSpec as P

DOMAINS = 4
norm_epsilon = 1e-05
clip_limit = 1.0
first_decay = 0.9
second_decay = 0.999
adam_epsilon = 1e-08
norm_rate = 0.5
weight_decay = 0.01

HALO = 6
SPACE = 28
AXES = ("maps", "rows")
F32 = jnp.float32
BF16 = jnp.bfloat16


class Sizes:
    def __init__(self, maps, bands, rows, width, channels):
        self.maps = maps
        self.bands = bands
        self.devices = maps * bands
        self.rows = rows
        self.width = width
        self.channels = channels
        self.height = rows * bands
        self.short_height = 2 * (self.height * 7 // 16)
        self.short_width = 2 * (width * 13 // 32)
        self.pixels = rows * width
        self.quarter = channels // bands


def spec(space):
    return pl.BlockSpec(memory_space=space)


def params(megabytes):
    return pltpu.CompilerParams(vmem_limit_bytes=megabytes << 20)


class Copies:
    def __init__(self, sems):
        self.sems = sems
        self.used = 0

    def start(self, source, target):
        copy = pltpu.make_async_copy(source, target, self.sems.at[self.used])
        self.used += 1
        copy.start()
        return copy


def wait(*copies):
    for copy in copies:
        copy.wait()


def line_share(ref, start, step, size):
    return ref.at[pl.ds(pl.multiple_of(start, step), size)]


def own_sums(gathered_ref, weights_ref):
    return jnp.sum(gathered_ref[...] * weights_ref[...], axis=0)


def all_sums(gathered_ref):
    return jnp.sum(gathered_ref[...], axis=0)


def split_rows(tile, channels):
    first = jnp.concatenate([tile[k : k + 1, :] for k in range(4)], axis=1)
    second = jnp.concatenate([tile[k : k + 1, :] for k in range(4, 8)], axis=1)
    return first, second


def join_rows(first, second):
    lanes = first.shape[1] // 4
    return jnp.concatenate(
        [row[:, k * lanes : (k + 1) * lanes] for row in (first, second) for k in range(4)], axis=0
    )


def tiled(sz, value):
    return jnp.concatenate([value] * (sz.channels // value.shape[1]), axis=1)


class Masks:
    def __init__(self, sz, limits_ref):
        self.col = lax.broadcasted_iota(jnp.int32, (sz.width, 128), 0)
        self.wide = jnp.where(self.col < limits_ref[2:3, :], 1.0, 0.0)
        self.inner_left = jnp.where(self.col > 0, 1.0, 0.0)
        self.inner_right = jnp.where(self.col < sz.width - 1, 1.0, 0.0)
        self.limits_ref = limits_ref

    def valid(self, row):
        inside = (self.limits_ref[0:1, :] <= row) & (self.limits_ref[1:2, :] > row)
        return self.wide * jnp.where(inside, 1.0, 0.0)

    def valid_of_map(self, row):
        return self.wide * jnp.where(self.limits_ref[3:4, :] > row, 1.0, 0.0)


def line(sz, row):
    return slice(row * sz.width, (row + 1) * sz.width)


def shifted_right(sz, masks, value):
    mask = masks.inner_left
    return pltpu.roll(value, 1, 0) * (mask if value.shape[1] == 128 else tiled(sz, mask))


def shifted_left(sz, masks, value):
    mask = masks.inner_right
    return pltpu.roll(value, sz.width - 1, 0) * (mask if value.shape[1] == 128 else tiled(sz, mask))


def put_shifted(sz, masks, x3_ref, row, value, reverse=False):
    before = shifted_right(sz, masks, value)
    after = shifted_left(sz, masks, value)
    if reverse:
        before, after = after, before
    c = sz.channels
    x3_ref[line(sz, row), 0:c] = before.astype(BF16)
    x3_ref[line(sz, row), c : 2 * c] = value.astype(BF16)
    x3_ref[line(sz, row), 2 * c : 3 * c] = after.astype(BF16)


def fold(value):
    total = value[0:8, :]
    for k in range(1, value.shape[0] // 8):
        total = total + value[8 * k : 8 * (k + 1), :]
    return total


HEAD = 1


class Weights:
    def __init__(self, copies, head_ref, weights_hbm, buffer_ref, layer):
        self.head_ref, self.buffer_ref = head_ref, buffer_ref
        self.loads = {
            first: copies.start(
                weights_hbm.at[layer, pl.ds(first, 3 - first % 3)],
                buffer_ref.at[pl.ds(first - HEAD, 3 - first % 3)],
            )
            for first in (HEAD, 3, 6)
        }

    def wait(self, tap):
        if tap in self.loads:
            wait(self.loads[tap])

    def taps(self, first, last):
        if first < HEAD:
            part = self.head_ref[first:last]
        else:
            part = self.buffer_ref[first - HEAD : last - HEAD]
        return part.reshape(-1, part.shape[-1])


def conv_rows(sz, x3_ref, weights, out_ref, rows, reverse=False):
    c, w = sz.channels, sz.width
    n = rows * w
    spans = [(0, HEAD), (HEAD, 3), (3, 6), (6, 9)]
    if reverse:
        spans = [(tap, tap + 1) for tap in range(9)]
    for first, last in spans:
        weights.wait(first)
        i = first // 3
        start = (2 - i if reverse else i) * w
        lhs = x3_ref[start : start + n, (first - 3 * i) * c : (last - 3 * i) * c]
        across = 1 if reverse else 0
        term = lax.dot_general(
            lhs, weights.taps(first, last), (((1,), (across,)), ((), ())), preferred_element_type=F32
        )
        if first == 0:
            out_ref[...] = term
        else:
            out_ref[...] += term


def put_stats(sz, first, second, out_ref):
    tile = join_rows(jnp.sum(first, axis=0, keepdims=True), jnp.sum(second, axis=0, keepdims=True))
    out_ref[...] = jnp.broadcast_to(tile[None], out_ref.shape)


def silu_parts(half):
    t = jnp.tanh(half)
    product = half * t
    return half + product, (0.5 + 0.5 * t) * (1.0 + (half - product))


class Stats:
    def __init__(self, sz):
        self.first = jnp.zeros((8, sz.channels), F32)
        self.second = jnp.zeros((8, sz.channels), F32)

    def add(self, first, second):
        self.first = self.first + fold(first)
        self.second = self.second + fold(second)


def add_conv_rows(sz, masks, stats, conv_ref, skip, first, last):
    for row in range(max(first, skip), min(last, skip + sz.rows)):
        value = conv_ref[line(sz, row), :]
        masked = value * tiled(sz, masks.valid(row - skip))
        stats.add(masked, masked * value)


def band_lanes(sz, n):
    return pl.ds(pl.multiple_of((lax.axis_index("rows") ^ n) * sz.quarter, sz.quarter), sz.quarter)


def send_shares(sz, copies, source_ref, targets, first):
    lines = source_ref.shape[0]
    return [
        copies.start(source_ref.at[:, band_lanes(sz, n)], target.at[pl.ds(first, lines)])
        for n, target in enumerate(targets)
    ]


def kernel_spans(sz, given_ref, *rest):
    shares, sems = rest[: sz.bands], rest[sz.bands]
    copies = Copies(sems)
    span = sz.rows // 2 * (sz.width // 2)
    wait(*[
        copies.start(line_share(given_ref, (lax.axis_index("rows") ^ n) * span, span, share.shape[0]), share)
        for n, share in enumerate(shares)
    ])


def kernel_edges(sz, x_hbm, index_hbm, near_ref, far_ref, x_ref, index_ref, sems):
    copies = Copies(sems)
    edge = HALO * sz.width
    few = sz.width
    odd = lax.axis_index("rows") % 2
    last = index_hbm.shape[0] - few
    loads = []
    rest = []
    for k, (first, target) in enumerate(((1 - odd, near_ref), (odd, far_ref))):
        loads.append(copies.start(line_share(index_hbm, first * last, few, few), index_ref.at[k]))
        rest.append(copies.start(line_share(x_hbm, first * (sz.pixels - edge), edge, edge), target.at[pl.ds(0, edge)]))
    rest.append(copies.start(x_hbm, x_ref))
    wait(*loads)
    near_ref[edge : edge + few, :] = index_ref[0].astype(BF16)
    far_ref[edge : edge + few, :] = index_ref[1].astype(BF16)
    wait(*rest)


def kernel_places(sz, kind_ref, domain_ref, limits_ref, member_ref, _):
    m, r = lax.axis_index("maps"), lax.axis_index("rows")
    start = r * sz.rows

    def rows_of(k):
        return jnp.where(kind_ref[k] == 1, sz.height, sz.short_height)

    def cols_of(k):
        return jnp.where(kind_ref[k] == 1, sz.short_width, sz.width)

    own = domain_ref[m]
    area = jnp.int32(0)
    for k in range(sz.maps):
        area = area + jnp.where(domain_ref[k] == own, rows_of(k) * cols_of(k), 0)
    tile = member_ref.shape[1:]
    weight = 1.0 / jnp.full(tile, area.astype(F32))
    for k in range(sz.maps):
        value = jnp.where(domain_ref[k] == own, weight, 0.0)
        for b in range(sz.bands):
            member_ref[k * sz.bands + b] = value
    line = lax.broadcasted_iota(jnp.int32, limits_ref.shape, 0)
    limits_ref[...] = jnp.where(
        line == 0, -start, jnp.where(line == 1, rows_of(m) - start, jnp.where(line == 2, cols_of(m), rows_of(m)))
    )


def kernel_first(sz, limits_ref, near_ref, x_ref, far_ref, head_ref, weights_hbm, stats_ref, conv_ref, act_hbm, x3_ref,
                 buffer_ref, sems):
    copies = Copies(sems)
    weights = Weights(copies, head_ref, weights_hbm, buffer_ref, 0)
    masks = Masks(sz, limits_ref)
    stats = Stats(sz)

    odd = lax.axis_index("rows") % 2 == 1

    def prepare(row):
        if row < HALO:
            value = jnp.where(odd, near_ref[line(sz, row), :], far_ref[line(sz, row), :])
        elif row < HALO + sz.rows:
            value = x_ref[line(sz, row - HALO), :]
        else:
            below = line(sz, row - HALO - sz.rows)
            value = jnp.where(odd, far_ref[below, :], near_ref[below, :])
        put_shifted(sz, masks, x3_ref, row, value.astype(F32))

    def work(first, last):
        conv_rows(sz, x3_ref, weights, conv_ref, last)
        add_conv_rows(sz, masks, stats, conv_ref, HALO - 1, first, last)

    for row in range(sz.rows + 2 * HALO):
        prepare(row)
    work(0, sz.rows + 2 * HALO - 2)
    out = copies.start(x_ref, act_hbm)
    put_stats(sz, stats.first, stats.second, stats_ref)
    wait(out)


def norm_of(sz, gathered_ref, member_ref):
    mean, squares = split_rows(own_sums(gathered_ref, member_ref), sz.channels)
    return mean, lax.rsqrt(squares - mean * mean + norm_epsilon)


def kernel_forward(sz, layer, limits_ref, member_ref, gathered_ref, before_ref, norm_ref, head_ref, weights_hbm, *rest):
    stats_ref, conv_ref, moments_ref, act_hbm, saved_hbm, x3_ref, buffer_ref, sems = rest
    copies = Copies(sems)
    weights = Weights(copies, head_ref, weights_hbm, buffer_ref, layer)
    halo = HALO - layer
    rows = sz.rows + 2 * halo
    skip = (halo - layer) * sz.width
    outs = []
    mean, inverse = norm_of(sz, gathered_ref, member_ref)
    moments_ref[...] = join_rows(mean, inverse)
    scale = 0.5 * norm_ref[layer - 1, 0:1, :] * inverse
    offset = 0.5 * norm_ref[layer - 1, 1:2, :] - mean * scale
    masks = Masks(sz, limits_ref)
    stats = Stats(sz)
    c = sz.channels

    def prepare(row):
        value = before_ref[line(sz, row), :]
        act, _ = silu_parts(value * scale + offset)
        put_shifted(sz, masks, x3_ref, row, act * tiled(sz, masks.valid(row - halo)))
        if row == halo + sz.rows - 1:
            outs.append(copies.start(x3_ref.at[pl.ds(halo * sz.width, sz.pixels), pl.ds(c, c)], act_hbm))

    def work(first, last):
        conv_rows(sz, x3_ref, weights, conv_ref, last)
        outs.append(copies.start(before_ref.at[pl.ds(skip, saved_hbm.shape[0])], saved_hbm))
        add_conv_rows(sz, masks, stats, conv_ref, halo - 1, first, last)

    for row in range(rows):
        prepare(row)
    work(0, rows - 2)
    put_stats(sz, stats.first, stats.second, stats_ref)
    wait(*outs)


def kernel_pool(sz, limits_ref, member_ref, gathered_ref, before_ref, norm_ref, index_hbm, near_hbm, far_hbm, *rest):
    cotangents, rest = rest[: sz.bands], rest[sz.bands :]
    (stats_ref, grad_ref, normed_ref, moments_ref), rest = rest[:4], rest[4:]
    shares, rest = rest[: sz.bands], rest[sz.bands :]
    (index_ref, near_ref, far_ref, cotangent_ref, spread_ref, act_ref, pooled_ref, grad16_ref, normed16_ref, sems) = rest
    c, w = sz.channels, sz.width
    half = w // 2
    windows = sz.rows // 2
    edge = HALO * w
    copies = Copies(sems)
    inputs = [
        copies.start(index_hbm, index_ref),
        copies.start(near_hbm.at[pl.ds(edge, w)], near_ref),
        copies.start(far_hbm.at[pl.ds(edge, w)], far_ref),
    ]
    inputs += [
        copies.start(
            ref, cotangent_ref.at[:, band_lanes(sz, n)]
        )
        for n, ref in enumerate(cotangents)
    ]
    mean, inverse = norm_of(sz, gathered_ref, member_ref)
    moments_ref[...] = join_rows(mean, inverse)
    gain = 0.5 * norm_ref[2, 0:1, :]
    shift = 0.5 * norm_ref[2, 1:2, :]
    halo = HALO - 3
    rows = sz.rows + 2 * halo
    lines = sz.pixels // 4
    groups = c // 128
    masks = Masks(sz, limits_ref)
    for row in range(rows):
        normed = (before_ref[line(sz, row), :] - mean) * inverse
        normed_ref[line(sz, row), :] = normed.astype(BF16)
        act, slope = silu_parts(normed * gain + shift)
        valid = tiled(sz, masks.valid(row - halo))
        grad_ref[line(sz, row), :] = slope * valid
        if halo <= row < halo + sz.rows:
            normed16_ref[line(sz, row - halo), :] = normed.astype(BF16)
            act = act * valid
            for g in range(groups):
                act_ref[g, line(sz, row - halo), :] = act[:, g * 128 : (g + 1) * 128]
    outs = send_shares(sz, copies, normed16_ref, shares, lines + sz.pixels)
    wait(*inputs)
    for p in range(windows):
        index = index_ref[p * half : (p + 1) * half, :]
        result = jnp.zeros(index.shape, F32)
        for corner in range(4):
            start = (2 * p + corner // 2) * w + corner % 2
            taken = jnp.concatenate(
                [act_ref[g, pl.ds(start, half, stride=2), :] for g in range(groups)], axis=1
            )
            result = jnp.where(index == corner, taken, result)
        pooled_ref[p * half : (p + 1) * half, :] = result.astype(BF16)
    outs += send_shares(sz, copies, pooled_ref, shares, 0)
    odd = lax.axis_index("rows") % 2 == 1
    for p in range(windows + 4):
        if p < 2:
            place = slice(p * half, (p + 1) * half)
            index = jnp.where(odd, near_ref[place, :].astype(jnp.int32), far_ref[place, :].astype(jnp.int32))
        elif p < windows + 2:
            index = index_ref[(p - 2) * half : (p - 1) * half, :]
        else:
            place = slice((p - windows - 2) * half, (p - windows - 1) * half)
            index = jnp.where(odd, far_ref[place, :].astype(jnp.int32), near_ref[place, :].astype(jnp.int32))
        given = cotangent_ref[p * half : (p + 1) * half, :].astype(F32)
        for corner in range(4):
            start = (2 * p + corner // 2) * w + corner % 2
            placed = jnp.where(index == corner, given, 0.0)
            for g in range(groups):
                spread_ref[g, pl.ds(start, half, stride=2), :] = placed[:, g * 128 : (g + 1) * 128]
    stats = Stats(sz)
    for row in range(rows):
        upstream = jnp.concatenate([spread_ref[g, line(sz, row + 1), :] for g in range(groups)], axis=1)
        grad = upstream * grad_ref[line(sz, row), :]
        grad_ref[line(sz, row), :] = grad
        if halo <= row < halo + sz.rows:
            grad16_ref[line(sz, row - halo), :] = grad.astype(BF16)
            stats.add(grad, grad * normed_ref[line(sz, row), :].astype(F32))
    outs += send_shares(sz, copies, grad16_ref, shares, lines)
    put_stats(sz, stats.first, stats.second, stats_ref)
    wait(*outs)


class ConvGrad:
    def __init__(self, sz, layer, masks, member_ref, moments_ref, gathered_ref, norm_ref):
        self.sz, self.masks = sz, masks
        _, inverse = split_rows(moments_ref[...], sz.channels)
        one, two = split_rows(own_sums(gathered_ref, member_ref), sz.channels)
        self.scale = norm_ref[layer, 0:1, :] * inverse
        self.one, self.two = one, two

    def row(self, row, grad, normed):
        value = self.scale * (grad - self.one - normed * self.two)
        return value * tiled(self.sz, self.masks.valid(row))


def kernel_backward(sz, layer, limits_ref, member_ref, gathered_ref, grad_ref, normed_ref, moments_ref, norm_ref,
                    head_ref, weights_hbm, saved_hbm, moments_below_ref, stats_ref, below_ref, normed_below_ref, totals_ref,
                    *rest):
    shares, (saved_ref, x3_ref, buffer_ref, grad16_ref, normed16_ref, sems) = rest[: sz.bands], rest[sz.bands :]
    copies = Copies(sems)
    weights = Weights(copies, head_ref, weights_hbm, buffer_ref, layer)
    saved = copies.start(saved_hbm, saved_ref)
    halo = layer + 1
    rows = sz.rows + 2 * halo
    masks = Masks(sz, limits_ref)
    conv_grad = ConvGrad(sz, layer, masks, member_ref, moments_ref, gathered_ref, norm_ref)
    below = layer - 1
    mean, inverse = split_rows(moments_below_ref[...], sz.channels)
    gain = 0.5 * norm_ref[below, 0:1, :]
    shift = 0.5 * norm_ref[below, 1:2, :]
    stats = Stats(sz)
    outs = []

    def prepare(row):
        value = conv_grad.row(row - halo, grad_ref[line(sz, row), :], normed_ref[line(sz, row), :].astype(F32))
        put_shifted(sz, masks, x3_ref, row, value, True)

    def work(first, last):
        conv_rows(sz, x3_ref, weights, below_ref, last, True)
        if first == 0:
            wait(saved)
        for row in range(first, last):
            normed = (saved_ref[line(sz, row), :] - mean) * inverse
            normed_below_ref[line(sz, row), :] = normed.astype(BF16)
            _, slope = silu_parts(normed * gain + shift)
            own = row - (halo - 1)
            grad = below_ref[line(sz, row), :] * slope * tiled(sz, masks.valid(own))
            below_ref[line(sz, row), :] = grad
            if 0 <= own < sz.rows:
                grad16_ref[line(sz, own), :] = grad.astype(BF16)
                normed16_ref[line(sz, own), :] = normed.astype(BF16)
                stats.add(grad, grad * normed)

    for row in range(rows):
        prepare(row)
    work(0, rows - 2)
    outs += send_shares(sz, copies, grad16_ref, shares, 0)
    outs += send_shares(sz, copies, normed16_ref, shares, sz.pixels)
    put_stats(sz, stats.first, stats.second, stats_ref)
    totals_ref[...] = all_sums(gathered_ref)
    wait(*outs)


def kernel_last(sz, limits_ref, member_ref, gathered_ref, grad_ref, normed_ref, moments_ref, norm_ref, head_ref,
                weights_hbm, *rest):
    parts, (out_hbm, totals_ref, pooled_hbm, x3_ref, buffer_ref, acc_ref, out_ref, sems) = (
        rest[: sz.bands], rest[sz.bands :]
    )
    copies = Copies(sems)
    weights = Weights(copies, head_ref, weights_hbm, buffer_ref, 0)
    lines = sz.pixels // 4
    outs = []
    for n, ref in enumerate(parts):
        target = line_share(pooled_hbm, (lax.axis_index("rows") ^ n) * lines, lines, lines)
        outs.append(copies.start(ref.at[pl.ds(0, lines)], target))
    totals_ref[...] = all_sums(gathered_ref)
    masks = Masks(sz, limits_ref)
    conv_grad = ConvGrad(sz, 0, masks, member_ref, moments_ref, gathered_ref, norm_ref)

    def prepare(row):
        value = conv_grad.row(row - 1, grad_ref[line(sz, row), :], normed_ref[line(sz, row), :].astype(F32))
        put_shifted(sz, masks, x3_ref, row, value, True)

    def work(first, last):
        conv_rows(sz, x3_ref, weights, acc_ref, last, True)
        pixels = slice(first * sz.width, last * sz.width)
        out_ref[pixels, :] = acc_ref[pixels, :].astype(BF16)

    for row in range(sz.rows + 2):
        prepare(row)
    work(0, sz.rows)
    outs.append(copies.start(out_ref, out_hbm))
    wait(*outs)


def kernel_weight_grad(sz, layer, first, limits_ref, member_ref, gathered_ref, moments_ref, norm_ref, *rest):
    w, q, c, bands = sz.width, sz.quarter, sz.channels, sz.bands
    pixels = sz.height * w
    given, rest = rest[:bands], rest[bands:]
    acts, rest = rest[:bands], rest[bands:]
    keep_hbm, send_hbm, grad_ref, normed_ref, act_ref, x9_ref, term_ref, *spaces, sems = rest
    keep_ref, send_ref = spaces or (keep_hbm, send_hbm)
    copies = Copies(sems)
    inputs = []
    for n in range(bands):
        start = (lax.axis_index("rows") ^ n) * sz.pixels
        for source, target, top in ((given[n], grad_ref, first[0]), (given[n], normed_ref, first[1])):
            inputs.append(
                copies.start(source.at[pl.ds(top, sz.pixels)], line_share(target, start, sz.pixels, sz.pixels))
            )
    act_loads = [
        copies.start(
            acts[n], line_share(act_ref, (lax.axis_index("rows") ^ n) * sz.pixels, sz.pixels, sz.pixels)
        )
        for n in range(bands)
    ]
    band = lax.axis_index("rows")
    own = lax.axis_index("maps")
    tile = own_sums(gathered_ref, member_ref)
    one, two, inverse, gain = (jnp.zeros((1, q), F32) for _ in range(4))
    for b in range(bands):
        here = band == b
        one = jnp.where(here, tile[b : b + 1, :], one)
        two = jnp.where(here, tile[b + 4 : b + 5, :], two)
        inverse = jnp.where(here, moments_ref[b + 4 : b + 5, :], inverse)
        gain = jnp.where(here, norm_ref[layer, 0:1, b * q : (b + 1) * q], gain)
    wait(*inputs)
    masks = Masks(sz, limits_ref)
    blank = jnp.zeros((w, q), BF16)
    for row in range(sz.height):
        value = grad_ref[line(sz, row), :].astype(F32) - one - normed_ref[line(sz, row), :].astype(F32) * two
        value = (gain * inverse) * value * masks.valid_of_map(row)
        for j, piece in enumerate((shifted_left(sz, masks, value), value, shifted_right(sz, masks, value))):
            piece = piece.astype(BF16)
            for i in range(3):
                if 0 <= row + i - 1 < sz.height:
                    x9_ref[line(sz, row + i - 1), (3 * i + j) * q : (3 * i + j + 1) * q] = piece
    for j in range(3):
        x9_ref[line(sz, sz.height - 1), j * q : (j + 1) * q] = blank
        x9_ref[line(sz, 0), (6 + j) * q : (7 + j) * q] = blank
    share = c // sz.maps
    wait(*act_loads)
    term = lax.dot_general(
        act_ref[...], x9_ref[...], (((0,), (0,)), ((), ())), preferred_element_type=F32
    )
    term_ref[...] = term
    if layer == 0:
        others = [2 * place + (own & 1) for place in range(sz.maps // 2)]
        order = others + [other ^ 1 for other in others]
    else:
        order = [own ^ relative for relative in halving_order(sz.maps)]
    for position, other in enumerate(order):
        lines = pl.ds(pl.multiple_of(other * share, share), share)
        for tap in range(9):
            place = slice(tap * share, (tap + 1) * share)
            part = term_ref[lines, tap * q : (tap + 1) * q]
            if position < sz.maps // 2:
                keep_ref[position, place, :] = part
            else:
                send_ref[position - sz.maps // 2, place, :] = part.astype(BF16)
    if spaces:
        wait(copies.start(keep_ref, keep_hbm), copies.start(send_ref, send_hbm))


def halving_order(maps):
    bits = maps.bit_length() - 1
    return [sum(((place >> (bits - 1 - k)) & 1) << k for k in range(bits)) for place in range(maps)]


def kernel_add(keep_hbm, received_ref, out_ref, keep_ref, sems):
    copies = Copies(sems)
    loads = [copies.start(keep_hbm.at[k], keep_ref.at[k]) for k in range(keep_ref.shape[0])]
    for k, load in enumerate(loads):
        wait(load)
        out_ref[k] = (keep_ref[k] + received_ref[k].astype(F32)).astype(BF16)


def kernel_halve(keep_hbm, received_ref, next_keep_hbm, next_send_hbm, keep_ref, send_ref, sems):
    half = next_keep_hbm.shape[0]
    copies = Copies(sems)
    loads = [copies.start(keep_hbm.at[part], keep_ref.at[part]) for part in (pl.ds(half, half), pl.ds(0, half))]
    wait(loads[0])
    send_ref[...] = (keep_ref[half:] + received_ref[half:].astype(F32)).astype(BF16)
    first = copies.start(send_ref, next_send_hbm)
    wait(loads[1])
    keep_ref[:half] += received_ref[:half].astype(F32)
    wait(first, copies.start(keep_ref.at[pl.ds(0, half)], next_keep_hbm))


def kernel_squares(sz, received_ref, keep1_hbm, last1_hbm, keep2_hbm, last2_hbm, totals2_ref, totals1_ref,
                   totals0_ref, squares_ref, shard_ref, norm_grad_ref, keep_ref, last_ref, sems):
    copies = Copies(sems)
    loads = [
        copies.start(source.at[0], target.at[k])
        for k, pair in enumerate(((keep1_hbm, last1_hbm), (keep2_hbm, last2_hbm)))
        for source, target in zip(pair, (keep_ref, last_ref))
    ]
    for layer, ref in enumerate((totals0_ref, totals1_ref, totals2_ref)):
        shift_row, gain_row = split_rows(ref[...], sz.channels)
        norm_grad_ref[layer, 0:1, :] = gain_row
        norm_grad_ref[layer, 1:2, :] = shift_row
    value = received_ref[0].astype(F32)
    for m in range(1, received_ref.shape[0]):
        value = value + received_ref[m].astype(F32)
    shard_ref[0] = value
    total = jnp.sum(value * value, axis=0, keepdims=True)
    wait(*loads)
    for layer in (1, 2):
        value = keep_ref[layer - 1] + last_ref[layer - 1].astype(F32)
        shard_ref[layer] = value
        total = total + jnp.sum(value * value, axis=0, keepdims=True)
    squares_ref[...] = jnp.broadcast_to(total[None], squares_ref.shape)


def kernel_adam(sz, rate, every_ref, step_ref, shard_ref, master_hbm, first_hbm, second_hbm, norm_grad_ref, norm_ref,
                norm_first_ref, norm_second_ref, total_hbm, first_out_hbm, second_out_hbm, master_out_hbm,
                norm_first_hbm, norm_second_hbm, norm_hbm,
                total_ref, master_ref, first_ref, second_ref, small_ref, sems):
    copies = Copies(sems)
    loads = [
        [
            copies.start(source.at[layer], target.at[layer])
            for source, target in ((master_hbm, master_ref), (first_hbm, first_ref), (second_hbm, second_ref))
        ]
        for layer in range(3)
    ]
    norm_grad = norm_grad_ref[...]
    square = jnp.sum(jnp.sum(every_ref[...], axis=0)) + jnp.sum(norm_grad * norm_grad)
    total = jnp.sqrt(jnp.full((1, 128), square, F32))
    total_ref[...] = total
    outs = [copies.start(total_ref, total_hbm)]
    scale = jnp.minimum(1.0, clip_limit / total)
    count = jnp.full((1, 128), step_ref[0].astype(F32), F32)
    first_fix = 1.0 - jnp.exp(count * math.log(first_decay))
    second_fix = 1.0 - jnp.exp(count * math.log(second_decay))
    for layer in range(3):
        wait(*loads[layer])
        first_ref[layer], second_ref[layer], master_ref[layer] = adam(
            master_ref[layer], shard_ref[layer], first_ref[layer], second_ref[layer], rate, weight_decay,
            scale, first_fix, second_fix,
        )
        for source, target in (
            (first_ref, first_out_hbm), (second_ref, second_out_hbm), (master_ref, master_out_hbm)
        ):
            outs.append(copies.start(source.at[layer], target.at[layer]))
    wide = [jnp.concatenate([v] * (sz.channels // 128), axis=1) for v in (scale, first_fix, second_fix)]
    for layer in range(3):
        small_ref[0, layer], small_ref[1, layer], small_ref[2, layer] = adam(
            norm_ref[layer], norm_grad[layer], norm_first_ref[layer], norm_second_ref[layer], norm_rate, 0.0, *wide
        )
    for k, target in enumerate((norm_first_hbm, norm_second_hbm, norm_hbm)):
        outs.append(copies.start(small_ref.at[k], target))
    wait(*outs)


def adam(param, grad, first, second, rate, decay, scale, first_fix, second_fix):
    clipped = scale * grad
    first_new = first_decay * first + (1.0 - first_decay) * clipped
    second_new = second_decay * second + (1.0 - second_decay) * clipped * clipped
    update = first_new / first_fix / (jnp.sqrt(second_new / second_fix) + adam_epsilon)
    return first_new, second_new, param - rate * (update + decay * param)


def call(kernel, name, outs, ins, scratch=(), flops=0, moved=0, hbm_ins=(), hbm_outs=(), smem_ins=(), sems=1):
    spaces_in = [
        pltpu.SMEM if k in smem_ins else pltpu.HBM if k in hbm_ins else pltpu.VMEM for k in range(len(ins))
    ]
    spaces_out = [pltpu.HBM if k in hbm_outs else pltpu.VMEM for k in range(len(outs))]
    return pl.pallas_call(
        kernel,
        out_shape=tuple(space(out.shape, out.dtype) for space, out in zip(spaces_out, outs)),
        in_specs=[spec(space) for space in spaces_in],
        out_specs=tuple(spec(space) for space in spaces_out),
        scratch_shapes=list(scratch) + [pltpu.SemaphoreType.DMA((sems,))],
        compiler_params=params(SPACE),
        cost_estimate=pl.CostEstimate(flops=flops, bytes_accessed=moved, transcendentals=0),
        name=name,
    )(*[v if k in smem_ins else pltpu.with_memory_space_constraint(v, spaces_in[k]) for k, v in enumerate(ins)])


def local(sz, block_input, conv_weights, norm_params, pool_index, task_mask, map_kind, map_domain, out_grad, step,
          conv_master, conv_moment1, conv_moment2, norm_moment1, norm_moment2):
    w, c, q = sz.width, sz.channels, sz.quarter
    half = w // 2
    n_maps, bands = sz.maps, sz.bands
    x = block_input.reshape(sz.pixels, c)
    index = pool_index.reshape(sz.pixels // 4, c)
    norms, norm_first, norm_second = (v.transpose(1, 0, 2) for v in (norm_params, norm_moment1, norm_moment2))
    edge = HALO * w
    lines = sz.pixels // 4

    def shape(dims, dtype):
        return jax.ShapeDtypeStruct(dims, dtype)

    def pixel_shape(rows, dtype):
        return shape((rows * w, c), dtype)

    def pixel_space(rows, dtype, times=1):
        return pltpu.VMEM((rows * w, times * c), dtype)

    def share_shapes(count):
        return [shape((count, q), BF16)] * bands

    stats_shape = shape((sz.devices, 8, c // 4), F32)
    tile_shape = shape((8, c // 4), F32)
    weight_space = pltpu.VMEM((9 - HEAD, c, c), BF16)


    def conv_flops(rows):
        return rows * w * 9 * c * c * 2

    def spread(stats):
        return lax.all_to_all(stats, AXES, 0, 0, tiled=True)

    def trade(shares):
        return [shares[0]] + [
            lax.ppermute(shares[n], "rows", [(i, i ^ n) for i in range(bands)]) for n in range(1, bands)
        ]

    def swap(act, n):
        return lax.ppermute(act, "rows", [(i, i ^ n) for i in range(bands)])

    tie = lax.optimization_barrier

    to_near, to_far, own_x = call(
        functools.partial(kernel_edges, sz), "edges",
        [shape((edge + 2 * half, c), BF16)] * 2 + [pixel_shape(sz.rows, BF16)], [x, index],
        [pltpu.VMEM((2, 2 * half, c), jnp.int32)], hbm_ins=(0, 1), sems=5,
    )
    far = lax.ppermute(to_far, "rows", [(i + 1 - k, i + k) for i in range(1, bands - 1, 2) for k in (0, 1)])
    near = swap(to_near, 1)

    limits, member = call(
        functools.partial(kernel_places, sz), "places", [shape((8, 128), jnp.int32), stats_shape],
        [map_kind, map_domain], smem_ins=(0, 1),
    )
    labelled = (out_grad * task_mask[..., None].astype(BF16)).reshape(sz.height // 2 * half, q)
    labelled = jnp.pad(labelled, ((2 * half, 2 * half), (0, 0)))
    consts = [limits, member]

    rows = sz.rows + 2 * HALO
    stats, conv, kept = call(
        functools.partial(kernel_first, sz), "first",
        [stats_shape, pixel_shape(rows - 2, F32), pixel_shape(sz.rows, BF16)], [limits, near, own_x, far, conv_weights[0, :HEAD], conv_weights],
        [pixel_space(rows, BF16, 3), weight_space], conv_flops(rows - 2), hbm_ins=(5,), hbm_outs=(2,), sems=4,
    )
    def head(layer, weights):
        return weights[layer, :HEAD]

    cot_lines = (sz.rows // 2 + 4) * half
    cots = call(functools.partial(kernel_spans, sz), "spans", share_shapes(cot_lines), [labelled], hbm_outs=range(bands), sems=bands)
    stats, weights, *cots = tie((stats, conv_weights, *cots))
    gathered = spread(stats)
    cots = trade(cots)
    acts = [[kept, swap(kept, 1), swap(kept, 2)]]
    moments = []
    saves = []
    for layer in (1, 2):
        rows = sz.rows + 2 * (HALO - layer)
        outs = [
            stats_shape, pixel_shape(rows - 2, F32), tile_shape, pixel_shape(sz.rows, BF16),
            pixel_shape(sz.rows + 2 * layer, F32),
        ]
        scratch = [pixel_space(rows, BF16, 3), weight_space]
        stats, conv, moment, act, saved = call(
            functools.partial(kernel_forward, sz, layer), "forward", outs,
            consts + [gathered, conv, norms, head(layer, weights), conv_weights], scratch,
            conv_flops(rows - 2), hbm_ins=(6,), hbm_outs=(3, 4), sems=5,
        )
        moments.append(moment)
        saves.append(saved)
        if layer == 1:
            stats, weights, *acts[0] = tie((stats, conv_weights, *acts[0]))
            gathered = spread(stats)
        else:
            stats, *cots = tie((stats, *cots))
            gathered = spread(stats)
        if layer == 1:
            acts[0].append(swap(acts[0][2], 1))
        acts.append([act, swap(act, 1), swap(act, 2)])

    rows = sz.rows + 2 * (HALO - 3)
    stats, grad, normed, moment, *shares = call(
        functools.partial(kernel_pool, sz), "pool",
        [stats_shape, pixel_shape(rows, F32), pixel_shape(rows, BF16), tile_shape]
        + share_shapes(lines + 2 * sz.pixels),
        consts + [gathered, conv, norms, index, near, far] + cots,
        [
            pltpu.VMEM((lines, c), jnp.int32), pltpu.VMEM((2 * half, c), BF16), pltpu.VMEM((2 * half, c), BF16),
            pltpu.VMEM((cot_lines, c), BF16),
            pltpu.VMEM((c // 128, (rows + 2) * w, 128), F32), pltpu.VMEM((c // 128, sz.pixels, 128), F32),
            pltpu.VMEM((lines, c), BF16), pixel_space(sz.rows, BF16), pixel_space(sz.rows, BF16),
        ],
        conv_flops(4), hbm_ins=range(5, 8 + bands), hbm_outs=range(4, 4 + bands), sems=3 + 4 * bands,
    )
    moments.append(moment)
    stats, weights, acts[0][3], *rest = tie((stats, conv_weights, acts[0][3], *acts[1], *acts[2]))
    acts[1], acts[2] = rest[:3], rest[3:]
    acts[1].append(swap(acts[1][2], 1))
    gathered = spread(stats)
    exchanged = trade(shares)
    acts[2].append(swap(acts[2][2], 1))
    pooled_parts = exchanged

    totals = [None, None, None]
    share = 9 * (c // n_maps)
    steps = n_maps.bit_length() - 1

    def part_shape(parts, dtype):
        return shape((parts, share, q), dtype)

    def part_space(parts, dtype):
        return pltpu.VMEM((parts, share, q), dtype)

    def weight_grad(layer, gathered, given, first):
        scratch = [
            pltpu.VMEM((sz.height * w, q), BF16),
            pltpu.VMEM((sz.height * w, q), BF16),
            pltpu.VMEM((sz.height * w, c), BF16),
            pltpu.VMEM((sz.height * w, 9 * q), BF16),
        ]
        outs = [part_shape(n_maps // 2, dtype) for dtype in (F32, BF16)]
        scratch.append(pltpu.VMEM((c, 9 * q), F32))
        if layer > 0:
            scratch += [part_space(n_maps // 2, dtype) for dtype in (F32, BF16)]
        return call(
            functools.partial(kernel_weight_grad, sz, layer, first), "weight_grad", outs,
            consts + [gathered, moments[layer], norms] + given + acts[layer], scratch, conv_flops(sz.rows),
            hbm_ins=range(5, 5 + 2 * bands), hbm_outs=() if layer == 0 else (0, 1), sems=3 * bands + 2,
        )

    def step_of(send, k):
        return lax.ppermute(send, "maps", [(m, m ^ (1 << k)) for m in range(n_maps)])

    def halved(keep, received):
        size = keep.shape[0] // 2
        return call(
            kernel_halve, "halve", [part_shape(size, dtype) for dtype in (F32, BF16)], [keep, received],
            [part_space(2 * size, F32), part_space(size, BF16)],
            hbm_ins=(0,), hbm_outs=(0, 1), sems=4,
        )

    def halve(keep, received, k):
        while k < steps - 1:
            k += 1
            keep, send = halved(keep, received)
            received = step_of(send, k)
        return keep, received

    shards = [None, None, None]
    for layer in (2, 1):
        halo = layer + 1
        rows = sz.rows + 2 * halo
        received, gathered_here = exchanged, gathered
        stats, grad, normed, totals[layer], *shares = call(
            functools.partial(kernel_backward, sz, layer), "backward",
            [stats_shape, pixel_shape(rows - 2, F32), pixel_shape(rows - 2, BF16), tile_shape]
            + share_shapes(2 * sz.pixels),
            consts + [
                gathered, grad, normed, moments[layer], norms, head(layer, weights), conv_weights, saves[layer - 1],
                moments[layer - 1],
            ],
            [
                pixel_space(rows - 2, F32), pixel_space(rows, BF16, 3), weight_space, pixel_space(sz.rows, BF16),
                pixel_space(sz.rows, BF16),
            ],
            conv_flops(rows - 2), hbm_ins=(8, 9), hbm_outs=range(4, 4 + bands), sems=4 + 2 * bands,
        )
        if layer == 2:
            stats, weights, acts[1][3], acts[2][3], *received = tie(
                (stats, conv_weights, acts[1][3], acts[2][3], *received)
            )
            gathered = spread(stats)
            exchanged = trade(shares)
            keep2, send2 = weight_grad(2, gathered_here, received, (lines, lines + sz.pixels))
            gathered, send2 = tie((gathered, send2))
            arrived2 = step_of(send2, 0)
        else:
            stats, weights, *received = tie((stats, conv_weights, *received))
            gathered = spread(stats)
            exchanged = trade(shares)
            keep1, send1 = weight_grad(1, gathered_here, received, (0, sz.pixels))
            gathered, send1, arrived2 = tie((gathered, send1, arrived2))
            arrived1 = step_of(send1, 0)
            keep2, send2 = halved(keep2, arrived2)

    arrived2 = step_of(send2, 1)
    keep0, send0 = weight_grad(0, gathered, exchanged, (0, sz.pixels))
    send0, arrived2 = tie((send0, arrived2))
    arrived0 = step_of(send0, 0)
    keep1, send1 = halved(keep1, arrived1)
    keep2, send2 = halved(keep2, arrived2)
    arrived1 = step_of(send1, 1)
    arrived2 = step_of(send2, 2)
    arrived0, arrived1, arrived2 = tie((arrived0, arrived1, arrived2))
    half_maps = n_maps // 2
    (partial,) = call(
        kernel_add, "add", [part_shape(half_maps, BF16)], [keep0, arrived0],
        [part_space(half_maps, F32)], hbm_ins=(0,), sems=half_maps,
    )
    alike = [[m for m in range(n_maps) if m & 1 == bit] for bit in (0, 1)]
    received = lax.all_to_all(partial, "maps", 0, 0, tiled=True, axis_index_groups=alike)
    shards[2] = halve(keep2, arrived2, 2)
    shards[1] = halve(keep1, arrived1, 1)
    input_grad, totals[0], pooled = call(
        functools.partial(kernel_last, sz), "last",
        [pixel_shape(sz.rows, BF16), tile_shape, shape((sz.height // 2 * half, q), BF16)],
        consts + [gathered, grad, normed, moments[0], norms, head(0, weights), conv_weights] + pooled_parts,
        [pixel_space(sz.rows + 2, BF16, 3), weight_space, pixel_space(sz.rows, F32), pixel_space(sz.rows, BF16)],
        conv_flops(sz.rows), hbm_ins=range(8, 9 + bands), hbm_outs=(0, 2), sems=4 + bands,
    )

    norm_shape = shape((3, 2, c), F32)
    squares, shard, norm_grad = call(
        functools.partial(kernel_squares, sz), "squares",
        [shape((sz.devices, 1, q), F32), part_shape(3, F32), norm_shape],
        [received, *shards[1], *shards[2], totals[2], totals[1], totals[0]],
        [part_space(2, F32), part_space(2, BF16)], hbm_ins=range(1, 5), sems=4,
    )
    every = lax.all_to_all(squares, AXES, 0, 0, tiled=True)
    rate = 2.0 / math.sqrt(9.0 * c)
    total, conv_first, conv_second, conv_new, norm_first, norm_second, norm_new = call(
        functools.partial(kernel_adam, sz, rate), "adam",
        [shape((1, 128), F32)] + [part_shape(3, F32)] * 3 + [norm_shape] * 3,
        [every, step, shard]
        + [v.reshape(3, share, q) for v in (conv_master, conv_moment1, conv_moment2)]
        + [norm_grad, norms, norm_first, norm_second],
        [pltpu.VMEM((1, 128), F32)] + [part_space(3, F32)] * 3 + [pltpu.VMEM((3, 3, 2, c), F32)],
        hbm_ins=(3, 4, 5), hbm_outs=range(7), smem_ins=(1,), sems=22,
    )
    return (
        pooled.reshape(1, sz.height // 2, half, q),
        input_grad.reshape(block_input.shape),
        total[0, :1],
        conv_first.reshape(conv_master.shape),
        conv_second.reshape(conv_master.shape),
        conv_new.reshape(conv_master.shape),
        norm_first.transpose(1, 0, 2),
        norm_second.transpose(1, 0, 2),
        norm_new.transpose(1, 0, 2),
    )


def solution(mesh):
    def run(*args):
        bands = mesh.shape["rows"]
        maps = mesh.shape["maps"]
        shape = args[0].shape
        sz = Sizes(maps, bands, shape[1] // bands, shape[2], shape[3])
        return jax.shard_map(
            functools.partial(local, sz),
            mesh=mesh,
            in_specs=(
                P("maps", "rows", None, None),
                P(),
                P(),
                P("maps", "rows", None, None),
                P("maps", None, None),
                P(),
                P(),
                P("maps", None, None, "rows"),
                P(),
                P(None, None, "maps", "rows"),
                P(None, None, "maps", "rows"),
                P(None, None, "maps", "rows"),
                P(),
                P(),
            ),
            out_specs=(
                P("maps", None, None, "rows"),
                P("maps", "rows", None, None),
                P(),
                P(None, None, "maps", "rows"),
                P(None, None, "maps", "rows"),
                P(None, None, "maps", "rows"),
                P(),
                P(),
                P(),
            ),
            check_vma=False,
        )(*args)

    return run
```

```python
import functools
import math

import jax
import jax.numpy as jnp
from jax import lax
from jax.experimental import pallas as pl
from jax.experimental.pallas import tpu as pltpu
from jax.sharding import PartitionSpec as P

DOMAINS = 4
norm_epsilon = 1e-05
clip_limit = 1.0
first_decay = 0.9
second_decay = 0.999
adam_epsilon = 1e-08
norm_rate = 0.5
weight_decay = 0.01

HALO = 6
SPACE = 28
AXES = ("maps", "rows")
F32 = jnp.float32
BF16 = jnp.bfloat16


class Sizes:
    def __init__(self, maps, bands, rows, width, channels):
        self.maps = maps
        self.bands = bands
        self.devices = maps * bands
        self.rows = rows
        self.width = width
        self.channels = channels
        self.height = rows * bands
        self.short_height = 2 * (self.height * 7 // 16)
        self.short_width = 2 * (width * 13 // 32)
        self.pixels = rows * width
        self.quarter = channels // bands


def spec(space):
    return pl.BlockSpec(memory_space=space)


def params(megabytes):
    return pltpu.CompilerParams(vmem_limit_bytes=megabytes << 20)


class Copies:
    def __init__(self, sems):
        self.sems = sems
        self.used = 0

    def start(self, source, target):
        copy = pltpu.make_async_copy(source, target, self.sems.at[self.used])
        self.used += 1
        copy.start()
        return copy


def wait(*copies):
    for copy in copies:
        copy.wait()


def line_share(ref, start, step, size):
    return ref.at[pl.ds(pl.multiple_of(start, step), size)]


def own_sums(gathered_ref, weights_ref):
    return jnp.sum(gathered_ref[...] * weights_ref[...], axis=0)


def all_sums(gathered_ref):
    return jnp.sum(gathered_ref[...], axis=0)


def split_rows(tile, channels):
    first = jnp.concatenate([tile[k : k + 1, :] for k in range(4)], axis=1)
    second = jnp.concatenate([tile[k : k + 1, :] for k in range(4, 8)], axis=1)
    return first, second


def join_rows(first, second):
    lanes = first.shape[1] // 4
    return jnp.concatenate(
        [row[:, k * lanes : (k + 1) * lanes] for row in (first, second) for k in range(4)], axis=0
    )


def tiled(sz, value):
    return jnp.concatenate([value] * (sz.channels // value.shape[1]), axis=1)


class Masks:
    def __init__(self, sz, limits_ref):
        self.col = lax.broadcasted_iota(jnp.int32, (sz.width, 128), 0)
        self.wide = jnp.where(self.col < limits_ref[2:3, :], 1.0, 0.0)
        self.inner_left = jnp.where(self.col > 0, 1.0, 0.0)
        self.inner_right = jnp.where(self.col < sz.width - 1, 1.0, 0.0)
        self.limits_ref = limits_ref

    def valid(self, row):
        inside = (self.limits_ref[0:1, :] <= row) & (self.limits_ref[1:2, :] > row)
        return self.wide * jnp.where(inside, 1.0, 0.0)

    def valid_of_map(self, row):
        return self.wide * jnp.where(self.limits_ref[3:4, :] > row, 1.0, 0.0)


def line(sz, row):
    return slice(row * sz.width, (row + 1) * sz.width)


def shifted_right(sz, masks, value):
    mask = masks.inner_left
    return pltpu.roll(value, 1, 0) * (mask if value.shape[1] == 128 else tiled(sz, mask))


def shifted_left(sz, masks, value):
    mask = masks.inner_right
    return pltpu.roll(value, sz.width - 1, 0) * (mask if value.shape[1] == 128 else tiled(sz, mask))


def put_shifted(sz, masks, x3_ref, row, value, reverse=False):
    before = shifted_right(sz, masks, value)
    after = shifted_left(sz, masks, value)
    if reverse:
        before, after = after, before
    c = sz.channels
    x3_ref[line(sz, row), 0:c] = before.astype(BF16)
    x3_ref[line(sz, row), c : 2 * c] = value.astype(BF16)
    x3_ref[line(sz, row), 2 * c : 3 * c] = after.astype(BF16)


def fold(value):
    total = value[0:8, :]
    for k in range(1, value.shape[0] // 8):
        total = total + value[8 * k : 8 * (k + 1), :]
    return total


HEAD = 1


class Weights:
    def __init__(self, copies, head_ref, weights_hbm, buffer_ref, layer):
        self.head_ref, self.buffer_ref = head_ref, buffer_ref
        self.loads = {
            first: copies.start(
                weights_hbm.at[layer, pl.ds(first, 3 - first % 3)],
                buffer_ref.at[pl.ds(first - HEAD, 3 - first % 3)],
            )
            for first in (HEAD, 3, 6)
        }

    def wait(self, tap):
        if tap in self.loads:
            wait(self.loads[tap])

    def taps(self, first, last):
        if first < HEAD:
            part = self.head_ref[first:last]
        else:
            part = self.buffer_ref[first - HEAD : last - HEAD]
        return part.reshape(-1, part.shape[-1])


def conv_rows(sz, x3_ref, weights, out_ref, rows, reverse=False):
    c, w = sz.channels, sz.width
    n = rows * w
    spans = [(0, HEAD), (HEAD, 3), (3, 6), (6, 9)]
    if reverse:
        spans = [(tap, tap + 1) for tap in range(9)]
    for first, last in spans:
        weights.wait(first)
        i = first // 3
        start = (2 - i if reverse else i) * w
        lhs = x3_ref[start : start + n, (first - 3 * i) * c : (last - 3 * i) * c]
        across = 1 if reverse else 0
        term = lax.dot_general(
            lhs, weights.taps(first, last), (((1,), (across,)), ((), ())), preferred_element_type=F32
        )
        if first == 0:
            out_ref[...] = term
        else:
            out_ref[...] += term


def put_stats(sz, first, second, out_ref):
    tile = join_rows(jnp.sum(first, axis=0, keepdims=True), jnp.sum(second, axis=0, keepdims=True))
    out_ref[...] = jnp.broadcast_to(tile[None], out_ref.shape)


def silu_parts(half):
    t = jnp.tanh(half)
    product = half * t
    return half + product, (0.5 + 0.5 * t) * (1.0 + (half - product))


class Stats:
    def __init__(self, sz):
        self.first = jnp.zeros((8, sz.channels), F32)
        self.second = jnp.zeros((8, sz.channels), F32)

    def add(self, first, second):
        self.first = self.first + fold(first)
        self.second = self.second + fold(second)


def add_conv_rows(sz, masks, stats, conv_ref, skip, first, last):
    for row in range(max(first, skip), min(last, skip + sz.rows)):
        value = conv_ref[line(sz, row), :]
        masked = value * tiled(sz, masks.valid(row - skip))
        stats.add(masked, masked * value)


def band_lanes(sz, n):
    return pl.ds(pl.multiple_of((lax.axis_index("rows") ^ n) * sz.quarter, sz.quarter), sz.quarter)


def send_shares(sz, copies, source_ref, targets, first):
    lines = source_ref.shape[0]
    return [
        copies.start(source_ref.at[:, band_lanes(sz, n)], target.at[pl.ds(first, lines)])
        for n, target in enumerate(targets)
    ]


def kernel_spans(sz, given_ref, *rest):
    shares, sems = rest[: sz.bands], rest[sz.bands]
    copies = Copies(sems)
    span = sz.rows // 2 * (sz.width // 2)
    wait(*[
        copies.start(line_share(given_ref, (lax.axis_index("rows") ^ n) * span, span, share.shape[0]), share)
        for n, share in enumerate(shares)
    ])


def kernel_edges(sz, x_hbm, index_hbm, near_ref, far_ref, x_ref, index_ref, sems):
    copies = Copies(sems)
    edge = HALO * sz.width
    few = sz.width
    odd = lax.axis_index("rows") % 2
    last = index_hbm.shape[0] - few
    loads = []
    rest = []
    for k, (first, target) in enumerate(((1 - odd, near_ref), (odd, far_ref))):
        loads.append(copies.start(line_share(index_hbm, first * last, few, few), index_ref.at[k]))
        rest.append(copies.start(line_share(x_hbm, first * (sz.pixels - edge), edge, edge), target.at[pl.ds(0, edge)]))
    rest.append(copies.start(x_hbm, x_ref))
    wait(*loads)
    near_ref[edge : edge + few, :] = index_ref[0].astype(BF16)
    far_ref[edge : edge + few, :] = index_ref[1].astype(BF16)
    wait(*rest)


def kernel_places(sz, kind_ref, domain_ref, limits_ref, member_ref, _):
    m, r = lax.axis_index("maps"), lax.axis_index("rows")
    start = r * sz.rows

    def rows_of(k):
        return jnp.where(kind_ref[k] == 1, sz.height, sz.short_height)

    def cols_of(k):
        return jnp.where(kind_ref[k] == 1, sz.short_width, sz.width)

    own = domain_ref[m]
    area = jnp.int32(0)
    for k in range(sz.maps):
        area = area + jnp.where(domain_ref[k] == own, rows_of(k) * cols_of(k), 0)
    tile = member_ref.shape[1:]
    weight = 1.0 / jnp.full(tile, area.astype(F32))
    for k in range(sz.maps):
        value = jnp.where(domain_ref[k] == own, weight, 0.0)
        for b in range(sz.bands):
            member_ref[k * sz.bands + b] = value
    line = lax.broadcasted_iota(jnp.int32, limits_ref.shape, 0)
    limits_ref[...] = jnp.where(
        line == 0, -start, jnp.where(line == 1, rows_of(m) - start, jnp.where(line == 2, cols_of(m), rows_of(m)))
    )


def kernel_first(sz, limits_ref, near_ref, x_ref, far_ref, head_ref, weights_hbm, stats_ref, conv_ref, act_hbm, x3_ref,
                 buffer_ref, sems):
    copies = Copies(sems)
    weights = Weights(copies, head_ref, weights_hbm, buffer_ref, 0)
    masks = Masks(sz, limits_ref)
    stats = Stats(sz)

    odd = lax.axis_index("rows") % 2 == 1

    def prepare(row):
        if row < HALO:
            value = jnp.where(odd, near_ref[line(sz, row), :], far_ref[line(sz, row), :])
        elif row < HALO + sz.rows:
            value = x_ref[line(sz, row - HALO), :]
        else:
            below = line(sz, row - HALO - sz.rows)
            value = jnp.where(odd, far_ref[below, :], near_ref[below, :])
        put_shifted(sz, masks, x3_ref, row, value.astype(F32))

    def work(first, last):
        conv_rows(sz, x3_ref, weights, conv_ref, last)
        add_conv_rows(sz, masks, stats, conv_ref, HALO - 1, first, last)

    for row in range(sz.rows + 2 * HALO):
        prepare(row)
    work(0, sz.rows + 2 * HALO - 2)
    out = copies.start(x_ref, act_hbm)
    put_stats(sz, stats.first, stats.second, stats_ref)
    wait(out)


def norm_of(sz, gathered_ref, member_ref):
    mean, squares = split_rows(own_sums(gathered_ref, member_ref), sz.channels)
    return mean, lax.rsqrt(squares - mean * mean + norm_epsilon)


def kernel_forward(sz, layer, limits_ref, member_ref, gathered_ref, before_ref, norm_ref, head_ref, weights_hbm, *rest):
    stats_ref, conv_ref, moments_ref, act_hbm, saved_hbm, x3_ref, buffer_ref, sems = rest
    copies = Copies(sems)
    weights = Weights(copies, head_ref, weights_hbm, buffer_ref, layer)
    halo = HALO - layer
    rows = sz.rows + 2 * halo
    skip = (halo - layer) * sz.width
    outs = []
    mean, inverse = norm_of(sz, gathered_ref, member_ref)
    moments_ref[...] = join_rows(mean, inverse)
    scale = 0.5 * norm_ref[layer - 1, 0:1, :] * inverse
    offset = 0.5 * norm_ref[layer - 1, 1:2, :] - mean * scale
    masks = Masks(sz, limits_ref)
    stats = Stats(sz)
    c = sz.channels

    def prepare(row):
        value = before_ref[line(sz, row), :]
        act, _ = silu_parts(value * scale + offset)
        put_shifted(sz, masks, x3_ref, row, act * tiled(sz, masks.valid(row - halo)))
        if row == halo + sz.rows - 1:
            outs.append(copies.start(x3_ref.at[pl.ds(halo * sz.width, sz.pixels), pl.ds(c, c)], act_hbm))

    def work(first, last):
        conv_rows(sz, x3_ref, weights, conv_ref, last)
        outs.append(copies.start(before_ref.at[pl.ds(skip, saved_hbm.shape[0])], saved_hbm))
        add_conv_rows(sz, masks, stats, conv_ref, halo - 1, first, last)

    for row in range(rows):
        prepare(row)
    work(0, rows - 2)
    put_stats(sz, stats.first, stats.second, stats_ref)
    wait(*outs)


def kernel_pool(sz, limits_ref, member_ref, gathered_ref, before_ref, norm_ref, index_hbm, near_hbm, far_hbm, *rest):
    cotangents, rest = rest[: sz.bands], rest[sz.bands :]
    (stats_ref, grad_ref, normed_ref, moments_ref), rest = rest[:4], rest[4:]
    shares, rest = rest[: sz.bands], rest[sz.bands :]
    (index_ref, near_ref, far_ref, cotangent_ref, spread_ref, act_ref, pooled_ref, grad16_ref, normed16_ref, sems) = rest
    c, w = sz.channels, sz.width
    half = w // 2
    windows = sz.rows // 2
    edge = HALO * w
    copies = Copies(sems)
    inputs = [
        copies.start(index_hbm, index_ref),
        copies.start(near_hbm.at[pl.ds(edge, w)], near_ref),
        copies.start(far_hbm.at[pl.ds(edge, w)], far_ref),
    ]
    inputs += [
        copies.start(
            ref, cotangent_ref.at[:, band_lanes(sz, n)]
        )
        for n, ref in enumerate(cotangents)
    ]
    mean, inverse = norm_of(sz, gathered_ref, member_ref)
    moments_ref[...] = join_rows(mean, inverse)
    gain = 0.5 * norm_ref[2, 0:1, :]
    shift = 0.5 * norm_ref[2, 1:2, :]
    halo = HALO - 3
    rows = sz.rows + 2 * halo
    lines = sz.pixels // 4
    groups = c // 128
    masks = Masks(sz, limits_ref)
    for row in range(rows):
        normed = (before_ref[line(sz, row), :] - mean) * inverse
        normed_ref[line(sz, row), :] = normed.astype(BF16)
        act, slope = silu_parts(normed * gain + shift)
        valid = tiled(sz, masks.valid(row - halo))
        grad_ref[line(sz, row), :] = slope * valid
        if halo <= row < halo + sz.rows:
            normed16_ref[line(sz, row - halo), :] = normed.astype(BF16)
            act = act * valid
            for g in range(groups):
                act_ref[g, line(sz, row - halo), :] = act[:, g * 128 : (g + 1) * 128]
    outs = send_shares(sz, copies, normed16_ref, shares, lines + sz.pixels)
    wait(*inputs)
    for p in range(windows):
        index = index_ref[p * half : (p + 1) * half, :]
        result = jnp.zeros(index.shape, F32)
        for corner in range(4):
            start = (2 * p + corner // 2) * w + corner % 2
            taken = jnp.concatenate(
                [act_ref[g, pl.ds(start, half, stride=2), :] for g in range(groups)], axis=1
            )
            result = jnp.where(index == corner, taken, result)
        pooled_ref[p * half : (p + 1) * half, :] = result.astype(BF16)
    outs += send_shares(sz, copies, pooled_ref, shares, 0)
    odd = lax.axis_index("rows") % 2 == 1
    for p in range(windows + 4):
        if p < 2:
            place = slice(p * half, (p + 1) * half)
            index = jnp.where(odd, near_ref[place, :].astype(jnp.int32), far_ref[place, :].astype(jnp.int32))
        elif p < windows + 2:
            index = index_ref[(p - 2) * half : (p - 1) * half, :]
        else:
            place = slice((p - windows - 2) * half, (p - windows - 1) * half)
            index = jnp.where(odd, far_ref[place, :].astype(jnp.int32), near_ref[place, :].astype(jnp.int32))
        given = cotangent_ref[p * half : (p + 1) * half, :].astype(F32)
        for corner in range(4):
            start = (2 * p + corner // 2) * w + corner % 2
            placed = jnp.where(index == corner, given, 0.0)
            for g in range(groups):
                spread_ref[g, pl.ds(start, half, stride=2), :] = placed[:, g * 128 : (g + 1) * 128]
    stats = Stats(sz)
    for row in range(rows):
        upstream = jnp.concatenate([spread_ref[g, line(sz, row + 1), :] for g in range(groups)], axis=1)
        grad = upstream * grad_ref[line(sz, row), :]
        grad_ref[line(sz, row), :] = grad
        if halo <= row < halo + sz.rows:
            grad16_ref[line(sz, row - halo), :] = grad.astype(BF16)
            stats.add(grad, grad * normed_ref[line(sz, row), :].astype(F32))
    outs += send_shares(sz, copies, grad16_ref, shares, lines)
    put_stats(sz, stats.first, stats.second, stats_ref)
    wait(*outs)


class ConvGrad:
    def __init__(self, sz, layer, masks, member_ref, moments_ref, gathered_ref, norm_ref):
        self.sz, self.masks = sz, masks
        _, inverse = split_rows(moments_ref[...], sz.channels)
        one, two = split_rows(own_sums(gathered_ref, member_ref), sz.channels)
        self.scale = norm_ref[layer, 0:1, :] * inverse
        self.one, self.two = one, two

    def row(self, row, grad, normed):
        value = self.scale * (grad - self.one - normed * self.two)
        return value * tiled(self.sz, self.masks.valid(row))


def kernel_backward(sz, layer, limits_ref, member_ref, gathered_ref, grad_ref, normed_ref, moments_ref, norm_ref,
                    head_ref, weights_hbm, saved_hbm, moments_below_ref, stats_ref, below_ref, normed_below_ref, totals_ref,
                    *rest):
    shares, (saved_ref, x3_ref, buffer_ref, grad16_ref, normed16_ref, sems) = rest[: sz.bands], rest[sz.bands :]
    copies = Copies(sems)
    weights = Weights(copies, head_ref, weights_hbm, buffer_ref, layer)
    saved = copies.start(saved_hbm, saved_ref)
    halo = layer + 1
    rows = sz.rows + 2 * halo
    masks = Masks(sz, limits_ref)
    conv_grad = ConvGrad(sz, layer, masks, member_ref, moments_ref, gathered_ref, norm_ref)
    below = layer - 1
    mean, inverse = split_rows(moments_below_ref[...], sz.channels)
    gain = 0.5 * norm_ref[below, 0:1, :]
    shift = 0.5 * norm_ref[below, 1:2, :]
    stats = Stats(sz)
    outs = []

    def prepare(row):
        value = conv_grad.row(row - halo, grad_ref[line(sz, row), :], normed_ref[line(sz, row), :].astype(F32))
        put_shifted(sz, masks, x3_ref, row, value, True)

    def work(first, last):
        conv_rows(sz, x3_ref, weights, below_ref, last, True)
        if first == 0:
            wait(saved)
        for row in range(first, last):
            normed = (saved_ref[line(sz, row), :] - mean) * inverse
            normed_below_ref[line(sz, row), :] = normed.astype(BF16)
            _, slope = silu_parts(normed * gain + shift)
            own = row - (halo - 1)
            grad = below_ref[line(sz, row), :] * slope * tiled(sz, masks.valid(own))
            below_ref[line(sz, row), :] = grad
            if 0 <= own < sz.rows:
                grad16_ref[line(sz, own), :] = grad.astype(BF16)
                normed16_ref[line(sz, own), :] = normed.astype(BF16)
                stats.add(grad, grad * normed)

    for row in range(rows):
        prepare(row)
    work(0, rows - 2)
    outs += send_shares(sz, copies, grad16_ref, shares, 0)
    outs += send_shares(sz, copies, normed16_ref, shares, sz.pixels)
    put_stats(sz, stats.first, stats.second, stats_ref)
    totals_ref[...] = all_sums(gathered_ref)
    wait(*outs)


def kernel_last(sz, limits_ref, member_ref, gathered_ref, grad_ref, normed_ref, moments_ref, norm_ref, head_ref,
                weights_hbm, *rest):
    parts, (out_hbm, totals_ref, pooled_hbm, x3_ref, buffer_ref, acc_ref, out_ref, sems) = (
        rest[: sz.bands], rest[sz.bands :]
    )
    copies = Copies(sems)
    weights = Weights(copies, head_ref, weights_hbm, buffer_ref, 0)
    lines = sz.pixels // 4
    outs = []
    for n, ref in enumerate(parts):
        target = line_share(pooled_hbm, (lax.axis_index("rows") ^ n) * lines, lines, lines)
        outs.append(copies.start(ref.at[pl.ds(0, lines)], target))
    totals_ref[...] = all_sums(gathered_ref)
    masks = Masks(sz, limits_ref)
    conv_grad = ConvGrad(sz, 0, masks, member_ref, moments_ref, gathered_ref, norm_ref)

    def prepare(row):
        value = conv_grad.row(row - 1, grad_ref[line(sz, row), :], normed_ref[line(sz, row), :].astype(F32))
        put_shifted(sz, masks, x3_ref, row, value, True)

    def work(first, last):
        conv_rows(sz, x3_ref, weights, acc_ref, last, True)
        pixels = slice(first * sz.width, last * sz.width)
        out_ref[pixels, :] = acc_ref[pixels, :].astype(BF16)

    for row in range(sz.rows + 2):
        prepare(row)
    work(0, sz.rows)
    outs.append(copies.start(out_ref, out_hbm))
    wait(*outs)


def kernel_weight_grad(sz, layer, first, limits_ref, member_ref, gathered_ref, moments_ref, norm_ref, *rest):
    w, q, c, bands = sz.width, sz.quarter, sz.channels, sz.bands
    pixels = sz.height * w
    given, rest = rest[:bands], rest[bands:]
    acts, rest = rest[:bands], rest[bands:]
    keep_hbm, send_hbm, grad_ref, normed_ref, act_ref, x9_ref, term_ref, *spaces, sems = rest
    keep_ref, send_ref = spaces or (keep_hbm, send_hbm)
    copies = Copies(sems)
    inputs = []
    for n in range(bands):
        start = (lax.axis_index("rows") ^ n) * sz.pixels
        for source, target, top in ((given[n], grad_ref, first[0]), (given[n], normed_ref, first[1])):
            inputs.append(
                copies.start(source.at[pl.ds(top, sz.pixels)], line_share(target, start, sz.pixels, sz.pixels))
            )
    act_loads = [
        copies.start(
            acts[n], line_share(act_ref, (lax.axis_index("rows") ^ n) * sz.pixels, sz.pixels, sz.pixels)
        )
        for n in range(bands)
    ]
    band = lax.axis_index("rows")
    own = lax.axis_index("maps")
    tile = own_sums(gathered_ref, member_ref)
    one, two, inverse, gain = (jnp.zeros((1, q), F32) for _ in range(4))
    for b in range(bands):
        here = band == b
        one = jnp.where(here, tile[b : b + 1, :], one)
        two = jnp.where(here, tile[b + 4 : b + 5, :], two)
        inverse = jnp.where(here, moments_ref[b + 4 : b + 5, :], inverse)
        gain = jnp.where(here, norm_ref[layer, 0:1, b * q : (b + 1) * q], gain)
    wait(*inputs)
    masks = Masks(sz, limits_ref)
    blank = jnp.zeros((w, q), BF16)
    for row in range(sz.height):
        value = grad_ref[line(sz, row), :].astype(F32) - one - normed_ref[line(sz, row), :].astype(F32) * two
        value = (gain * inverse) * value * masks.valid_of_map(row)
        for j, piece in enumerate((shifted_left(sz, masks, value), value, shifted_right(sz, masks, value))):
            piece = piece.astype(BF16)
            for i in range(3):
                if 0 <= row + i - 1 < sz.height:
                    x9_ref[line(sz, row + i - 1), (3 * i + j) * q : (3 * i + j + 1) * q] = piece
    for j in range(3):
        x9_ref[line(sz, sz.height - 1), j * q : (j + 1) * q] = blank
        x9_ref[line(sz, 0), (6 + j) * q : (7 + j) * q] = blank
    share = c // sz.maps
    wait(*act_loads)
    term = lax.dot_general(
        act_ref[...], x9_ref[...], (((0,), (0,)), ((), ())), preferred_element_type=F32
    )
    term_ref[...] = term
    if layer == 0:
        others = [2 * place + (own & 1) for place in range(sz.maps // 2)]
        order = others + [other ^ 1 for other in others]
    else:
        order = [own ^ relative for relative in halving_order(sz.maps)]
    for position, other in enumerate(order):
        lines = pl.ds(pl.multiple_of(other * share, share), share)
        for tap in range(9):
            place = slice(tap * share, (tap + 1) * share)
            part = term_ref[lines, tap * q : (tap + 1) * q]
            if position < sz.maps // 2:
                keep_ref[position, place, :] = part
            else:
                send_ref[position - sz.maps // 2, place, :] = part.astype(BF16)
    if spaces:
        wait(copies.start(keep_ref, keep_hbm), copies.start(send_ref, send_hbm))


def halving_order(maps):
    bits = maps.bit_length() - 1
    return [sum(((place >> (bits - 1 - k)) & 1) << k for k in range(bits)) for place in range(maps)]


def kernel_add(keep_hbm, received_ref, out_ref, keep_ref, sems):
    copies = Copies(sems)
    loads = [copies.start(keep_hbm.at[k], keep_ref.at[k]) for k in range(keep_ref.shape[0])]
    for k, load in enumerate(loads):
        wait(load)
        out_ref[k] = (keep_ref[k] + received_ref[k].astype(F32)).astype(BF16)


def kernel_halve(keep_hbm, received_ref, next_keep_hbm, next_send_hbm, keep_ref, send_ref, sems):
    half = next_keep_hbm.shape[0]
    copies = Copies(sems)
    loads = [copies.start(keep_hbm.at[part], keep_ref.at[part]) for part in (pl.ds(half, half), pl.ds(0, half))]
    wait(loads[0])
    send_ref[...] = (keep_ref[half:] + received_ref[half:].astype(F32)).astype(BF16)
    first = copies.start(send_ref, next_send_hbm)
    wait(loads[1])
    keep_ref[:half] += received_ref[:half].astype(F32)
    wait(first, copies.start(keep_ref.at[pl.ds(0, half)], next_keep_hbm))


def kernel_squares(sz, received_ref, keep1_hbm, last1_hbm, keep2_hbm, last2_hbm, totals2_ref, totals1_ref,
                   totals0_ref, squares_ref, shard_ref, norm_grad_ref, keep_ref, last_ref, sems):
    copies = Copies(sems)
    loads = [
        copies.start(source.at[0], target.at[k])
        for k, pair in enumerate(((keep1_hbm, last1_hbm), (keep2_hbm, last2_hbm)))
        for source, target in zip(pair, (keep_ref, last_ref))
    ]
    for layer, ref in enumerate((totals0_ref, totals1_ref, totals2_ref)):
        shift_row, gain_row = split_rows(ref[...], sz.channels)
        norm_grad_ref[layer, 0:1, :] = gain_row
        norm_grad_ref[layer, 1:2, :] = shift_row
    value = received_ref[0].astype(F32)
    for m in range(1, received_ref.shape[0]):
        value = value + received_ref[m].astype(F32)
    shard_ref[0] = value
    total = jnp.sum(value * value, axis=0, keepdims=True)
    wait(*loads)
    for layer in (1, 2):
        value = keep_ref[layer - 1] + last_ref[layer - 1].astype(F32)
        shard_ref[layer] = value
        total = total + jnp.sum(value * value, axis=0, keepdims=True)
    squares_ref[...] = jnp.broadcast_to(total[None], squares_ref.shape)


def kernel_adam(sz, rate, every_ref, step_ref, shard_ref, master_hbm, first_old_ref, second_old_ref, norm_grad_ref, norm_ref,
                norm_first_ref, norm_second_ref, total_hbm, first_out_hbm, second_out_hbm, master_out_hbm,
                norm_first_hbm, norm_second_hbm, norm_hbm,
                total_ref, master_ref, first_ref, second_ref, small_ref, sems):
    copies = Copies(sems)
    loads = [
        [
            copies.start(source.at[layer], target.at[layer])
            for source, target in ((master_hbm, master_ref),)
        ]
        for layer in range(3)
    ]
    norm_grad = norm_grad_ref[...]
    square = jnp.sum(jnp.sum(every_ref[...], axis=0)) + jnp.sum(norm_grad * norm_grad)
    total = jnp.sqrt(jnp.full((1, 128), square, F32))
    total_ref[...] = total
    outs = [copies.start(total_ref, total_hbm)]
    scale = jnp.minimum(1.0, clip_limit / total)
    count = jnp.full((1, 128), step_ref[0].astype(F32), F32)
    first_fix = 1.0 - jnp.exp(count * math.log(first_decay))
    second_fix = 1.0 - jnp.exp(count * math.log(second_decay))
    for layer in range(3):
        wait(*loads[layer])
        first_ref[layer], second_ref[layer], master_ref[layer] = adam(
            master_ref[layer], shard_ref[layer], first_old_ref[layer], second_old_ref[layer], rate, weight_decay,
            scale, first_fix, second_fix,
        )
        for source, target in (
            (first_ref, first_out_hbm), (second_ref, second_out_hbm), (master_ref, master_out_hbm)
        ):
            outs.append(copies.start(source.at[layer], target.at[layer]))
    wide = [jnp.concatenate([v] * (sz.channels // 128), axis=1) for v in (scale, first_fix, second_fix)]
    for layer in range(3):
        small_ref[0, layer], small_ref[1, layer], small_ref[2, layer] = adam(
            norm_ref[layer], norm_grad[layer], norm_first_ref[layer], norm_second_ref[layer], norm_rate, 0.0, *wide
        )
    for k, target in enumerate((norm_first_hbm, norm_second_hbm, norm_hbm)):
        outs.append(copies.start(small_ref.at[k], target))
    wait(*outs)


def adam(param, grad, first, second, rate, decay, scale, first_fix, second_fix):
    clipped = scale * grad
    first_new = first_decay * first + (1.0 - first_decay) * clipped
    second_new = second_decay * second + (1.0 - second_decay) * clipped * clipped
    update = first_new / first_fix / (jnp.sqrt(second_new / second_fix) + adam_epsilon)
    return first_new, second_new, param - rate * (update + decay * param)


def call(kernel, name, outs, ins, scratch=(), flops=0, moved=0, hbm_ins=(), hbm_outs=(), smem_ins=(), sems=1):
    spaces_in = [
        pltpu.SMEM if k in smem_ins else pltpu.HBM if k in hbm_ins else pltpu.VMEM for k in range(len(ins))
    ]
    spaces_out = [pltpu.HBM if k in hbm_outs else pltpu.VMEM for k in range(len(outs))]
    return pl.pallas_call(
        kernel,
        out_shape=tuple(space(out.shape, out.dtype) for space, out in zip(spaces_out, outs)),
        in_specs=[spec(space) for space in spaces_in],
        out_specs=tuple(spec(space) for space in spaces_out),
        scratch_shapes=list(scratch) + [pltpu.SemaphoreType.DMA((sems,))],
        compiler_params=params(SPACE),
        cost_estimate=pl.CostEstimate(flops=flops, bytes_accessed=moved, transcendentals=0),
        name=name,
    )(*[v if k in smem_ins else pltpu.with_memory_space_constraint(v, spaces_in[k]) for k, v in enumerate(ins)])


def local(sz, block_input, conv_weights, norm_params, pool_index, task_mask, map_kind, map_domain, out_grad, step,
          conv_master, conv_moment1, conv_moment2, norm_moment1, norm_moment2):
    w, c, q = sz.width, sz.channels, sz.quarter
    half = w // 2
    n_maps, bands = sz.maps, sz.bands
    x = block_input.reshape(sz.pixels, c)
    index = pool_index.reshape(sz.pixels // 4, c)
    norms, norm_first, norm_second = (v.transpose(1, 0, 2) for v in (norm_params, norm_moment1, norm_moment2))
    edge = HALO * w
    lines = sz.pixels // 4

    def shape(dims, dtype):
        return jax.ShapeDtypeStruct(dims, dtype)

    def pixel_shape(rows, dtype):
        return shape((rows * w, c), dtype)

    def pixel_space(rows, dtype, times=1):
        return pltpu.VMEM((rows * w, times * c), dtype)

    def share_shapes(count):
        return [shape((count, q), BF16)] * bands

    stats_shape = shape((sz.devices, 8, c // 4), F32)
    tile_shape = shape((8, c // 4), F32)
    weight_space = pltpu.VMEM((9 - HEAD, c, c), BF16)


    def conv_flops(rows):
        return rows * w * 9 * c * c * 2

    def spread(stats):
        return lax.all_to_all(stats, AXES, 0, 0, tiled=True)

    def trade(shares):
        return [shares[0]] + [
            lax.ppermute(shares[n], "rows", [(i, i ^ n) for i in range(bands)]) for n in range(1, bands)
        ]

    def swap(act, n):
        return lax.ppermute(act, "rows", [(i, i ^ n) for i in range(bands)])

    tie = lax.optimization_barrier

    to_near, to_far, own_x = call(
        functools.partial(kernel_edges, sz), "edges",
        [shape((edge + 2 * half, c), BF16)] * 2 + [pixel_shape(sz.rows, BF16)], [x, index],
        [pltpu.VMEM((2, 2 * half, c), jnp.int32)], hbm_ins=(0, 1), sems=5,
    )
    far = lax.ppermute(to_far, "rows", [(i + 1 - k, i + k) for i in range(1, bands - 1, 2) for k in (0, 1)])
    near = swap(to_near, 1)

    limits, member = call(
        functools.partial(kernel_places, sz), "places", [shape((8, 128), jnp.int32), stats_shape],
        [map_kind, map_domain], smem_ins=(0, 1),
    )
    labelled = (out_grad * task_mask[..., None].astype(BF16)).reshape(sz.height // 2 * half, q)
    labelled = jnp.pad(labelled, ((2 * half, 2 * half), (0, 0)))
    consts = [limits, member]

    rows = sz.rows + 2 * HALO
    stats, conv, kept = call(
        functools.partial(kernel_first, sz), "first",
        [stats_shape, pixel_shape(rows - 2, F32), pixel_shape(sz.rows, BF16)], [limits, near, own_x, far, conv_weights[0, :HEAD], conv_weights],
        [pixel_space(rows, BF16, 3), weight_space], conv_flops(rows - 2), hbm_ins=(5,), hbm_outs=(2,), sems=4,
    )
    def head(layer, weights):
        return weights[layer, :HEAD]

    cot_lines = (sz.rows // 2 + 4) * half
    cots = call(functools.partial(kernel_spans, sz), "spans", share_shapes(cot_lines), [labelled], hbm_outs=range(bands), sems=bands)
    stats, weights, *cots = tie((stats, conv_weights, *cots))
    gathered = spread(stats)
    cots = trade(cots)
    acts = [[kept, swap(kept, 1), swap(kept, 2)]]
    moments = []
    saves = []
    for layer in (1, 2):
        rows = sz.rows + 2 * (HALO - layer)
        outs = [
            stats_shape, pixel_shape(rows - 2, F32), tile_shape, pixel_shape(sz.rows, BF16),
            pixel_shape(sz.rows + 2 * layer, F32),
        ]
        scratch = [pixel_space(rows, BF16, 3), weight_space]
        stats, conv, moment, act, saved = call(
            functools.partial(kernel_forward, sz, layer), "forward", outs,
            consts + [gathered, conv, norms, head(layer, weights), conv_weights], scratch,
            conv_flops(rows - 2), hbm_ins=(6,), hbm_outs=(3, 4), sems=5,
        )
        moments.append(moment)
        saves.append(saved)
        if layer == 1:
            stats, weights, *acts[0] = tie((stats, conv_weights, *acts[0]))
            gathered = spread(stats)
        else:
            stats, *cots = tie((stats, *cots))
            gathered = spread(stats)
        if layer == 1:
            acts[0].append(swap(acts[0][2], 1))
        acts.append([act, swap(act, 1), swap(act, 2)])

    rows = sz.rows + 2 * (HALO - 3)
    stats, grad, normed, moment, *shares = call(
        functools.partial(kernel_pool, sz), "pool",
        [stats_shape, pixel_shape(rows, F32), pixel_shape(rows, BF16), tile_shape]
        + share_shapes(lines + 2 * sz.pixels),
        consts + [gathered, conv, norms, index, near, far] + cots,
        [
            pltpu.VMEM((lines, c), jnp.int32), pltpu.VMEM((2 * half, c), BF16), pltpu.VMEM((2 * half, c), BF16),
            pltpu.VMEM((cot_lines, c), BF16),
            pltpu.VMEM((c // 128, (rows + 2) * w, 128), F32), pltpu.VMEM((c // 128, sz.pixels, 128), F32),
            pltpu.VMEM((lines, c), BF16), pixel_space(sz.rows, BF16), pixel_space(sz.rows, BF16),
        ],
        conv_flops(4), hbm_ins=range(5, 8 + bands), hbm_outs=range(4, 4 + bands), sems=3 + 4 * bands,
    )
    moments.append(moment)
    stats, weights, acts[0][3], *rest = tie((stats, conv_weights, acts[0][3], *acts[1], *acts[2]))
    acts[1], acts[2] = rest[:3], rest[3:]
    acts[1].append(swap(acts[1][2], 1))
    gathered = spread(stats)
    exchanged = trade(shares)
    acts[2].append(swap(acts[2][2], 1))
    pooled_parts = exchanged

    totals = [None, None, None]
    share = 9 * (c // n_maps)
    steps = n_maps.bit_length() - 1

    def part_shape(parts, dtype):
        return shape((parts, share, q), dtype)

    def part_space(parts, dtype):
        return pltpu.VMEM((parts, share, q), dtype)

    def weight_grad(layer, gathered, given, first):
        scratch = [
            pltpu.VMEM((sz.height * w, q), BF16),
            pltpu.VMEM((sz.height * w, q), BF16),
            pltpu.VMEM((sz.height * w, c), BF16),
            pltpu.VMEM((sz.height * w, 9 * q), BF16),
        ]
        outs = [part_shape(n_maps // 2, dtype) for dtype in (F32, BF16)]
        scratch.append(pltpu.VMEM((c, 9 * q), F32))
        if layer > 0:
            scratch += [part_space(n_maps // 2, dtype) for dtype in (F32, BF16)]
        return call(
            functools.partial(kernel_weight_grad, sz, layer, first), "weight_grad", outs,
            consts + [gathered, moments[layer], norms] + given + acts[layer], scratch, conv_flops(sz.rows),
            hbm_ins=range(5, 5 + 2 * bands), hbm_outs=() if layer == 0 else (0, 1), sems=3 * bands + 2,
        )

    def step_of(send, k):
        return lax.ppermute(send, "maps", [(m, m ^ (1 << k)) for m in range(n_maps)])

    def halved(keep, received):
        size = keep.shape[0] // 2
        return call(
            kernel_halve, "halve", [part_shape(size, dtype) for dtype in (F32, BF16)], [keep, received],
            [part_space(2 * size, F32), part_space(size, BF16)],
            hbm_ins=(0,), hbm_outs=(0, 1), sems=4,
        )

    def halve(keep, received, k):
        while k < steps - 1:
            k += 1
            keep, send = halved(keep, received)
            received = step_of(send, k)
        return keep, received

    shards = [None, None, None]
    for layer in (2, 1):
        halo = layer + 1
        rows = sz.rows + 2 * halo
        received, gathered_here = exchanged, gathered
        stats, grad, normed, totals[layer], *shares = call(
            functools.partial(kernel_backward, sz, layer), "backward",
            [stats_shape, pixel_shape(rows - 2, F32), pixel_shape(rows - 2, BF16), tile_shape]
            + share_shapes(2 * sz.pixels),
            consts + [
                gathered, grad, normed, moments[layer], norms, head(layer, weights), conv_weights, saves[layer - 1],
                moments[layer - 1],
            ],
            [
                pixel_space(rows - 2, F32), pixel_space(rows, BF16, 3), weight_space, pixel_space(sz.rows, BF16),
                pixel_space(sz.rows, BF16),
            ],
            conv_flops(rows - 2), hbm_ins=(8, 9), hbm_outs=range(4, 4 + bands), sems=4 + 2 * bands,
        )
        if layer == 2:
            stats, weights, acts[1][3], acts[2][3], *received = tie(
                (stats, conv_weights, acts[1][3], acts[2][3], *received)
            )
            gathered = spread(stats)
            exchanged = trade(shares)
            keep2, send2 = weight_grad(2, gathered_here, received, (lines, lines + sz.pixels))
            gathered, send2 = tie((gathered, send2))
            arrived2 = step_of(send2, 0)
        else:
            stats, weights, *received = tie((stats, conv_weights, *received))
            gathered = spread(stats)
            exchanged = trade(shares)
            keep1, send1 = weight_grad(1, gathered_here, received, (0, sz.pixels))
            gathered, send1, arrived2 = tie((gathered, send1, arrived2))
            arrived1 = step_of(send1, 0)
            keep2, send2 = halved(keep2, arrived2)

    arrived2 = step_of(send2, 1)
    keep0, send0 = weight_grad(0, gathered, exchanged, (0, sz.pixels))
    arrived0 = step_of(send0, 0)
    arrived1, arrived2 = tie((arrived1, arrived2))
    keep1, send1 = halved(keep1, arrived1)
    keep2, send2 = halved(keep2, arrived2)
    arrived1 = step_of(send1, 1)
    arrived2 = step_of(send2, 2)
    arrived0, arrived1, arrived2 = tie((arrived0, arrived1, arrived2))
    half_maps = n_maps // 2
    (partial,) = call(
        kernel_add, "add", [part_shape(half_maps, BF16)], [keep0, arrived0],
        [part_space(half_maps, F32)], hbm_ins=(0,), sems=half_maps,
    )
    alike = [[m for m in range(n_maps) if m & 1 == bit] for bit in (0, 1)]
    received = lax.all_to_all(partial, "maps", 0, 0, tiled=True, axis_index_groups=alike)
    shards[2] = halve(keep2, arrived2, 2)
    shards[1] = halve(keep1, arrived1, 1)
    input_grad, totals[0], pooled = call(
        functools.partial(kernel_last, sz), "last",
        [pixel_shape(sz.rows, BF16), tile_shape, shape((sz.height // 2 * half, q), BF16)],
        consts + [gathered, grad, normed, moments[0], norms, head(0, weights), conv_weights] + pooled_parts,
        [pixel_space(sz.rows + 2, BF16, 3), weight_space, pixel_space(sz.rows, F32), pixel_space(sz.rows, BF16)],
        conv_flops(sz.rows), hbm_ins=range(8, 9 + bands), hbm_outs=(0, 2), sems=4 + bands,
    )

    norm_shape = shape((3, 2, c), F32)
    squares, shard, norm_grad = call(
        functools.partial(kernel_squares, sz), "squares",
        [shape((sz.devices, 1, q), F32), part_shape(3, F32), norm_shape],
        [received, *shards[1], *shards[2], totals[2], totals[1], totals[0]],
        [part_space(2, F32), part_space(2, BF16)], hbm_ins=range(1, 5), sems=4,
    )
    every = lax.all_to_all(squares, AXES, 0, 0, tiled=True)
    rate = 2.0 / math.sqrt(9.0 * c)
    total, conv_first, conv_second, conv_new, norm_first, norm_second, norm_new = call(
        functools.partial(kernel_adam, sz, rate), "adam",
        [shape((1, 128), F32)] + [part_shape(3, F32)] * 3 + [norm_shape] * 3,
        [every, step, shard]
        + [v.reshape(3, share, q) for v in (conv_master, conv_moment1, conv_moment2)]
        + [norm_grad, norms, norm_first, norm_second],
        [pltpu.VMEM((1, 128), F32)] + [part_space(3, F32)] * 3 + [pltpu.VMEM((3, 3, 2, c), F32)],
        hbm_ins=(3,), hbm_outs=range(7), smem_ins=(1,), sems=16,
    )
    return (
        pooled.reshape(1, sz.height // 2, half, q),
        input_grad.reshape(block_input.shape),
        total[0, :1],
        conv_first.reshape(conv_master.shape),
        conv_second.reshape(conv_master.shape),
        conv_new.reshape(conv_master.shape),
        norm_first.transpose(1, 0, 2),
        norm_second.transpose(1, 0, 2),
        norm_new.transpose(1, 0, 2),
    )


def solution(mesh):
    def run(*args):
        bands = mesh.shape["rows"]
        maps = mesh.shape["maps"]
        shape = args[0].shape
        sz = Sizes(maps, bands, shape[1] // bands, shape[2], shape[3])
        return jax.shard_map(
            functools.partial(local, sz),
            mesh=mesh,
            in_specs=(
                P("maps", "rows", None, None),
                P(),
                P(),
                P("maps", "rows", None, None),
                P("maps", None, None),
                P(),
                P(),
                P("maps", None, None, "rows"),
                P(),
                P(None, None, "maps", "rows"),
                P(None, None, "maps", "rows"),
                P(None, None, "maps", "rows"),
                P(),
                P(),
            ),
            out_specs=(
                P("maps", None, None, "rows"),
                P("maps", "rows", None, None),
                P(),
                P(None, None, "maps", "rows"),
                P(None, None, "maps", "rows"),
                P(None, None, "maps", "rows"),
                P(),
                P(),
                P(),
            ),
            check_vma=False,
        )(*args)

    return run
```
